32 devices in a mesh: dp: 8 (over z, x), seq: 4 (over y, core).
Axes of the slice: x: 2, y: 2, z: 4, core: 2. Of those that a mesh axis runs over, the one named last changes fastest.
Arguments:
- hidden_in: bfloat16 [8, 2048, 2048], P('dp', 'seq'), may hold values from -6 to 6
- widths: int32 [8], P('dp'), may hold values from 0 to 3
- norm_gain: bfloat16 [2048], P(('dp', 'seq')), may hold values from 0.099609375 to 1.8984375
- w_in: bfloat16 [2048, 8448], P(('dp', 'seq')), may hold values from -0.125 to 0.125
- w_dt: bfloat16 [2048, 64], P(('dp', 'seq')), may hold values from -0.125 to 0.125
- conv_weight: bfloat16 [4, 4352], replicated, may hold values from -3 to 3
- dt_bias: float32 [64], replicated, may hold values from -3 to 0
- a_log: float32 [64], replicated, may hold values from -9 to -2.3
- skip_gain: float32 [64], replicated, may hold values from 0.5 to 1.5
- gate_gain: bfloat16 [4096], P(('dp', 'seq')), may hold values from 0.099609375 to 1.8984375
- w_out: bfloat16 [4096, 2048], P(('dp', 'seq')), may hold values from -0.125 to 0.125
- grad_out: bfloat16 [8, 2048, 2048], P('dp', 'seq'), may hold values from -6 to 6
Outputs:
- hidden_out: bfloat16 [8, 2048, 2048], P('dp', 'seq')
- grad_in: bfloat16 [8, 2048, 2048], P('dp', 'seq')
- grad_norm_gain: float32 [2048], P(('dp', 'seq'))
- grad_w_in: float32 [2048, 8448], P(('dp', 'seq'))
- grad_w_dt: float32 [2048, 64], P(('dp', 'seq'))
- grad_conv: float32 [4, 4352], replicated
- grad_dt_bias: float32 [64], replicated
- grad_a_log: float32 [64], replicated
- grad_skip: float32 [64], replicated
- grad_gate_gain: float32 [4096], P(('dp', 'seq'))
- grad_w_out: float32 [4096, 2048], P(('dp', 'seq'))
The draws below stay inside these ranges and needn't reach their ends.
Inputs may be any that keep to these rules, and one draw needn't show every extreme that they name: `widths`: level of the nested width of each sequence: it uses the first 4096 * 2^level / 8 inner units and their heads.
All inputs are finite; a program needn't handle non-finite values.
Results may differ from the reference program's by a relative error of at most 0.0095.
Values may be sent and summed in bfloat16 or wider, within the bound.
No kernel may reach another device: no remote copies, remote signals or barrier semaphores. Data moves between devices by JAX's collectives and lax.ppermute only.
A program may use at most 448 MiB of HBM per device.

```python
import jax
import jax.numpy as jnp
from jax import lax

D = 2048
INNER = 4096
HEAD_DIM = 64
STATE = 128
CONV = 4
BLOCK = 256
HEADS = 64
CHANNELS = 4352
PROJ = 8448
LENGTH = 2048
SEQS = 8


def touch_ends(drawn, own_key, low, top_value):
    extent = drawn.shape
    place = [jax.random.randint(jax.random.fold_in(own_key, axis), (), 0, extent[axis]) for axis in range(len(extent))]
    drawn = drawn.at[tuple(place)].set(low)
    longest = extent.index(max(extent))
    place[longest] = (place[longest] + 1) % extent[longest]
    return drawn.at[tuple(place)].set(top_value)


def block_levels(rng, dims, shards, smallest, high):
    def one(dim, blocks):
        draws = jax.random.uniform(jax.random.fold_in(jax.random.fold_in(rng, 6), dim), (blocks,), jnp.float32, smallest / len(shards), high / len(shards))
        return jnp.repeat(jnp.exp(draws), dims[dim] // blocks).reshape((-1,) + (1,) * (len(dims) - dim - 1))

    gain = one(*shards[0])
    for cut in shards[1:]:
        gain = gain * one(*cut)
    return gain


def scatter_about(rng, shape, width, reach, split=(), held_as=jnp.bfloat16):
    loudness = block_levels(rng, shape, split, -0.22, 0.18) if split else 1.0
    entries = jax.random.normal(rng, shape, jnp.float32) * width * loudness
    return jnp.minimum(jnp.maximum(entries, -reach), reach).astype(held_as)


def setup_inputs(seed: int = 0) -> dict:
    key_list = jax.random.split(jax.random.key(seed), 13)
    return {
        "hidden_in": scatter_about(key_list[0], (SEQS, LENGTH, D), 1.0, 6.0, ((0, 8), (1, 4))),
        "widths": touch_ends(jax.random.randint(key_list[1], (SEQS,), 0, 4), jax.random.fold_in(key_list[1], 1), 0, 3).astype(jnp.int32),
        "norm_gain": jnp.clip(1.0 + 0.18 * jax.random.normal(key_list[2], (D,), jnp.float32), 0.099609375, 1.8984375).astype(jnp.bfloat16),
        "w_in": scatter_about(key_list[3], (D, PROJ), D ** -0.5, 0.125, ((0, 32),)),
        "w_dt": scatter_about(key_list[4], (D, HEADS), D ** -0.5, 0.125, ((0, 32),)),
        "conv_weight": scatter_about(key_list[5], (CONV, CHANNELS), CONV ** -0.5, 3.0),
        "dt_bias": jnp.clip(jax.random.uniform(key_list[6], (HEADS,), jnp.float32, -3.0, 0.0), -3.0, 0.0),
        "a_log": jnp.clip(jax.random.uniform(key_list[7], (HEADS,), jnp.float32, -9.0, -2.3), -9.0, -2.3),
        "skip_gain": jnp.clip(jax.random.uniform(key_list[8], (HEADS,), jnp.float32, 0.5, 1.5), 0.5, 1.5),
        "gate_gain": jnp.clip(1.0 + 0.18 * jax.random.normal(key_list[9], (INNER,), jnp.float32), 0.099609375, 1.8984375).astype(jnp.bfloat16),
        "w_out": scatter_about(key_list[10], (INNER, D), (INNER // 2) ** -0.5, 0.125, ((0, 32),)),
        "grad_out": scatter_about(key_list[11], (SEQS, LENGTH, D), 1.0, 6.0, ((0, 8), (1, 4))),
    }


@jax.custom_vjp
def low(v):
    return lax.optimization_barrier(v.astype(jnp.bfloat16)).astype(jnp.float32)

@jax.custom_vjp
def low_back(v):
    return v

def low_keep(v):
    return (low(v), None)

def low_pass(kept, grad):
    return (grad,)

def back_keep(v):
    return (v, None)

def back_low(kept, grad):
    return (low(grad),)
low.defvjp(low_keep, low_pass)
low_back.defvjp(back_keep, back_low)
epsilon = 1e-05
highest = lax.Precision.HIGHEST

def matmul(first_op, second_op):
    return jnp.dot(first_op, second_op, precision=highest, preferred_element_type=jnp.float32)

def block_step(carry_state, inputs):
    values, keys_b, reads_c, steps_dt, log_decay = inputs
    cumulative = jnp.cumsum(log_decay, axis=0)
    position = jnp.arange(values.shape[0])
    causal = (position[:, None] >= position[None, :])[:, :, None]
    spread = cumulative[:, None, :] - cumulative[None, :, :]
    decays = jnp.where(causal, jnp.exp(jnp.where(causal, spread, 0.0)), 0.0)
    intersection = matmul(reads_c, keys_b.T)
    mixing = decays * intersection[:, :, None] * steps_dt[None, :, :]
    output = jnp.einsum('tsh,shp->thp', mixing, values, precision=highest)
    output = output + jnp.exp(cumulative)[:, :, None] * jnp.einsum('hpn,tn->thp', carry_state, reads_c, precision=highest)
    weights_end = jnp.exp(cumulative[-1][None, :] - cumulative) * steps_dt
    updated = jnp.exp(cumulative[-1])[:, None, None] * carry_state + jnp.einsum('sh,shp,sn->hpn', weights_end, values, keys_b, precision=highest)
    return (updated, output)

def one_sequence(x_in, width_level, norm_gain, w_in, w_dt, conv_weight, dt_bias, a_log, skip_gain, gate_gain, w_out):
    used_units = INNER // 8 * jnp.left_shift(jnp.int32(1), width_level)
    channel_mask = (jnp.arange(INNER) < used_units).astype(jnp.float32)
    head_mask = (jnp.arange(HEADS) * HEAD_DIM < used_units).astype(jnp.float32)
    inverse_rms = lax.rsqrt(lax.optimization_barrier(jnp.mean(x_in * x_in, axis=1, keepdims=True)) + epsilon)
    normed = low(x_in * inverse_rms * norm_gain)
    projection = matmul(normed, w_in)
    z_gate = low_back(projection[:, :INNER] * channel_mask)
    conv_raw = jnp.concatenate([projection[:, INNER:2 * INNER] * channel_mask, projection[:, 2 * INNER:]], axis=1)
    conv_input = low_back(low(conv_raw))
    dt_raw = low_back(matmul(normed, w_dt) * head_mask)
    padded = jnp.concatenate([jnp.zeros((CONV - 1, CHANNELS), jnp.float32), conv_input], axis=0)
    pre_act = jnp.zeros((LENGTH, CHANNELS), jnp.float32)
    for offset in range(CONV):
        pre_act = pre_act + conv_weight[offset] * padded[offset:offset + LENGTH]
    activated = low(jax.nn.silu(pre_act))
    values = activated[:, :INNER].reshape(LENGTH, HEADS, HEAD_DIM)
    keys_b = activated[:, INNER:INNER + STATE]
    reads_c = activated[:, INNER + STATE:]
    steps_dt = jax.nn.softplus(dt_raw + dt_bias)
    log_decay = -jnp.exp(a_log) * steps_dt
    blocks = LENGTH // BLOCK
    inputs = (values.reshape(blocks, BLOCK, HEADS, HEAD_DIM), keys_b.reshape(blocks, BLOCK, STATE), reads_c.reshape(blocks, BLOCK, STATE), steps_dt.reshape(blocks, BLOCK, HEADS), log_decay.reshape(blocks, BLOCK, HEADS))
    start_state = jnp.zeros((HEADS, HEAD_DIM, STATE), jnp.float32)
    final_state, outputs = lax.scan(jax.checkpoint(block_step), start_state, inputs)
    y_ssd = outputs.reshape(LENGTH, HEADS, HEAD_DIM) + skip_gain[:, None] * values
    y_ssd = y_ssd.reshape(LENGTH, INNER)
    gated = y_ssd * jax.nn.silu(z_gate)
    inverse_gate = lax.rsqrt(lax.optimization_barrier(jnp.sum(gated * gated, axis=1, keepdims=True)) / used_units.astype(jnp.float32) + epsilon)
    rounded_out = low(gated * inverse_gate * gate_gain)
    return x_in + matmul(rounded_out, w_out)

def reference(hidden_in, widths, norm_gain, w_in, w_dt, conv_weight, dt_bias, a_log, skip_gain, gate_gain, w_out, grad_out):
    params = tuple((item.astype(jnp.float32) for item in (norm_gain, w_in, w_dt, conv_weight, dt_bias, a_log, skip_gain, gate_gain, w_out)))
    x_all = hidden_in.astype(jnp.float32)

    def forward(x_values, *weights):

        def run_one(pair):
            return one_sequence(pair[0], pair[1], *weights)
        return lax.map(jax.checkpoint(run_one), (x_values, widths))
    result, pullback = jax.vjp(forward, x_all, *params)
    grads = pullback(grad_out.astype(jnp.float32))
    return (result.astype(jnp.bfloat16), grads[0].astype(jnp.bfloat16), grads[1], grads[2], grads[3], grads[4], grads[5], grads[6], grads[7], grads[8], grads[9])
```

```python
import functools

import jax
import jax.numpy as jnp
from jax import lax
from jax.experimental import pallas as pl
from jax.experimental.pallas import tpu as pltpu
from jax.sharding import PartitionSpec as P

D = 2048
INNER = 4096
HEAD_DIM = 64
STATE = 128
CONV = 4
HEADS = 64
CHANNELS = 4352

PART = 4
LANES = 128
STRIPS = INNER // LANES // PART
OWN = STRIPS * LANES
OWN_HEADS = OWN // HEAD_DIM
OWN_BC = 2 * STATE // PART
CONV_COLS = OWN + LANES
Q = 256
HALF = Q // 2

epsilon = 1e-05
highest = lax.Precision.HIGHEST
f32 = jnp.float32
bf16 = jnp.bfloat16
LOG2E = 1.4426950408889634


def swap(value, axis, pairs):
    return lax.ppermute(value, axis, pairs)


def xor_seq(value, bits):
    return lax.ppermute(value, "seq", [(s, s ^ bits) for s in range(PART)])


def seq_gather(block):
    me = lax.axis_index("seq")
    sibling = xor_seq(block, 1)
    across = xor_seq(block, 2)
    corner = xor_seq(across, 1)
    out = jnp.zeros((PART,) + block.shape, block.dtype)
    for bits, piece in ((0, block), (1, sibling), (2, across), (3, corner)):
        out = lax.dynamic_update_index_in_dim(out, piece, me ^ bits, 0)
    return out


def seq_scatter(blocks):
    me = lax.axis_index("seq")
    core, row = me % 2, me // 2
    view = blocks.reshape((2, 2) + blocks.shape[1:])
    mine = lax.dynamic_index_in_dim(view, core, 1, False)
    other = lax.dynamic_index_in_dim(view, 1 - core, 1, False)
    half = mine.astype(f32) + xor_seq(other, 1).astype(f32)
    keep = lax.dynamic_index_in_dim(half, row, 0, False)
    give = lax.dynamic_index_in_dim(half, 1 - row, 0, False).astype(bf16)
    return keep + xor_seq(give, 2).astype(f32)


def seq_transpose(pieces):
    me = lax.axis_index("seq")
    out = jnp.zeros_like(pieces)
    for bits in range(PART):
        piece = lax.dynamic_index_in_dim(pieces, me ^ bits, 0, False)
        if bits:
            piece = xor_seq(piece, bits)
        out = lax.dynamic_update_index_in_dim(out, piece, me ^ bits, 0)
    return out


def seq_total(value):
    value = value + xor_seq(value, 1)
    return value + xor_seq(value, 2)


def fast_mesh():
    return lax.axis_size("dp") == 8


def dp_shift_z(value, steps):
    pairs = [(z * 2 + x, (z + steps) % 4 * 2 + x) for z in range(4) for x in range(2)]
    return lax.ppermute(value, "dp", pairs)


def dp_swap_x(value):
    return lax.ppermute(value, "dp", [(d, d ^ 1) for d in range(8)])


def dp_gather(block):
    me = lax.axis_index("dp")
    z, x = me // 2, me % 2
    out = jnp.zeros((8,) + block.shape, block.dtype)
    for steps in range(4):
        piece = dp_shift_z(block, steps) if steps else block
        source = (z - steps + 4) % 4
        out = lax.dynamic_update_index_in_dim(out, piece, source * 2 + x, 0)
        out = lax.dynamic_update_index_in_dim(out, dp_swap_x(piece), source * 2 + 1 - x, 0)
    return out


def dp_scatter(blocks):
    me = lax.axis_index("dp")
    z, x = me // 2, me % 2
    view = blocks.reshape((4, 2) + blocks.shape[1:])
    mine = lax.dynamic_index_in_dim(view, x, 1, False)
    other = lax.dynamic_index_in_dim(view, 1 - x, 1, False)
    half = mine.astype(f32) + dp_swap_x(other).astype(f32)
    total = lax.dynamic_index_in_dim(half, z, 0, False)
    for steps in range(1, 4):
        give = lax.dynamic_index_in_dim(half, (z + steps) % 4, 0, False).astype(bf16)
        total = total + dp_shift_z(give, steps).astype(f32)
    return total


def dp_total(value):
    if not fast_mesh():
        return lax.psum(value, "dp")
    value = value + dp_swap_x(value)
    return value + dp_shift_z(value, 1) + dp_shift_z(value, 2) + dp_shift_z(value, 3)


def by_owner(columns):
    rows = columns.shape[0]
    return (
        columns.reshape(rows, STRIPS, PART, LANES).transpose(2, 0, 1, 3).reshape(PART, rows, OWN)
    )


def from_owner(pieces):
    rows = pieces.shape[1]
    return (
        pieces.reshape(PART, rows, STRIPS, LANES).transpose(1, 2, 0, 3).reshape(rows, INNER)
    )


def heads_by_owner(columns):
    rows = columns.shape[0]
    return (
        columns.reshape(rows, STRIPS, PART, 2).transpose(2, 0, 1, 3).reshape(PART, rows, OWN_HEADS)
    )


def heads_from_owner(pieces):
    rows = pieces.shape[1]
    return (
        pieces.reshape(PART, rows, STRIPS, 2).transpose(1, 2, 0, 3).reshape(rows, HEADS)
    )


def gather_in(pieces):
    if fast_mesh():
        own = seq_transpose(pieces)
        block = own.reshape(-1, own.shape[2])
        return dp_gather(block).reshape(D, -1)
    full = lax.all_gather(pieces, ("dp", "seq"), axis=1, tiled=True)
    return lax.dynamic_index_in_dim(full, lax.axis_index("seq"), 0, False)


def scatter_in(grads):
    columns = grads.shape[1]
    if fast_mesh():
        total = dp_scatter(grads.reshape(8, -1, columns))
        return seq_transpose(total.reshape(PART, -1, columns).astype(bf16)).astype(f32)
    full = jnp.zeros((PART,) + grads.shape, grads.dtype)
    full = lax.dynamic_update_index_in_dim(full, grads, lax.axis_index("seq"), 0)
    return lax.psum_scatter(full, ("dp", "seq"), scatter_dimension=1, tiled=True).astype(f32)


def gather_out(rows):
    if fast_mesh():
        return dp_gather(rows).reshape(OWN, -1)
    full = lax.all_gather(rows, ("dp", "seq"), axis=0, tiled=True)
    full = full.reshape(STRIPS, PART, LANES, -1)
    return lax.dynamic_index_in_dim(full, lax.axis_index("seq"), 1, False).reshape(OWN, -1)


def scatter_out(grads):
    if fast_mesh():
        return dp_scatter(grads.reshape(8, LANES, -1))
    full = jnp.zeros((STRIPS, PART, LANES, grads.shape[1]), grads.dtype)
    full = lax.dynamic_update_index_in_dim(
        full, grads.reshape(STRIPS, LANES, -1), lax.axis_index("seq"), 1
    )
    full = full.reshape(INNER, -1)
    return lax.psum_scatter(full, ("dp", "seq"), scatter_dimension=0, tiled=True).astype(f32)


def dot_nn(a, b):
    return lax.dot_general(a, b, (((1,), (0,)), ((), ())), preferred_element_type=f32)


def dot_nt(a, b):
    return lax.dot_general(a, b, (((1,), (1,)), ((), ())), preferred_element_type=f32)


def dot_tn(a, b):
    return lax.dot_general(a, b, (((0,), (0,)), ((), ())), preferred_element_type=f32)


def dot_exact(a, b):
    return lax.dot_general(
        a, b, (((1,), (0,)), ((), ())), precision=highest, preferred_element_type=f32
    )


def sigmoid(v):
    return 0.5 + 0.5 * jnp.tanh(0.5 * v)


def decay_terms(dt_ref, rows_ref):
    v = dt_ref[...] * rows_ref[2:3, :] + rows_ref[0:1, :]
    steps = jnp.maximum(v, 0.0) + jnp.log1p(jnp.exp(-jnp.abs(v)))
    log2_decay = rows_ref[1:2, :] * LOG2E * steps
    row = lax.broadcasted_iota(jnp.int32, (Q, Q), 0)
    column = lax.broadcasted_iota(jnp.int32, (Q, Q), 1)
    lower = jnp.where(row >= column, 1.0, 0.0)
    running = dot_exact(lower, log2_decay)
    shifted = running - jnp.log(steps) * LOG2E
    end = running[Q - 1 : Q, :]
    return v, steps, running, shifted, end


def forward_kernel(
    ci_ref, bc_ref, dt_ref, cw_ref, rows_ref, skip_ref, y_ref, act_ref, s_ref, state, xf
):
    @pl.when(pl.program_id(0) == 0)
    def _():
        state[...] = jnp.zeros_like(state)
        xf[0:8, :] = jnp.zeros((8, OWN), f32)

    @pl.when(pl.program_id(0) > 0)
    def _():
        xf[0:8, :] = xf[Q : Q + 8, :]

    xf[8 : Q + 8, :] = ci_ref[...].astype(f32)
    _, _, running, shifted, end = decay_terms(dt_ref, rows_ref)
    shifted_t = shifted.T
    e_run = jnp.exp2(running)
    w_end = jnp.exp2(end - shifted)
    e_end = jnp.exp2(end)
    keys = bc_ref[:, :STATE]
    reads = bc_ref[:, STATE:]
    keys_t = keys.T
    cb = dot_nt(reads, keys)
    causal = lax.broadcasted_iota(jnp.int32, (HALF, HALF), 0) >= lax.broadcasted_iota(
        jnp.int32, (HALF, HALF), 1
    )
    left = lax.broadcasted_iota(jnp.int32, (1, LANES), 1) < HEAD_DIM
    s_ref[0] = state[...].astype(bf16)
    for strip in range(STRIPS):
        at = slice(strip * LANES, (strip + 1) * LANES)
        h0, h1 = 2 * strip, 2 * strip + 1
        pre = cw_ref[0:1, at] * xf[5 : 5 + Q, at]
        for tap in range(1, CONV):
            pre = pre + cw_ref[tap : tap + 1, at] * xf[5 + tap : 5 + tap + Q, at]
        act = (pre * sigmoid(pre)).astype(bf16)
        act_ref[:, at] = act
        actf = act.astype(f32)
        inter = dot_nn(reads, s_ref[0, :, at]) * jnp.where(
            left, e_run[:, h0 : h0 + 1], e_run[:, h1 : h1 + 1]
        )
        inter = inter + skip_ref[0:1, at] * actf
        top, bottom = inter[:HALF], inter[HALF:]
        for h, side in ((h0, left), (h1, jnp.logical_not(left))):
            x_h = jnp.where(side, actf, 0.0).astype(bf16)
            m00 = jnp.where(
                causal,
                jnp.exp2(running[:HALF, h : h + 1] - shifted_t[h : h + 1, :HALF]) * cb[:HALF, :HALF],
                0.0,
            )
            m10 = jnp.exp2(running[HALF:, h : h + 1] - shifted_t[h : h + 1, :HALF]) * cb[HALF:, :HALF]
            m11 = jnp.where(
                causal,
                jnp.exp2(running[HALF:, h : h + 1] - shifted_t[h : h + 1, HALF:]) * cb[HALF:, HALF:],
                0.0,
            )
            top = top + dot_nn(m00.astype(bf16), x_h[:HALF])
            bottom = bottom + dot_nn(
                jnp.concatenate([m10.astype(bf16), m11.astype(bf16)], axis=1), x_h
            )
        y_ref[:HALF, at] = top
        y_ref[HALF:, at] = bottom
        weighted = (actf * jnp.where(left, w_end[:, h0 : h0 + 1], w_end[:, h1 : h1 + 1])).astype(bf16)
        state[:, at] = state[:, at] * jnp.where(
            left, e_end[:, h0 : h0 + 1], e_end[:, h1 : h1 + 1]
        ) + dot_nn(keys_t, weighted)


def recurrence_forward(conv_in, bc, dt_tile, taps, rows, skip_row):
    length = conv_in.shape[0]
    blocks = length // Q
    whole = lambda i: (0, 0)
    along = lambda i: (i, 0)
    return pl.pallas_call(
        forward_kernel,
        grid=(blocks,),
        in_specs=[
            pl.BlockSpec((Q, OWN), along),
            pl.BlockSpec((Q, 2 * STATE), along),
            pl.BlockSpec((Q, LANES), along),
            pl.BlockSpec((8, OWN), whole),
            pl.BlockSpec((8, LANES), whole),
            pl.BlockSpec((8, OWN), whole),
        ],
        out_specs=[
            pl.BlockSpec((Q, OWN), along),
            pl.BlockSpec((Q, OWN), along),
            pl.BlockSpec((1, STATE, OWN), lambda i: (i, 0, 0)),
        ],
        out_shape=[
            jax.ShapeDtypeStruct((length, OWN), f32),
            jax.ShapeDtypeStruct((length, OWN), bf16),
            jax.ShapeDtypeStruct((blocks, STATE, OWN), bf16),
        ],
        scratch_shapes=[pltpu.VMEM((STATE, OWN), f32), pltpu.VMEM((Q + 8, OWN), f32)],
        compiler_params=pltpu.CompilerParams(
            dimension_semantics=("arbitrary",), vmem_limit_bytes=40 * 2**20
        ),
        cost_estimate=pl.CostEstimate(
            flops=12 * 10**9, bytes_accessed=24 * 2**20, transcendentals=10**7
        ),
        name="recurrence_forward",
    )(conv_in, bc, dt_tile, taps, rows, skip_row)


def backward_kernel(
    ci_ref,
    prev_ref,
    act_ref,
    dy_ref,
    y_ref,
    bc_ref,
    dt_ref,
    s_ref,
    cw_ref,
    rows_ref,
    skip_ref,
    dci_ref,
    dbc_ref,
    ddt_ref,
    gconv_ref,
    grow_ref,
    back,
    back16,
    dp,
    xf,
    edy,
    wx,
    dcb,
    p12h,
    p12l,
    p3,
    p23,
    cross,
):
    step = pl.program_id(0)
    last = pl.num_programs(0) - 1

    @pl.when(step == 0)
    def _():
        back[...] = jnp.zeros_like(back)
        dp[Q : Q + 8, :] = jnp.zeros((8, OWN), f32)
        gconv_ref[...] = jnp.zeros_like(gconv_ref)
        grow_ref[...] = jnp.zeros_like(grow_ref)
        cross[...] = jnp.zeros_like(cross)

    @pl.when(step > 0)
    def _():
        dp[Q : Q + 8, :] = dp[0:8, :]

    before = prev_ref[8:16, :].astype(f32)
    xf[0:8, :] = jnp.where(step == last, 0.0, before)
    xf[8 : Q + 8, :] = ci_ref[...].astype(f32)
    v, steps, running, shifted, end = decay_terms(dt_ref, rows_ref)
    running_t = running.T
    e_run = jnp.exp2(running)
    w_end = jnp.exp2(end - shifted)
    e_end = jnp.exp2(end)
    keys = bc_ref[:, :STATE]
    reads = bc_ref[:, STATE:]
    reads_t = reads.T
    cbt = dot_nt(keys, reads)
    ahead = lax.broadcasted_iota(jnp.int32, (HALF, HALF), 0) <= lax.broadcasted_iota(
        jnp.int32, (HALF, HALF), 1
    )
    left = lax.broadcasted_iota(jnp.int32, (1, LANES), 1) < HEAD_DIM
    back16[...] = back[...].astype(bf16)
    dcb[...] = jnp.zeros_like(dcb)
    for strip in range(STRIPS):
        at = slice(strip * LANES, (strip + 1) * LANES)
        h0, h1 = 2 * strip, 2 * strip + 1
        act = act_ref[:, at]
        dy = dy_ref[:, at]
        actf = act.astype(f32)
        dyf = dy.astype(f32)
        skip = skip_ref[0:1, at]
        w_pair = jnp.where(left, w_end[:, h0 : h0 + 1], w_end[:, h1 : h1 + 1])
        e_pair = jnp.where(left, e_run[:, h0 : h0 + 1], e_run[:, h1 : h1 + 1])
        decayed = (dyf * e_pair).astype(bf16)
        edy[:, at] = decayed
        wx[:, at] = (actf * w_pair).astype(bf16)
        inter = dot_nn(keys, back16[:, at]) * w_pair
        top = jnp.zeros((HALF, LANES), f32)
        bottom = jnp.zeros((HALF, LANES), f32)
        for h, side in ((h0, left), (h1, jnp.logical_not(left))):
            x_h = jnp.where(side, actf, 0.0).astype(bf16)
            dy_h = jnp.where(side, dyf, 0.0).astype(bf16)
            g_top = dot_nt(x_h[:HALF], dy)
            g_bottom = dot_nt(x_h[HALF:], dy[HALF:])
            l00 = jnp.exp2(running_t[h : h + 1, :HALF] - shifted[:HALF, h : h + 1])
            l01 = jnp.exp2(running_t[h : h + 1, HALF:] - shifted[:HALF, h : h + 1])
            l11 = jnp.exp2(running_t[h : h + 1, HALF:] - shifted[HALF:, h : h + 1])
            m00 = jnp.where(ahead, l00 * cbt[:HALF, :HALF], 0.0).astype(bf16)
            m01 = (l01 * cbt[:HALF, HALF:]).astype(bf16)
            m11 = jnp.where(ahead, l11 * cbt[HALF:, HALF:], 0.0).astype(bf16)
            top = top + dot_nn(jnp.concatenate([m00, m01], axis=1), dy_h)
            bottom = bottom + dot_nn(m11, dy_h[HALF:])
            dcb[:HALF, :HALF] += jnp.where(ahead, l00 * g_top[:, :HALF], 0.0)
            dcb[:HALF, HALF:] += l01 * g_top[:, HALF:]
            dcb[HALF:, HALF:] += jnp.where(ahead, l11 * g_bottom, 0.0)
        intra = jnp.concatenate([top, bottom], axis=0)
        d_values = intra + inter
        p_12 = dyf * (y_ref[:, at] - skip * actf) - actf * intra
        p_12h = p_12.astype(bf16)
        p12h[:, at] = p_12h
        p12l[:, at] = (p_12 - p_12h.astype(f32)).astype(bf16)
        p3[:, at] = (actf * inter).astype(bf16)
        p23[:, at] = (actf * d_values).astype(bf16)
        d_act = d_values + skip * dyf
        pre = cw_ref[0:1, at] * xf[5 : 5 + Q, at]
        for tap in range(1, CONV):
            pre = pre + cw_ref[tap : tap + 1, at] * xf[5 + tap : 5 + tap + Q, at]
        squashed = sigmoid(pre)
        d_pre = d_act * squashed * (1.0 + pre * (1.0 - squashed))
        dp[0:Q, at] = d_pre
        sums = [
            jnp.sum(d_pre * xf[5 + tap : 5 + tap + Q, at], axis=0, keepdims=True)
            for tap in range(CONV)
        ]
        sums.append(jnp.sum(dyf * actf, axis=0, keepdims=True))
        for place, total in enumerate(sums):
            gconv_ref[place : place + 1, at] += total
        d_in = cw_ref[CONV - 1 : CONV, at] * d_pre
        for tap in range(CONV - 1):
            d_in = d_in + cw_ref[tap : tap + 1, at] * dp[CONV - 1 - tap : CONV - 1 - tap + Q, at]
        dci_ref[:, at] = d_in.astype(bf16)
        kept = back[:, at] * jnp.where(left, e_end[:, h0 : h0 + 1], e_end[:, h1 : h1 + 1])
        cross[0:1, at] = jnp.sum(kept * s_ref[0, :, at].astype(f32), axis=0, keepdims=True)
        back[:, at] = kept + dot_nn(reads_t, decayed)
    dcb_t = dcb[...]
    d_keys = dot_nn(dcb_t.astype(bf16), reads) + dot_nt(wx[...], back16[...])
    d_reads = dot_nn(dcb_t.T.astype(bf16), keys) + dot_nt(edy[...], s_ref[0])
    dbc_ref[:, :STATE] = d_keys.astype(dbc_ref.dtype)
    dbc_ref[:, STATE:] = d_reads.astype(dbc_ref.dtype)
    unit = lax.broadcasted_iota(jnp.int32, (OWN, LANES), 0)
    head = lax.broadcasted_iota(jnp.int32, (OWN, LANES), 1)
    member = jnp.where(unit // HEAD_DIM == head, 1.0, 0.0)
    member16 = member.astype(bf16)
    s_12 = dot_nn(p12h[...], member16) + dot_nn(p12l[...], member16)
    s_3 = dot_nn(p3[...], member16)
    s_23 = dot_nn(p23[...], member16)
    through = dot_exact(cross[...], member)[0:1, :]
    row = lax.broadcasted_iota(jnp.int32, (Q, Q), 0)
    column = lax.broadcasted_iota(jnp.int32, (Q, Q), 1)
    suffix = jnp.where(column >= row, 1.0, 0.0)
    prefix = jnp.where(column < row, 1.0, 0.0)
    d_log = dot_exact(suffix, s_12) + dot_exact(prefix, s_3) + through
    slope = sigmoid(v)
    ratio = jnp.where(steps > 0.0, slope / steps, 0.0)
    rate = rows_ref[1:2, :]
    d_sum = s_23 * ratio + rate * d_log * slope
    ddt_ref[...] = d_sum * rows_ref[2:3, :]
    grow_ref[0:1, :] += jnp.sum(d_sum, axis=0, keepdims=True)
    grow_ref[1:2, :] += jnp.sum(d_log * rate * steps, axis=0, keepdims=True)


def recurrence_backward(conv_in, act, dy, y, bc, dt_tile, entry, taps, rows, skip_row):
    length = conv_in.shape[0]
    blocks = length // Q
    whole = lambda i: (0, 0)
    along = lambda i: (blocks - 1 - i, 0)
    previous = lambda i: (jnp.maximum((blocks - 1 - i) * (Q // 16) - 1, 0), 0)
    return pl.pallas_call(
        backward_kernel,
        grid=(blocks,),
        in_specs=[
            pl.BlockSpec((Q, OWN), along),
            pl.BlockSpec((16, OWN), previous),
            pl.BlockSpec((Q, OWN), along),
            pl.BlockSpec((Q, OWN), along),
            pl.BlockSpec((Q, OWN), along),
            pl.BlockSpec((Q, 2 * STATE), along),
            pl.BlockSpec((Q, LANES), along),
            pl.BlockSpec((1, STATE, OWN), lambda i: (blocks - 1 - i, 0, 0)),
            pl.BlockSpec((8, OWN), whole),
            pl.BlockSpec((8, LANES), whole),
            pl.BlockSpec((8, OWN), whole),
        ],
        out_specs=[
            pl.BlockSpec((Q, OWN), along),
            pl.BlockSpec((Q, 2 * STATE), along),
            pl.BlockSpec((Q, LANES), along),
            pl.BlockSpec((8, OWN), whole),
            pl.BlockSpec((8, LANES), whole),
        ],
        out_shape=[
            jax.ShapeDtypeStruct((length, OWN), bf16),
            jax.ShapeDtypeStruct((length, 2 * STATE), bf16),
            jax.ShapeDtypeStruct((length, LANES), f32),
            jax.ShapeDtypeStruct((8, OWN), f32),
            jax.ShapeDtypeStruct((8, LANES), f32),
        ],
        scratch_shapes=[
            pltpu.VMEM((STATE, OWN), f32),
            pltpu.VMEM((STATE, OWN), bf16),
            pltpu.VMEM((Q + 8, OWN), f32),
            pltpu.VMEM((Q + 8, OWN), f32),
            pltpu.VMEM((Q, OWN), bf16),
            pltpu.VMEM((Q, OWN), bf16),
            pltpu.VMEM((Q, Q), f32),
            pltpu.VMEM((Q, OWN), bf16),
            pltpu.VMEM((Q, OWN), bf16),
            pltpu.VMEM((Q, OWN), bf16),
            pltpu.VMEM((Q, OWN), bf16),
            pltpu.VMEM((8, OWN), f32),
        ],
        compiler_params=pltpu.CompilerParams(
            dimension_semantics=("arbitrary",), vmem_limit_bytes=48 * 2**20
        ),
        cost_estimate=pl.CostEstimate(
            flops=30 * 10**9, bytes_accessed=36 * 2**20, transcendentals=2 * 10**7
        ),
        name="recurrence_backward",
    )(conv_in, conv_in, act, dy, y, bc, dt_tile, entry, taps, rows, skip_row)


def shifted_rows(array, steps):
    length = array.shape[0]
    if steps == 0:
        return array
    zeros = jnp.zeros((abs(steps),) + array.shape[1:], array.dtype)
    if steps > 0:
        return jnp.concatenate([zeros, array[: length - steps]], axis=0)
    return jnp.concatenate([array[-steps:], zeros], axis=0)


def per_device(
    hidden_in,
    widths,
    norm_gain,
    w_in,
    w_dt,
    conv_weight,
    dt_bias,
    a_log,
    skip_gain,
    gate_gain,
    w_out,
    grad_out,
):
    me = lax.axis_index("seq")
    tokens = hidden_in.shape[1]
    length = tokens * PART
    rows_in = w_in.shape[0]
    used_units = INNER // 8 * jnp.left_shift(jnp.int32(1), widths[0])
    units_float = used_units.astype(f32)
    block = jnp.arange(OWN) // LANES * PART + me
    unit_used = block * LANES < used_units
    head_used = ((jnp.arange(OWN_HEADS) // 2 * PART + me) * LANES < used_units).astype(f32)

    tail = jnp.concatenate(
        [
            heads_by_owner(w_dt),
            jnp.broadcast_to(norm_gain[None, :, None], (PART, rows_in, 1)),
            jnp.zeros((PART, rows_in, LANES - OWN_HEADS - 1 - OWN_BC), bf16),
            w_in[:, 2 * INNER :].reshape(rows_in, PART, OWN_BC).transpose(1, 0, 2),
        ],
        axis=2,
    )
    conv_pieces = jnp.concatenate([by_owner(w_in[:, INNER : 2 * INNER]), tail], axis=2)
    gate_pieces = by_owner(w_in[:, :INNER])
    out_rows = jnp.concatenate(
        [w_out, jnp.pad(gate_gain[:, None], ((0, 0), (0, LANES - 1)))], axis=1
    )

    x_all = seq_gather(hidden_in[0]).reshape(length, D)
    w_conv = gather_in(conv_pieces)
    w_gate = gather_in(gate_pieces)
    out_full = gather_out(out_rows)
    cot_all = seq_gather(grad_out[0]).reshape(length, D)
    w_o = out_full[:, :D]
    gate_row = out_full[:, D].astype(f32)[None, :]
    gain_row = w_conv[:, OWN + OWN_HEADS].astype(f32)[None, :]

    def own_heads(array):
        return lax.dynamic_index_in_dim(array.reshape(STRIPS, PART, 2), me, 1, False).reshape(-1)

    bias = own_heads(dt_bias)
    rate = -jnp.exp(own_heads(a_log))
    skip = own_heads(skip_gain)
    pad_heads = lambda a: jnp.pad(a, (0, LANES - OWN_HEADS))
    rows = jnp.stack(
        [pad_heads(bias), pad_heads(rate), pad_heads(head_used)] + [jnp.zeros((LANES,), f32)] * 5
    )
    skip_row = jnp.broadcast_to(jnp.repeat(skip, HEAD_DIM)[None, :], (8, OWN))
    taps = lax.dynamic_index_in_dim(
        conv_weight[:, :INNER].reshape(CONV, STRIPS, PART, LANES), me, 2, False
    ).reshape(CONV, OWN)
    taps = jnp.pad(taps.astype(f32), ((0, 8 - CONV), (0, 0)))
    taps_bc = lax.dynamic_slice_in_dim(conv_weight[:, INNER:], me * OWN_BC, OWN_BC, 1).astype(f32)

    x_float = x_all.astype(f32)
    inverse_rms = lax.rsqrt(jnp.mean(x_float * x_float, axis=1, keepdims=True) + epsilon)
    normed = (x_float * inverse_rms * gain_row).astype(bf16)
    dt_tile = dot_nn(normed, w_conv[:, OWN:])
    conv_bc = dt_tile[:, LANES - OWN_BC :].astype(bf16)
    conv_bc_float = conv_bc.astype(f32)
    pre_bc = sum(
        taps_bc[tap] * shifted_rows(conv_bc_float, CONV - 1 - tap) for tap in range(CONV)
    )
    act_bc = (pre_bc * sigmoid(pre_bc)).astype(bf16)
    bc = seq_gather(act_bc).transpose(1, 0, 2).reshape(length, 2 * STATE)
    conv_in = jnp.where(unit_used, dot_nn(normed, w_conv[:, :OWN]), 0.0).astype(bf16)
    y, act, entry = recurrence_forward(conv_in, bc, dt_tile, taps, rows, skip_row)
    z = jnp.where(unit_used, dot_nn(normed, w_gate), 0.0)
    d_rounded = dot_nt(cot_all, w_o)
    squashed = sigmoid(z)
    gate_act = z * squashed
    gated = y * gate_act
    e_gate = d_rounded * gate_row
    sums = jnp.stack(
        [jnp.sum(gated * gated, axis=1), jnp.sum(e_gate * gated, axis=1)]
    ).reshape(2, length // LANES, LANES)
    sums = seq_total(sums).reshape(2, length)
    inverse_gate = lax.rsqrt(sums[0] / units_float + epsilon)
    pull = (inverse_gate**3 * sums[1] / units_float)[:, None]
    inverse_gate = inverse_gate[:, None]
    normalized = gated * inverse_gate
    rounded_out = (normalized * gate_row).astype(bf16)
    grad_gate_local = jnp.sum(d_rounded * normalized, axis=0)
    d_gated = inverse_gate * e_gate - gated * pull
    d_y = (d_gated * gate_act).astype(bf16)
    d_z = (d_gated * y * squashed * (1.0 + z * (1.0 - squashed))).astype(bf16)

    grad_w_out = scatter_out(dot_tn(rounded_out, cot_all).astype(bf16))
    branch = dot_nn(rounded_out, w_o).astype(bf16).reshape(PART, tokens, D)
    x_own = hidden_in[0].astype(f32)
    hidden_out = (x_own + seq_scatter(branch)).astype(bf16)[None]
    grad_gate_in = scatter_in(dot_tn(normed, d_z).astype(bf16))

    d_conv_in, d_bc, d_dt, g_conv, g_rows = recurrence_backward(
        conv_in, act, d_y, y, bc, dt_tile, entry, taps, rows, skip_row
    )
    d_act_bc = seq_scatter(d_bc.reshape(length, PART, OWN_BC).transpose(1, 0, 2))
    squashed_bc = sigmoid(pre_bc)
    d_pre_bc = d_act_bc * squashed_bc * (1.0 + pre_bc * (1.0 - squashed_bc))
    g_conv_bc = jnp.stack(
        [
            jnp.sum(d_pre_bc * shifted_rows(conv_bc_float, CONV - 1 - tap), axis=0)
            for tap in range(CONV)
        ]
    )
    d_conv_bc = sum(
        taps_bc[tap] * shifted_rows(d_pre_bc, tap - (CONV - 1)) for tap in range(CONV)
    ).astype(bf16)
    d_project = jnp.concatenate(
        [
            d_conv_in,
            d_dt[:, :OWN_HEADS].astype(bf16),
            jnp.zeros((length, LANES - OWN_HEADS - OWN_BC), bf16),
            d_conv_bc,
        ],
        axis=1,
    )
    grad_conv_in = scatter_in(dot_tn(normed, d_project).astype(bf16))
    d_normed = dot_nt(d_z, w_gate) + dot_nt(d_project, w_conv)
    grad_norm_local = jnp.sum(d_normed * (x_float * inverse_rms), axis=0)
    d_own = seq_scatter(d_normed.astype(bf16).reshape(PART, tokens, D))
    own_rms = lax.rsqrt(jnp.mean(x_own * x_own, axis=1, keepdims=True) + epsilon)
    d_scaled = d_own * gain_row
    d_input = own_rms * d_scaled - x_own * own_rms**3 * jnp.mean(
        d_scaled * x_own, axis=1, keepdims=True
    )
    grad_in = (grad_out[0].astype(f32) + d_input).astype(bf16)[None]

    g_skip = jnp.sum(g_conv[4].reshape(OWN_HEADS, HEAD_DIM), axis=1)
    small = jnp.concatenate(
        [
            g_conv[:CONV].reshape(-1),
            g_conv_bc.reshape(-1),
            pad_heads(g_rows[0, :OWN_HEADS]),
            pad_heads(g_rows[1, :OWN_HEADS]),
            pad_heads(g_skip),
            grad_norm_local,
            grad_gate_local,
        ]
    )
    count = small.shape[0]
    padded = -(-count // (8 * LANES)) * 8 * LANES
    small = jnp.pad(small, (0, padded - count)).reshape(-1, LANES)
    every = seq_gather(dp_total(small)).reshape(PART, padded)
    start = 0

    def take(size):
        nonlocal start
        start += size
        return every[:, start - size : start]

    all_conv = take(CONV * OWN).reshape(PART, CONV, OWN)
    all_conv_bc = take(CONV * OWN_BC).reshape(PART, CONV, OWN_BC)
    head_sums = [heads_from_owner(take(LANES)[:, None, :OWN_HEADS]).reshape(HEADS) for _ in range(3)]
    grad_norm = jnp.sum(take(D), axis=0)
    grad_gate = lax.dynamic_index_in_dim(take(OWN), me, 0, False)
    grad_conv = jnp.concatenate(
        [from_owner(all_conv), all_conv_bc.transpose(1, 0, 2).reshape(CONV, 2 * STATE)], axis=1
    )
    place = lax.axis_index(("dp", "seq"))
    norm_rows = norm_gain.shape[0]
    grad_norm_gain = lax.dynamic_slice_in_dim(grad_norm, place * norm_rows, norm_rows, 0)
    gate_rows = gate_gain.shape[0]
    if gate_rows == LANES:
        grad_gate_gain = lax.dynamic_slice_in_dim(
            grad_gate, lax.axis_index("dp") * gate_rows, gate_rows, 0
        )
    else:
        start = CONV * OWN + CONV * OWN_BC + 3 * LANES + D
        whole_gate = from_owner(take(OWN)[:, None, :]).reshape(INNER)
        grad_gate_gain = lax.dynamic_slice_in_dim(whole_gate, place * gate_rows, gate_rows, 0)

    grad_w_in = jnp.concatenate(
        [
            from_owner(grad_gate_in),
            from_owner(grad_conv_in[:, :, :OWN]),
            grad_conv_in[:, :, CONV_COLS - OWN_BC :].transpose(1, 0, 2).reshape(rows_in, 2 * STATE),
        ],
        axis=1,
    )
    grad_w_dt = heads_from_owner(grad_conv_in[:, :, OWN : OWN + OWN_HEADS])
    return (
        hidden_out,
        grad_in,
        grad_norm_gain,
        grad_w_in,
        grad_w_dt,
        grad_conv,
        head_sums[0],
        head_sums[1],
        head_sums[2],
        grad_gate_gain,
        grad_w_out,
    )


def solution(mesh):
    return jax.shard_map(
        per_device,
        mesh=mesh,
        in_specs=(
            P("dp", "seq", None),
            P("dp"),
            P(("dp", "seq")),
            P(("dp", "seq"), None),
            P(("dp", "seq"), None),
            P(),
            P(),
            P(),
            P(),
            P(("dp", "seq")),
            P(("dp", "seq"), None),
            P("dp", "seq", None),
        ),
        out_specs=(
            P("dp", "seq", None),
            P("dp", "seq", None),
            P(("dp", "seq")),
            P(("dp", "seq"), None),
            P(("dp", "seq"), None),
            P(),
            P(),
            P(),
            P(),
            P(("dp", "seq")),
            P(("dp", "seq"), None),
        ),
        check_vma=False,
    )
```

```python
import functools

import jax
import jax.numpy as jnp
from jax import lax
from jax.experimental import pallas as pl
from jax.experimental.pallas import tpu as pltpu
from jax.sharding import PartitionSpec as P

D = 2048
INNER = 4096
HEAD_DIM = 64
STATE = 128
CONV = 4
HEADS = 64
CHANNELS = 4352

PART = 4
LANES = 128
STRIPS = INNER // LANES // PART
OWN = STRIPS * LANES
OWN_HEADS = OWN // HEAD_DIM
OWN_BC = 2 * STATE // PART
CONV_COLS = OWN + LANES
Q = 256
HALF = Q // 2

epsilon = 1e-05
highest = lax.Precision.HIGHEST
f32 = jnp.float32
bf16 = jnp.bfloat16
LOG2E = 1.4426950408889634


def swap(value, axis, pairs):
    return lax.ppermute(value, axis, pairs)


def xor_seq(value, bits):
    return lax.ppermute(value, "seq", [(s, s ^ bits) for s in range(PART)])


def core_halves(blocks):
    core = lax.axis_index("seq") % 2
    view = blocks.reshape((2, 2) + blocks.shape[1:])
    mine = lax.dynamic_index_in_dim(view, core, 1, False)
    other = lax.dynamic_index_in_dim(view, 1 - core, 1, False)
    return mine, xor_seq(other, 1)


def halves_sum(mine, received):
    row = lax.axis_index("seq") // 2

    def of(which):
        a = lax.dynamic_index_in_dim(mine, which, 0, False)
        return a.astype(f32) + lax.dynamic_index_in_dim(received, which, 0, False).astype(f32)

    return of(row), of(1 - row).astype(bf16)


def seq_scatter_relative(blocks):
    view = blocks.reshape((2, 2) + blocks.shape[1:])
    half = view[:, 0].astype(f32) + xor_seq(view[:, 1], 1).astype(f32)
    return half[0] + xor_seq(half[1].astype(bf16), 2).astype(f32)


def by_partner(pieces):
    me = lax.axis_index("seq")
    odd, lower = me % 2 == 1, me >= 2
    a, b, c, d = pieces
    a, b = jnp.where(odd, b, a), jnp.where(odd, a, b)
    c, d = jnp.where(odd, d, c), jnp.where(odd, c, d)
    return (
        jnp.where(lower, c, a),
        jnp.where(lower, d, b),
        jnp.where(lower, a, c),
        jnp.where(lower, b, d),
    )


def seq_transpose(pieces):
    turned = by_partner([pieces[k] for k in range(PART)])
    moved = [turned[0]] + [xor_seq(turned[k], k) for k in range(1, PART)]
    return jnp.stack(by_partner(moved))


def seq_total(value):
    value = value + xor_seq(value, 1)
    return value + xor_seq(value, 2)


def fast_mesh():
    return lax.axis_size("dp") == 8


def dp_shift_z(value, steps):
    pairs = [(z * 2 + x, (z + steps) % 4 * 2 + x) for z in range(4) for x in range(2)]
    return lax.ppermute(value, "dp", pairs)


def dp_swap_x(value):
    return lax.ppermute(value, "dp", [(d, d ^ 1) for d in range(8)])


def tie_kernel(*refs):
    del refs


def tie(*values):
    anywhere = pl.BlockSpec(memory_space=pl.ANY)
    return pl.pallas_call(
        tie_kernel,
        in_specs=[anywhere] * len(values),
        out_specs=[anywhere] * len(values),
        out_shape=[jax.ShapeDtypeStruct(v.shape, v.dtype) for v in values],
        input_output_aliases={k: k for k in range(len(values))},
        name="tie",
    )(*values)


def after(values, needed):
    anywhere = pl.BlockSpec(memory_space=pl.ANY)
    return pl.pallas_call(
        tie_kernel,
        in_specs=[anywhere] * (len(values) + len(needed)),
        out_specs=[anywhere] * len(values),
        out_shape=[jax.ShapeDtypeStruct(v.shape, v.dtype) for v in values],
        input_output_aliases={k: k for k in range(len(values))},
        name="after",
    )(*values, *needed)


def assemble_kernel(places_ref, *refs):
    rows = refs[0].shape[0]
    for k, piece in enumerate(refs[:-1]):
        refs[-1][pl.ds(pl.multiple_of(places_ref[k] * rows, rows), rows), :] = piece[...]


def assemble(pieces, places, tile):
    rows, columns = pieces[0].shape
    count = len(pieces)
    along = lambda i, places: (0, i)
    return pl.pallas_call(
        assemble_kernel,
        grid_spec=pltpu.PrefetchScalarGridSpec(
            num_scalar_prefetch=1,
            grid=(columns // tile,),
            in_specs=[pl.BlockSpec((rows, tile), along)] * count,
            out_specs=pl.BlockSpec((rows * count, tile), along),
        ),
        out_shape=jax.ShapeDtypeStruct((rows * count, columns), pieces[0].dtype),
        compiler_params=pltpu.CompilerParams(vmem_limit_bytes=24 * 2**20),
        cost_estimate=pl.CostEstimate(
            flops=0, bytes_accessed=4 * rows * count * columns, transcendentals=0
        ),
        name="assemble",
    )(places, *pieces)


def seq_pass(pieces):
    me = lax.axis_index("seq")
    core, row = me % 2, me // 2
    view = pieces.reshape((2, 2) + pieces.shape[1:])
    give = lax.dynamic_index_in_dim(view, 1 - row, 0, False)
    keep = lax.dynamic_index_in_dim(view, row, 0, False)
    got = xor_seq(give, 2)
    lower = jnp.where(row == 0, keep, got)
    upper = jnp.where(row == 0, got, keep)
    both = jnp.stack([lower, upper])
    mine = lax.dynamic_index_in_dim(both, core, 1, False)
    other = xor_seq(lax.dynamic_index_in_dim(both, 1 - core, 1, False), 1)
    first = jnp.where(core == 0, mine, other)
    second = jnp.where(core == 0, other, mine)
    return jnp.stack([first, second], axis=1).reshape(pieces.shape)


def seq_pieces(block, after=None):
    source = block if after is None else tie(block, after)[0]
    across = xor_seq(source, 2)
    return block, xor_seq(block, 1), across, xor_seq(across, 1)


def gather_everything(conv_pieces, gate_pieces, o, x_block):
    c = seq_pass(conv_pieces).reshape(-1, CONV_COLS)
    w_conv = lax.all_gather(c, "dp", axis=0, tiled=True)
    x_across, gate_pieces = after([xor_seq(after([x_block], [c])[0], 2), gate_pieces], [])
    g = seq_pass(gate_pieces).reshape(-1, OWN)
    o_x, g, x_across, o = after([dp_swap_x(o), g, x_across, o], [w_conv])
    x_pieces = (x_block, xor_seq(x_block, 1), x_across, xor_seq(x_across, 1))
    w_gate = lax.all_gather(g, "dp", axis=0, tiled=True)
    out_rows = [o] + [dp_shift_z(o, steps) for steps in range(1, 4)] + [o_x]
    return w_conv, w_gate, out_rows, x_pieces


def out_places():
    dp = lax.axis_index("dp")
    sources = (dp // 2 - jnp.arange(4, dtype=jnp.int32) + 4) % 4 * 2
    return jnp.concatenate([sources + dp % 2, sources + 1 - dp % 2]).astype(jnp.int32)


def norm_rows(x, gain):
    x = x.astype(f32)
    inverse = lax.rsqrt(jnp.mean(x * x, axis=1, keepdims=True) + epsilon)
    return (x * inverse * gain).astype(bf16)


def positions_kernel(shares, with_norm, order_ref, *refs):
    step = pl.program_id(0)
    first = 0
    for k, share in enumerate(shares):

        @pl.when((step >= first) & (step < first + share))
        def _():
            if with_norm:
                refs[-1][...] = norm_rows(refs[k][...], refs[-2][0:1, :])
            else:
                refs[-1][...] = refs[k][...]

        first += share


def all_positions(pieces, order, gain_rows=None):
    tile = min(256, min(p.shape[0] for p in pieces))
    shares = [p.shape[0] // tile for p in pieces]
    steps = sum(shares)
    each = steps // PART

    def place(first, share):
        return lambda i, order: (jnp.clip(i - first, 0, share - 1), 0)

    specs, first = [], 0
    for share in shares:
        specs.append(pl.BlockSpec((tile, D), place(first, share)))
        first += share
    extra = []
    if gain_rows is not None:
        specs.append(pl.BlockSpec((8, D), lambda i, order: (0, 0)))
        extra.append(gain_rows)
    return pl.pallas_call(
        functools.partial(positions_kernel, shares, gain_rows is not None),
        grid_spec=pltpu.PrefetchScalarGridSpec(
            num_scalar_prefetch=1,
            grid=(steps,),
            in_specs=specs,
            out_specs=pl.BlockSpec((tile, D), lambda i, order: (order[i // each] * each + i % each, 0)),
        ),
        out_shape=jax.ShapeDtypeStruct((tile * steps, D), bf16),
        compiler_params=pltpu.CompilerParams(vmem_limit_bytes=32 * 2**20),
        cost_estimate=pl.CostEstimate(
            flops=4 * tile * steps * D, bytes_accessed=4 * tile * steps * D, transcendentals=0
        ),
        name="all_positions",
    )(order, *pieces, *extra)


def x_parts(blocks):
    x = lax.axis_index("dp") % 2
    view = blocks.reshape((4, 2) + blocks.shape[1:])
    mine = lax.dynamic_index_in_dim(view, x, 1, False)
    return mine, lax.dynamic_index_in_dim(view, 1 - x, 1, False)


def x_halves(blocks):
    mine, other = x_parts(blocks)
    return mine, dp_swap_x(other)


def z_gives(mine, received):
    z = lax.axis_index("dp") // 2

    def of(steps):
        which = (z + steps) % 4
        a = lax.dynamic_index_in_dim(mine, which, 0, False)
        return a.astype(f32) + lax.dynamic_index_in_dim(received, which, 0, False).astype(f32)

    return of(0), [of(steps).astype(bf16) for steps in range(1, 4)]


def dp_total(value):
    if not fast_mesh():
        return lax.psum(value, "dp")
    value = value + dp_swap_x(value)
    return value + dp_shift_z(value, 1) + dp_shift_z(value, 2) + dp_shift_z(value, 3)


def by_owner(columns):
    rows = columns.shape[0]
    return (
        columns.reshape(rows, STRIPS, PART, LANES).transpose(2, 0, 1, 3).reshape(PART, rows, OWN)
    )


def from_owner(pieces):
    rows = pieces.shape[1]
    return (
        pieces.reshape(PART, rows, STRIPS, LANES).transpose(1, 2, 0, 3).reshape(rows, INNER)
    )


def heads_by_owner(columns):
    rows = columns.shape[0]
    return (
        columns.reshape(rows, STRIPS, PART, 2).transpose(2, 0, 1, 3).reshape(PART, rows, OWN_HEADS)
    )


def heads_from_owner(pieces):
    rows = pieces.shape[1]
    return (
        pieces.reshape(PART, rows, STRIPS, 2).transpose(1, 2, 0, 3).reshape(rows, HEADS)
    )


def gather_in(pieces):
    full = lax.all_gather(pieces, ("dp", "seq"), axis=1, tiled=True)
    return lax.dynamic_index_in_dim(full, lax.axis_index("seq"), 0, False)


def dp_sum(product):
    return lax.psum_scatter(product, "dp", scatter_dimension=0, tiled=True)


def owners_rows(total):
    return seq_transpose(total.astype(bf16).reshape(PART, -1, total.shape[1])).astype(f32)


def scatter_in(grads):
    full = jnp.zeros((PART,) + grads.shape, grads.dtype)
    full = lax.dynamic_update_index_in_dim(full, grads, lax.axis_index("seq"), 0)
    return lax.psum_scatter(full, ("dp", "seq"), scatter_dimension=1, tiled=True).astype(f32)


def gather_out(rows):
    full = lax.all_gather(rows, ("dp", "seq"), axis=0, tiled=True)
    full = full.reshape(STRIPS, PART, LANES, -1)
    return lax.dynamic_index_in_dim(full, lax.axis_index("seq"), 1, False).reshape(OWN, -1)


def gather_plainly(conv_pieces, gate_pieces, out_rows, x_block):
    return (
        gather_in(conv_pieces),
        gather_in(gate_pieces),
        gather_out(out_rows),
        seq_pieces(x_block),
    )


def scatter_out(grads):
    full = jnp.zeros((STRIPS, PART, LANES, grads.shape[1]), grads.dtype)
    full = lax.dynamic_update_index_in_dim(
        full, grads.reshape(STRIPS, LANES, -1), lax.axis_index("seq"), 1
    )
    full = full.reshape(INNER, -1)
    return lax.psum_scatter(full, ("dp", "seq"), scatter_dimension=0, tiled=True).astype(f32)


def dot_nn(a, b):
    return lax.dot_general(a, b, (((1,), (0,)), ((), ())), preferred_element_type=f32)


def dot_nt(a, b):
    return lax.dot_general(a, b, (((1,), (1,)), ((), ())), preferred_element_type=f32)


def dot_tn(a, b):
    return lax.dot_general(a, b, (((0,), (0,)), ((), ())), preferred_element_type=f32)


def dot_exact(a, b):
    return lax.dot_general(
        a, b, (((1,), (0,)), ((), ())), precision=highest, preferred_element_type=f32
    )


def sigmoid(v):
    return 0.5 + 0.5 * jnp.tanh(0.5 * v)


def bc_forward_kernel(tile_ref, taps_ref, out_ref, padded):
    length = tile_ref.shape[0]
    padded[0:8, :] = jnp.zeros((8, LANES), f32)
    padded[8 : 8 + length, :] = tile_ref[...].astype(bf16).astype(f32)
    left = lax.broadcasted_iota(jnp.int32, (1, LANES), 1) < OWN_BC
    for block in range(length // Q):
        start = block * Q
        pre = taps_ref[0:1, :] * padded[start + 5 : start + 5 + Q, :]
        for tap in range(1, CONV):
            pre = pre + taps_ref[tap : tap + 1, :] * padded[start + 5 + tap : start + 5 + tap + Q, :]
        act = pre * sigmoid(pre)
        packed = jnp.where(left, pltpu.roll(act[HALF:], OWN_BC, 1), act[:HALF])
        out_ref[block * HALF : (block + 1) * HALF, :] = packed.astype(bf16)


def bc_forward(dt_tile, taps_tile):
    length = dt_tile.shape[0]
    return pl.pallas_call(
        bc_forward_kernel,
        out_shape=jax.ShapeDtypeStruct((length // 2, LANES), bf16),
        scratch_shapes=[pltpu.VMEM((8 + length, LANES), f32)],
        compiler_params=pltpu.CompilerParams(vmem_limit_bytes=16 * 2**20),
        cost_estimate=pl.CostEstimate(
            flops=20 * length * LANES, bytes_accessed=5 * length * LANES, transcendentals=0
        ),
        name="bc_forward",
    )(dt_tile, taps_tile)


def tail_kernel(tile_ref, grad_ref, ddt_ref, taps_ref, into_ref, out_ref, sums_ref, padded, dp):
    del into_ref
    length = tile_ref.shape[0]
    padded[0:8, :] = jnp.zeros((8, LANES), f32)
    padded[8 : 8 + length, :] = tile_ref[...].astype(bf16).astype(f32)
    dp[length : length + 8, :] = jnp.zeros((8, LANES), f32)
    lane = lax.broadcasted_iota(jnp.int32, (1, LANES), 1)
    left = lane < OWN_BC
    sums_ref[...] = jnp.zeros_like(sums_ref)
    for block in reversed(range(length // Q)):
        start = block * Q
        taken = [padded[start + 5 + tap : start + 5 + tap + Q, :] for tap in range(CONV)]
        pre = taps_ref[0:1, :] * taken[0]
        for tap in range(1, CONV):
            pre = pre + taps_ref[tap : tap + 1, :] * taken[tap]
        packed = grad_ref[block * HALF : (block + 1) * HALF, :]
        grad = jnp.concatenate([packed, pltpu.roll(packed, OWN_BC, 1)], axis=0)
        squashed = sigmoid(pre)
        d_pre = jnp.where(left, 0.0, grad * squashed * (1.0 + pre * (1.0 - squashed)))
        dp[start : start + Q, :] = d_pre
        for tap in range(CONV):
            sums_ref[tap : tap + 1, :] += jnp.sum(d_pre * taken[tap], axis=0, keepdims=True)
        d_in = taps_ref[CONV - 1 : CONV, :] * d_pre
        for tap in range(CONV - 1):
            first = start + CONV - 1 - tap
            d_in = d_in + taps_ref[tap : tap + 1, :] * dp[first : first + Q, :]
        d_dt = jnp.where(lane < OWN_HEADS, ddt_ref[start : start + Q, :], 0.0)
        out_ref[start : start + Q, :] = jnp.where(left, d_dt, d_in).astype(bf16)


def tail_backward(dt_tile, grad, d_dt, taps_tile, into):
    length = dt_tile.shape[0]
    whole = lambda i: (0, 0)
    return pl.pallas_call(
        tail_kernel,
        grid=(1,),
        in_specs=[
            pl.BlockSpec((length, LANES), whole),
            pl.BlockSpec((length // 2, LANES), whole),
            pl.BlockSpec((length, LANES), whole),
            pl.BlockSpec((8, LANES), whole),
            pl.BlockSpec(memory_space=pl.ANY),
        ],
        out_specs=[
            pl.BlockSpec((length, LANES), lambda i: (0, STRIPS)),
            pl.BlockSpec((8, LANES), whole),
        ],
        out_shape=[
            jax.ShapeDtypeStruct(into.shape, bf16),
            jax.ShapeDtypeStruct((8, LANES), f32),
        ],
        input_output_aliases={4: 0},
        scratch_shapes=[pltpu.VMEM((8 + length, LANES), f32), pltpu.VMEM((8 + length, LANES), f32)],
        compiler_params=pltpu.CompilerParams(vmem_limit_bytes=24 * 2**20),
        cost_estimate=pl.CostEstimate(
            flops=40 * length * LANES, bytes_accessed=14 * length * LANES, transcendentals=0
        ),
        name="tail_backward",
    )(dt_tile, grad, d_dt, taps_tile, into)


def keys_and_reads(me, refs):
    odd, lower = me % 2 == 1, me >= 2
    p = [ref[...].astype(f32) for ref in refs]
    r0, r1 = jnp.where(odd, p[1], p[0]), jnp.where(odd, p[0], p[1])
    r2, r3 = jnp.where(odd, p[3], p[2]), jnp.where(odd, p[2], p[3])
    q = (
        jnp.where(lower, r2, r0),
        jnp.where(lower, r3, r1),
        jnp.where(lower, r0, r2),
        jnp.where(lower, r1, r3),
    )
    left = lax.broadcasted_iota(jnp.int32, (1, LANES), 1) < OWN_BC

    def join(a, b):
        top = jnp.where(left, pltpu.roll(a, OWN_BC, 1), b)
        bottom = jnp.where(left, a, pltpu.roll(b, OWN_BC, 1))
        return jnp.concatenate([top, bottom], axis=0).astype(bf16)

    return join(q[0], q[1]), join(q[2], q[3])


def give_back(me, d_keys, d_reads, out_ref):
    left = lax.broadcasted_iota(jnp.int32, (1, LANES), 1) < OWN_BC
    for pair, array in enumerate((d_keys, d_reads)):
        top, bottom = array[:HALF], array[HALF:]
        low = jnp.where(left, bottom, pltpu.roll(top, OWN_BC, 1))
        high = jnp.where(left, pltpu.roll(bottom, OWN_BC, 1), top)
        out_ref[jnp.bitwise_xor(me, 2 * pair)] = low.astype(bf16)
        out_ref[jnp.bitwise_xor(me, 2 * pair + 1)] = high.astype(bf16)


def decay_terms(dt_ref, rows_ref):
    v = dt_ref[...] * rows_ref[2:3, :] + rows_ref[0:1, :]
    steps = jnp.maximum(v, 0.0) + jnp.log1p(jnp.exp(-jnp.abs(v)))
    log2_decay = rows_ref[1:2, :] * LOG2E * steps
    row = lax.broadcasted_iota(jnp.int32, (Q, Q), 0)
    column = lax.broadcasted_iota(jnp.int32, (Q, Q), 1)
    lower = jnp.where(row >= column, 1.0, 0.0)
    running = dot_exact(lower, log2_decay)
    shifted = running - jnp.log(steps) * LOG2E
    end = running[Q - 1 : Q, :]
    return v, steps, running, shifted, end


def forward_kernel(
    me_ref, ci_ref, b0, b1, b2, b3, dt_ref, cw_ref, rows_ref, skip_ref, y_ref, act_ref, s_ref, state, xf
):
    @pl.when(pl.program_id(0) == 0)
    def _():
        state[...] = jnp.zeros_like(state)
        xf[0:8, :] = jnp.zeros((8, OWN), f32)

    @pl.when(pl.program_id(0) > 0)
    def _():
        xf[0:8, :] = xf[Q : Q + 8, :]

    xf[8 : Q + 8, :] = ci_ref[...].astype(f32)
    _, _, running, shifted, end = decay_terms(dt_ref, rows_ref)
    shifted_t = shifted.T
    e_run = jnp.exp2(running)
    w_end = jnp.exp2(end - shifted)
    e_end = jnp.exp2(end)
    keys, reads = keys_and_reads(me_ref[0], (b0, b1, b2, b3))
    keys_t = keys.T
    cb = dot_nt(reads, keys)
    causal = lax.broadcasted_iota(jnp.int32, (HALF, HALF), 0) >= lax.broadcasted_iota(
        jnp.int32, (HALF, HALF), 1
    )
    left = lax.broadcasted_iota(jnp.int32, (1, LANES), 1) < HEAD_DIM
    s_ref[0] = state[...].astype(bf16)
    for strip in range(STRIPS):
        at = slice(strip * LANES, (strip + 1) * LANES)
        h0, h1 = 2 * strip, 2 * strip + 1
        pre = cw_ref[0:1, at] * xf[5 : 5 + Q, at]
        for tap in range(1, CONV):
            pre = pre + cw_ref[tap : tap + 1, at] * xf[5 + tap : 5 + tap + Q, at]
        act = (pre * sigmoid(pre)).astype(bf16)
        act_ref[:, at] = act
        actf = act.astype(f32)
        inter = dot_nn(reads, s_ref[0, :, at]) * jnp.where(
            left, e_run[:, h0 : h0 + 1], e_run[:, h1 : h1 + 1]
        )
        inter = inter + skip_ref[0:1, at] * actf
        top, bottom = inter[:HALF], inter[HALF:]
        for h, side in ((h0, left), (h1, jnp.logical_not(left))):
            x_h = jnp.where(side, actf, 0.0).astype(bf16)
            m00 = jnp.where(
                causal,
                jnp.exp2(running[:HALF, h : h + 1] - shifted_t[h : h + 1, :HALF]) * cb[:HALF, :HALF],
                0.0,
            )
            m10 = jnp.exp2(running[HALF:, h : h + 1] - shifted_t[h : h + 1, :HALF]) * cb[HALF:, :HALF]
            m11 = jnp.where(
                causal,
                jnp.exp2(running[HALF:, h : h + 1] - shifted_t[h : h + 1, HALF:]) * cb[HALF:, HALF:],
                0.0,
            )
            top = top + dot_nn(m00.astype(bf16), x_h[:HALF])
            bottom = bottom + dot_nn(
                jnp.concatenate([m10.astype(bf16), m11.astype(bf16)], axis=1), x_h
            )
        y_ref[:HALF, at] = top
        y_ref[HALF:, at] = bottom
        weighted = (actf * jnp.where(left, w_end[:, h0 : h0 + 1], w_end[:, h1 : h1 + 1])).astype(bf16)
        state[:, at] = state[:, at] * jnp.where(
            left, e_end[:, h0 : h0 + 1], e_end[:, h1 : h1 + 1]
        ) + dot_nn(keys_t, weighted)


def recurrence_forward(me, conv_in, bc, dt_tile, taps, rows, skip_row):
    length = conv_in.shape[0]
    blocks = length // Q
    whole = lambda i, me: (0, 0)
    along = lambda i, me: (i, 0)
    return pl.pallas_call(
        forward_kernel,
        grid_spec=pltpu.PrefetchScalarGridSpec(
            num_scalar_prefetch=1,
            grid=(blocks,),
            in_specs=[pl.BlockSpec((Q, OWN), along)]
            + [pl.BlockSpec((HALF, LANES), along)] * PART
            + [
                pl.BlockSpec((Q, LANES), along),
                pl.BlockSpec((8, OWN), whole),
                pl.BlockSpec((8, LANES), whole),
                pl.BlockSpec((8, OWN), whole),
            ],
            out_specs=[
                pl.BlockSpec((Q, OWN), along),
                pl.BlockSpec((Q, OWN), along),
                pl.BlockSpec((1, STATE, OWN), lambda i, me: (i, 0, 0)),
            ],
            scratch_shapes=[pltpu.VMEM((STATE, OWN), f32), pltpu.VMEM((Q + 8, OWN), f32)],
        ),
        out_shape=[
            jax.ShapeDtypeStruct((length, OWN), f32),
            jax.ShapeDtypeStruct((length, OWN), bf16),
            jax.ShapeDtypeStruct((blocks, STATE, OWN), bf16),
        ],
        compiler_params=pltpu.CompilerParams(
            dimension_semantics=("arbitrary",), vmem_limit_bytes=40 * 2**20
        ),
        cost_estimate=pl.CostEstimate(
            flops=30 * 10**9, bytes_accessed=2**24, transcendentals=10**7
        ),
        name="recurrence_forward",
    )(me, conv_in, *bc, dt_tile, taps, rows, skip_row)


def backward_kernel(
    me_ref,
    ci_ref,
    prev_ref,
    act_ref,
    dy_ref,
    y_ref,
    b0,
    b1,
    b2,
    b3,
    dt_ref,
    s_ref,
    cw_ref,
    rows_ref,
    skip_ref,
    dci_ref,
    dbc_ref,
    ddt_ref,
    gconv_ref,
    grow_ref,
    back,
    back16,
    dp,
    xf,
    edy,
    wx,
    dcb,
    p12h,
    p12l,
    p3,
    p23,
    cross,
):
    step = pl.program_id(0)
    last = pl.num_programs(0) - 1

    @pl.when(step == 0)
    def _():
        back[...] = jnp.zeros_like(back)
        dp[Q : Q + 8, :] = jnp.zeros((8, OWN), f32)
        gconv_ref[...] = jnp.zeros_like(gconv_ref)
        grow_ref[...] = jnp.zeros_like(grow_ref)
        cross[...] = jnp.zeros_like(cross)

    @pl.when(step > 0)
    def _():
        dp[Q : Q + 8, :] = dp[0:8, :]

    before = prev_ref[8:16, :].astype(f32)
    xf[0:8, :] = jnp.where(step == last, 0.0, before)
    xf[8 : Q + 8, :] = ci_ref[...].astype(f32)
    v, steps, running, shifted, end = decay_terms(dt_ref, rows_ref)
    running_t = running.T
    e_run = jnp.exp2(running)
    w_end = jnp.exp2(end - shifted)
    e_end = jnp.exp2(end)
    keys, reads = keys_and_reads(me_ref[0], (b0, b1, b2, b3))
    reads_t = reads.T
    cbt = dot_nt(keys, reads)
    ahead = lax.broadcasted_iota(jnp.int32, (HALF, HALF), 0) <= lax.broadcasted_iota(
        jnp.int32, (HALF, HALF), 1
    )
    left = lax.broadcasted_iota(jnp.int32, (1, LANES), 1) < HEAD_DIM
    back16[...] = back[...].astype(bf16)
    dcb[...] = jnp.zeros_like(dcb)
    for strip in range(STRIPS):
        at = slice(strip * LANES, (strip + 1) * LANES)
        h0, h1 = 2 * strip, 2 * strip + 1
        act = act_ref[:, at]
        dy = dy_ref[:, at]
        actf = act.astype(f32)
        dyf = dy.astype(f32)
        skip = skip_ref[0:1, at]
        w_pair = jnp.where(left, w_end[:, h0 : h0 + 1], w_end[:, h1 : h1 + 1])
        e_pair = jnp.where(left, e_run[:, h0 : h0 + 1], e_run[:, h1 : h1 + 1])
        decayed = (dyf * e_pair).astype(bf16)
        edy[:, at] = decayed
        wx[:, at] = (actf * w_pair).astype(bf16)
        inter = dot_nn(keys, back16[:, at]) * w_pair
        top = jnp.zeros((HALF, LANES), f32)
        bottom = jnp.zeros((HALF, LANES), f32)
        for h, side in ((h0, left), (h1, jnp.logical_not(left))):
            x_h = jnp.where(side, actf, 0.0).astype(bf16)
            dy_h = jnp.where(side, dyf, 0.0).astype(bf16)
            g_top = dot_nt(x_h[:HALF], dy)
            g_bottom = dot_nt(x_h[HALF:], dy[HALF:])
            l00 = jnp.exp2(running_t[h : h + 1, :HALF] - shifted[:HALF, h : h + 1])
            l01 = jnp.exp2(running_t[h : h + 1, HALF:] - shifted[:HALF, h : h + 1])
            l11 = jnp.exp2(running_t[h : h + 1, HALF:] - shifted[HALF:, h : h + 1])
            m00 = jnp.where(ahead, l00 * cbt[:HALF, :HALF], 0.0).astype(bf16)
            m01 = (l01 * cbt[:HALF, HALF:]).astype(bf16)
            m11 = jnp.where(ahead, l11 * cbt[HALF:, HALF:], 0.0).astype(bf16)
            top = top + dot_nn(jnp.concatenate([m00, m01], axis=1), dy_h)
            bottom = bottom + dot_nn(m11, dy_h[HALF:])
            dcb[:HALF, :HALF] += jnp.where(ahead, l00 * g_top[:, :HALF], 0.0)
            dcb[:HALF, HALF:] += l01 * g_top[:, HALF:]
            dcb[HALF:, HALF:] += jnp.where(ahead, l11 * g_bottom, 0.0)
        intra = jnp.concatenate([top, bottom], axis=0)
        d_values = intra + inter
        p_12 = dyf * (y_ref[:, at] - skip * actf) - actf * intra
        p_12h = p_12.astype(bf16)
        p12h[:, at] = p_12h
        p12l[:, at] = (p_12 - p_12h.astype(f32)).astype(bf16)
        p3[:, at] = (actf * inter).astype(bf16)
        p23[:, at] = (actf * d_values).astype(bf16)
        d_act = d_values + skip * dyf
        pre = cw_ref[0:1, at] * xf[5 : 5 + Q, at]
        for tap in range(1, CONV):
            pre = pre + cw_ref[tap : tap + 1, at] * xf[5 + tap : 5 + tap + Q, at]
        squashed = sigmoid(pre)
        d_pre = d_act * squashed * (1.0 + pre * (1.0 - squashed))
        dp[0:Q, at] = d_pre
        sums = [
            jnp.sum(d_pre * xf[5 + tap : 5 + tap + Q, at], axis=0, keepdims=True)
            for tap in range(CONV)
        ]
        sums.append(jnp.sum(dyf * actf, axis=0, keepdims=True))
        for place, total in enumerate(sums):
            gconv_ref[place : place + 1, at] += total
        d_in = cw_ref[CONV - 1 : CONV, at] * d_pre
        for tap in range(CONV - 1):
            d_in = d_in + cw_ref[tap : tap + 1, at] * dp[CONV - 1 - tap : CONV - 1 - tap + Q, at]
        dci_ref[:, at] = d_in.astype(bf16)
        kept = back[:, at] * jnp.where(left, e_end[:, h0 : h0 + 1], e_end[:, h1 : h1 + 1])
        cross[0:1, at] = jnp.sum(kept * s_ref[0, :, at].astype(f32), axis=0, keepdims=True)
        back[:, at] = kept + dot_nn(reads_t, decayed)
    dcb_t = dcb[...]
    d_keys = dot_nn(dcb_t.astype(bf16), reads) + dot_nt(wx[...], back16[...])
    d_reads = dot_nn(dcb_t.T.astype(bf16), keys) + dot_nt(edy[...], s_ref[0])
    give_back(me_ref[0], d_keys, d_reads, dbc_ref)
    unit = lax.broadcasted_iota(jnp.int32, (OWN, LANES), 0)
    head = lax.broadcasted_iota(jnp.int32, (OWN, LANES), 1)
    member = jnp.where(unit // HEAD_DIM == head, 1.0, 0.0)
    member16 = member.astype(bf16)
    s_12 = dot_nn(p12h[...], member16) + dot_nn(p12l[...], member16)
    s_3 = dot_nn(p3[...], member16)
    s_23 = dot_nn(p23[...], member16)
    through = dot_exact(cross[...], member)[0:1, :]
    row = lax.broadcasted_iota(jnp.int32, (Q, Q), 0)
    column = lax.broadcasted_iota(jnp.int32, (Q, Q), 1)
    suffix = jnp.where(column >= row, 1.0, 0.0)
    prefix = jnp.where(column < row, 1.0, 0.0)
    d_log = dot_exact(suffix, s_12) + dot_exact(prefix, s_3) + through
    slope = sigmoid(v)
    ratio = jnp.where(steps > 0.0, slope / steps, 0.0)
    rate = rows_ref[1:2, :]
    d_sum = s_23 * ratio + rate * d_log * slope
    ddt_ref[...] = d_sum * rows_ref[2:3, :]
    grow_ref[0:1, :] += jnp.sum(d_sum, axis=0, keepdims=True)
    grow_ref[1:2, :] += jnp.sum(d_log * rate * steps, axis=0, keepdims=True)


def recurrence_backward(me, conv_in, act, dy, y, bc, dt_tile, entry, taps, rows, skip_row):
    length = conv_in.shape[0]
    blocks = length // Q
    whole = lambda i, me: (0, 0)
    along = lambda i, me: (blocks - 1 - i, 0)
    previous = lambda i, me: (jnp.maximum((blocks - 1 - i) * (Q // 16) - 1, 0), 0)
    return pl.pallas_call(
        backward_kernel,
        grid_spec=pltpu.PrefetchScalarGridSpec(
            num_scalar_prefetch=1,
            grid=(blocks,),
            in_specs=[
                pl.BlockSpec((Q, OWN), along),
                pl.BlockSpec((16, OWN), previous),
                pl.BlockSpec((Q, OWN), along),
                pl.BlockSpec((Q, OWN), along),
                pl.BlockSpec((Q, OWN), along),
            ]
            + [pl.BlockSpec((HALF, LANES), along)] * PART
            + [
                pl.BlockSpec((Q, LANES), along),
                pl.BlockSpec((1, STATE, OWN), lambda i, me: (blocks - 1 - i, 0, 0)),
                pl.BlockSpec((8, OWN), whole),
                pl.BlockSpec((8, LANES), whole),
                pl.BlockSpec((8, OWN), whole),
            ],
            out_specs=[
                pl.BlockSpec((Q, OWN), along),
                pl.BlockSpec((PART, HALF, LANES), lambda i, me: (0, blocks - 1 - i, 0)),
                pl.BlockSpec((Q, LANES), along),
                pl.BlockSpec((8, OWN), whole),
                pl.BlockSpec((8, LANES), whole),
            ],
            scratch_shapes=[
                pltpu.VMEM((STATE, OWN), f32),
                pltpu.VMEM((STATE, OWN), bf16),
                pltpu.VMEM((Q + 8, OWN), f32),
                pltpu.VMEM((Q + 8, OWN), f32),
                pltpu.VMEM((Q, OWN), bf16),
                pltpu.VMEM((Q, OWN), bf16),
                pltpu.VMEM((Q, Q), f32),
                pltpu.VMEM((Q, OWN), bf16),
                pltpu.VMEM((Q, OWN), bf16),
                pltpu.VMEM((Q, OWN), bf16),
                pltpu.VMEM((Q, OWN), bf16),
                pltpu.VMEM((8, OWN), f32),
            ],
        ),
        out_shape=[
            jax.ShapeDtypeStruct((length, CONV_COLS), bf16),
            jax.ShapeDtypeStruct((PART, length // 2, LANES), bf16),
            jax.ShapeDtypeStruct((length, LANES), f32),
            jax.ShapeDtypeStruct((8, OWN), f32),
            jax.ShapeDtypeStruct((8, LANES), f32),
        ],
        compiler_params=pltpu.CompilerParams(
            dimension_semantics=("arbitrary",), vmem_limit_bytes=48 * 2**20
        ),
        cost_estimate=pl.CostEstimate(
            flops=70 * 10**9, bytes_accessed=2**24, transcendentals=10**7
        ),
        name="recurrence_backward",
    )(me, conv_in, conv_in, act, dy, y, *bc, dt_tile, entry, taps, rows, skip_row)


def gate_forward_kernel(n_ref, t_ref, y_ref, wg_ref, wo_ref, row_ref, z_ref, d_ref, sums_ref):
    z = dot_nn(n_ref[...], wg_ref[...]) * row_ref[1:2, :]
    d = dot_nt(t_ref[...], wo_ref[...])
    z_ref[...] = z
    d_ref[...] = d
    gated = y_ref[...] * (z * sigmoid(z))
    squares = jnp.sum(gated * gated, axis=1, keepdims=True)
    cross = jnp.sum(d * row_ref[0:1, :] * gated, axis=1, keepdims=True)
    lane = lax.broadcasted_iota(jnp.int32, (1, LANES), 1)
    both = jnp.where(lane == 0, squares, jnp.where(lane == 1, cross, 0.0))
    sums_ref[...] = both.T[0:8, :]


def gate_forward(normed, cot, y, w_gate, w_o, row):
    length = normed.shape[0]
    whole = lambda i: (0, 0)
    along = lambda i: (i, 0)
    return pl.pallas_call(
        gate_forward_kernel,
        grid=(length // Q,),
        in_specs=[
            pl.BlockSpec((Q, D), along),
            pl.BlockSpec((Q, D), along),
            pl.BlockSpec((Q, OWN), along),
            pl.BlockSpec((D, OWN), whole),
            pl.BlockSpec((OWN, D), whole),
            pl.BlockSpec((8, OWN), whole),
        ],
        out_specs=[
            pl.BlockSpec((Q, OWN), along),
            pl.BlockSpec((Q, OWN), along),
            pl.BlockSpec((8, Q), lambda i: (0, i)),
        ],
        out_shape=[
            jax.ShapeDtypeStruct((length, OWN), f32),
            jax.ShapeDtypeStruct((length, OWN), f32),
            jax.ShapeDtypeStruct((8, length), f32),
        ],
        compiler_params=pltpu.CompilerParams(vmem_limit_bytes=48 * 2**20),
        cost_estimate=pl.CostEstimate(
            flops=4 * length * D * OWN, bytes_accessed=2**25, transcendentals=length * OWN
        ),
        name="gate_forward",
    )(normed, cot, y, w_gate, w_o, row)


def gate_backward_kernel(y_ref, z_ref, d_ref, sums_ref, row_ref, out_ref, dy_ref, dz_ref, gain_ref):
    @pl.when(pl.program_id(0) == 0)
    def _():
        gain_ref[...] = jnp.zeros_like(gain_ref)

    units = row_ref[2:3, 0:1]
    sums = sums_ref[...]
    inverse = lax.rsqrt(sums[0:1, :] / units + epsilon)
    pull = inverse * inverse * inverse * sums[1:2, :] / units
    row = lax.broadcasted_iota(jnp.int32, (LANES, 1), 0)
    columns = jnp.where(row == 0, inverse, jnp.where(row == 1, pull, 0.0)).T
    inverse, pull = columns[:, 0:1], columns[:, 1:2]
    for strip in range(STRIPS):
        at = slice(strip * LANES, (strip + 1) * LANES)
        y, z, d = y_ref[:, at], z_ref[:, at], d_ref[:, at]
        gain = row_ref[0:1, at]
        squashed = sigmoid(z)
        act = z * squashed
        gated = y * act
        normalized = gated * inverse
        out_ref[:, at] = (normalized * gain).astype(bf16)
        gain_ref[0:1, at] += jnp.sum(d * normalized, axis=0, keepdims=True)
        d_gated = inverse * (d * gain) - gated * pull
        dy_ref[:, at] = (d_gated * act).astype(bf16)
        dz_ref[:, at] = (d_gated * y * squashed * (1.0 + z * (1.0 - squashed))).astype(bf16)


def gate_backward(y, z, d, sums, row):
    length = y.shape[0]
    whole = lambda i: (0, 0)
    along = lambda i: (i, 0)
    return pl.pallas_call(
        gate_backward_kernel,
        grid=(length // Q,),
        in_specs=[pl.BlockSpec((Q, OWN), along)] * 3
        + [pl.BlockSpec((8, Q), lambda i: (0, i)), pl.BlockSpec((8, OWN), whole)],
        out_specs=[pl.BlockSpec((Q, OWN), along)] * 3 + [pl.BlockSpec((8, OWN), whole)],
        out_shape=[jax.ShapeDtypeStruct((length, OWN), bf16)] * 3
        + [jax.ShapeDtypeStruct((8, OWN), f32)],
        compiler_params=pltpu.CompilerParams(vmem_limit_bytes=32 * 2**20),
        cost_estimate=pl.CostEstimate(
            flops=30 * length * OWN, bytes_accessed=18 * length * OWN, transcendentals=length * OWN
        ),
        name="gate_backward",
    )(y, z, d, sums, row)


def input_gradient_kernel(z_ref, p_ref, wg_ref, wc_ref, out_ref):
    out_ref[...] = (dot_nt(z_ref[...], wg_ref[...]) + dot_nt(p_ref[...], wc_ref[...])).astype(bf16)


def input_gradient(d_z, d_project, w_gate, w_conv):
    length = d_z.shape[0]
    whole = lambda i: (0, 0)
    along = lambda i: (i, 0)
    return pl.pallas_call(
        input_gradient_kernel,
        grid=(length // Q,),
        in_specs=[
            pl.BlockSpec((Q, OWN), along),
            pl.BlockSpec((Q, CONV_COLS), along),
            pl.BlockSpec((D, OWN), whole),
            pl.BlockSpec((D, CONV_COLS), whole),
        ],
        out_specs=pl.BlockSpec((Q, D), along),
        out_shape=jax.ShapeDtypeStruct((length, D), bf16),
        compiler_params=pltpu.CompilerParams(vmem_limit_bytes=48 * 2**20),
        cost_estimate=pl.CostEstimate(
            flops=200 * 10**9, bytes_accessed=2**25, transcendentals=0
        ),
        name="input_gradient",
    )(d_z, d_project, w_gate, w_conv)


def per_device(
    hidden_in,
    widths,
    norm_gain,
    w_in,
    w_dt,
    conv_weight,
    dt_bias,
    a_log,
    skip_gain,
    gate_gain,
    w_out,
    grad_out,
):
    me = lax.axis_index("seq")
    tokens = hidden_in.shape[1]
    length = tokens * PART
    rows_in = w_in.shape[0]
    used_units = INNER // 8 * jnp.left_shift(jnp.int32(1), widths[0])
    units_float = used_units.astype(f32)
    block = jnp.arange(OWN) // LANES * PART + me
    unit_used = block * LANES < used_units
    head_used = ((jnp.arange(OWN_HEADS) // 2 * PART + me) * LANES < used_units).astype(f32)

    every = lambda a: jnp.broadcast_to(a[None], (PART,) + a.shape)
    tail = jnp.concatenate(
        [
            heads_by_owner(w_dt),
            every(norm_gain[:, None]),
            every(gate_gain.reshape(2, rows_in).T),
            jnp.zeros((PART, rows_in, LANES - OWN_HEADS - 3 - OWN_BC), bf16),
            w_in[:, 2 * INNER :].reshape(rows_in, PART, OWN_BC).transpose(1, 0, 2),
        ],
        axis=2,
    )
    conv_pieces = jnp.concatenate([by_owner(w_in[:, INNER : 2 * INNER]), tail], axis=2)
    gate_pieces = by_owner(w_in[:, :INNER])
    gather = gather_everything if fast_mesh() else gather_plainly
    w_conv, w_gate, w_o, x_pieces = gather(conv_pieces, gate_pieces, w_out, hidden_in[0])
    order = jnp.stack([me, me ^ 1, me ^ 2, me ^ 3]).astype(jnp.int32)
    gate_all = w_conv[:, OWN + OWN_HEADS + 1 : OWN + OWN_HEADS + 3]
    gate_all = gate_all.reshape(D // rows_in, rows_in, 2).transpose(0, 2, 1)
    gate_row = lax.dynamic_index_in_dim(gate_all.reshape(STRIPS, PART, LANES), me, 1, False)
    gate_row = gate_row.reshape(1, OWN).astype(f32)
    gain_row = w_conv[:, OWN + OWN_HEADS].astype(f32)[None, :]

    def own_heads(array):
        return lax.dynamic_index_in_dim(array.reshape(STRIPS, PART, 2), me, 1, False).reshape(-1)

    bias = own_heads(dt_bias)
    rate = -jnp.exp(own_heads(a_log))
    skip = own_heads(skip_gain)
    pad_heads = lambda a: jnp.pad(a, (0, LANES - OWN_HEADS))
    rows = jnp.stack(
        [pad_heads(bias), pad_heads(rate), pad_heads(head_used)] + [jnp.zeros((LANES,), f32)] * 5
    )
    skip_row = jnp.broadcast_to(jnp.repeat(skip, HEAD_DIM)[None, :], (8, OWN))
    taps = lax.dynamic_index_in_dim(
        conv_weight[:, :INNER].reshape(CONV, STRIPS, PART, LANES), me, 2, False
    ).reshape(CONV, OWN)
    taps = jnp.pad(taps.astype(f32), ((0, 8 - CONV), (0, 0)))
    taps_bc = lax.dynamic_slice_in_dim(conv_weight[:, INNER:], me * OWN_BC, OWN_BC, 1).astype(f32)
    taps_tile = jnp.pad(taps_bc, ((0, 8 - CONV), (LANES - OWN_BC, 0)))
    place_me = me.astype(jnp.int32).reshape(1)

    normed = all_positions(x_pieces, order, jnp.broadcast_to(gain_row, (8, D)))
    dt_tile = dot_nn(normed, w_conv[:, OWN:])
    bc = seq_pieces(bc_forward(dt_tile, taps_tile))
    cot_across = xor_seq(tie(grad_out[0], bc[2])[0], 2)
    conv_in = jnp.where(unit_used, dot_nn(normed, w_conv[:, :OWN]), 0.0).astype(bf16)
    if fast_mesh():
        w_o[1], conv_in = tie(w_o[1], conv_in)
        w_o.append(dp_swap_x(w_o[1]))
    y, act, entry = recurrence_forward(place_me, conv_in, bc, dt_tile, taps, rows, skip_row)
    if fast_mesh():
        cot_across, *w_o[2:] = after([cot_across, *w_o[2:]], [entry])
        w_o += [dp_swap_x(w_o[2]), dp_swap_x(w_o[3])]
        w_o = assemble(w_o, out_places(), 512)
    cot_pieces = (grad_out[0], xor_seq(grad_out[0], 1), cot_across, xor_seq(cot_across, 1))
    cot_all = all_positions(cot_pieces, order)
    row = jnp.concatenate(
        [
            gate_row,
            unit_used.astype(f32)[None, :],
            jnp.full((6, OWN), units_float),
        ],
        axis=0,
    )
    z, d_rounded, sums = gate_forward(normed, cot_all, y, w_gate, w_o, row)
    rounded_out, d_y, d_z, grad_gate_rows = gate_backward(y, z, d_rounded, seq_total(sums), row)
    grad_gate_local = grad_gate_rows[0]

    out_product = dot_tn(rounded_out, cot_all).astype(bf16)
    gate_product = dot_tn(normed, d_z).astype(bf16)
    d_y, out_product, gate_product = tie(d_y, out_product, gate_product)
    if fast_mesh():
        out_mine, out_got = x_halves(out_product.reshape(8, LANES, D))
        gate_total = dp_sum(gate_product)

    d_values, d_bc, d_dt, g_conv, g_rows = recurrence_backward(
        place_me, conv_in, act, d_y, y, bc, dt_tile, entry, taps, rows, skip_row
    )
    if fast_mesh():
        d_values, d_bc, out_got, rounded_out = tie(d_values, d_bc, out_got, rounded_out)
    branch = dot_nn(rounded_out, w_o).astype(bf16).reshape(PART, tokens, D)
    branch_mine, branch_got = core_halves(branch)
    d_project, g_tail = tail_backward(
        dt_tile, seq_scatter_relative(d_bc), d_dt, taps_tile, d_values
    )
    g_skip = jnp.sum(g_conv[4].reshape(OWN_HEADS, HEAD_DIM), axis=1)
    small = jnp.concatenate(
        [
            g_conv[:CONV].reshape(-1),
            g_tail[:CONV, LANES - OWN_BC :].reshape(-1),
            pad_heads(g_rows[0, :OWN_HEADS]),
            pad_heads(g_rows[1, :OWN_HEADS]),
            pad_heads(g_skip),
            grad_gate_local,
        ]
    )
    count = small.shape[0]
    padded = -(-count // (8 * LANES)) * 8 * LANES
    small = jnp.pad(small, (0, padded - count)).reshape(-1, LANES)
    if fast_mesh():
        conv_product = dot_tn(normed, d_project).astype(bf16)
        d_project, conv_product, out_got = tie(d_project, conv_product, out_got)
        conv_total = dp_sum(conv_product)
        out_keep, out_gives = z_gives(out_mine, out_got)
        out_parts = [dp_shift_z(give, steps + 1) for steps, give in enumerate(out_gives)]
    branch_keep, branch_give = halves_sum(branch_mine, branch_got)
    branch_across = xor_seq(branch_give, 2)
    d_normed = input_gradient(d_z, d_project, w_gate, w_conv)
    if fast_mesh():
        *out_parts, branch_across, d_normed = tie(*out_parts, branch_across, d_normed)
        grad_w_out = out_keep + sum(part.astype(f32) for part in out_parts)
    else:
        grad_w_out = scatter_out(out_product)
    mine, got = core_halves(d_normed.reshape(PART, tokens, D))
    keep, give = halves_sum(mine, got)
    small, give = tie(small, give)
    across = xor_seq(give, 2)
    d_own = keep + across.astype(f32)
    if fast_mesh():
        (conv_total,) = after([conv_total], [across])
        grad_gate_in = owners_rows(gate_total)
        grad_conv_in = owners_rows(conv_total)
    else:
        grad_gate_in = scatter_in(gate_product)
        grad_conv_in = scatter_in(dot_tn(normed, d_project).astype(bf16))
    x_own = hidden_in[0].astype(f32)
    hidden_out = (x_own + branch_keep + branch_across.astype(f32)).astype(bf16)[None]
    own_rms = lax.rsqrt(jnp.mean(x_own * x_own, axis=1, keepdims=True) + epsilon)
    d_scaled = d_own * gain_row
    d_input = own_rms * d_scaled - x_own * own_rms**3 * jnp.mean(
        d_scaled * x_own, axis=1, keepdims=True
    )
    grad_in = (grad_out[0].astype(f32) + d_input).astype(bf16)[None]

    every = jnp.stack(by_partner(seq_pieces(dp_total(small)))).reshape(PART, padded)
    start = 0

    def take(size):
        nonlocal start
        start += size
        return every[:, start - size : start]

    all_conv = take(CONV * OWN).reshape(PART, CONV, OWN)
    all_conv_bc = take(CONV * OWN_BC).reshape(PART, CONV, OWN_BC)
    head_sums = [heads_from_owner(take(LANES)[:, None, :OWN_HEADS]).reshape(HEADS) for _ in range(3)]
    grad_gate = lax.dynamic_index_in_dim(take(OWN), me, 0, False)
    grad_conv = jnp.concatenate(
        [from_owner(all_conv), all_conv_bc.transpose(1, 0, 2).reshape(CONV, 2 * STATE)], axis=1
    )
    place = lax.axis_index(("dp", "seq"))
    gate_rows = gate_gain.shape[0]
    if gate_rows == LANES:
        grad_gate_gain = lax.dynamic_slice_in_dim(
            grad_gate, lax.axis_index("dp") * gate_rows, gate_rows, 0
        )
    else:
        start = CONV * OWN + CONV * OWN_BC + 3 * LANES
        whole_gate = from_owner(take(OWN)[:, None, :]).reshape(INNER)
        grad_gate_gain = lax.dynamic_slice_in_dim(whole_gate, place * gate_rows, gate_rows, 0)

    grad_w_in = jnp.concatenate(
        [
            from_owner(grad_gate_in),
            from_owner(grad_conv_in[:, :, :OWN]),
            grad_conv_in[:, :, CONV_COLS - OWN_BC :].transpose(1, 0, 2).reshape(rows_in, 2 * STATE),
        ],
        axis=1,
    )
    grad_w_dt = heads_from_owner(grad_conv_in[:, :, OWN : OWN + OWN_HEADS])
    grad_norm_gain = (
        jnp.sum(w_in.astype(f32) * grad_w_in, axis=1)
        + jnp.sum(w_dt.astype(f32) * grad_w_dt, axis=1)
    ) / norm_gain.astype(f32)
    return (
        hidden_out,
        grad_in,
        grad_norm_gain,
        grad_w_in,
        grad_w_dt,
        grad_conv,
        head_sums[0],
        head_sums[1],
        head_sums[2],
        grad_gate_gain,
        grad_w_out,
    )


def solution(mesh):
    return jax.shard_map(
        per_device,
        mesh=mesh,
        in_specs=(
            P("dp", "seq", None),
            P("dp"),
            P(("dp", "seq")),
            P(("dp", "seq"), None),
            P(("dp", "seq"), None),
            P(),
            P(),
            P(),
            P(),
            P(("dp", "seq")),
            P(("dp", "seq"), None),
            P("dp", "seq", None),
        ),
        out_specs=(
            P("dp", "seq", None),
            P("dp", "seq", None),
            P(("dp", "seq")),
            P(("dp", "seq"), None),
            P(("dp", "seq"), None),
            P(),
            P(),
            P(),
            P(),
            P(("dp", "seq")),
            P(("dp", "seq"), None),
        ),
        check_vma=False,
    )
```

```python
import functools

import jax
import jax.numpy as jnp
from jax import lax
from jax.experimental import pallas as pl
from jax.experimental.pallas import tpu as pltpu
from jax.sharding import PartitionSpec as P

D = 2048
INNER = 4096
HEAD_DIM = 64
STATE = 128
CONV = 4
HEADS = 64
CHANNELS = 4352

PART = 4
LANES = 128
STRIPS = INNER // LANES // PART
OWN = STRIPS * LANES
OWN_HEADS = OWN // HEAD_DIM
OWN_BC = 2 * STATE // PART
CONV_COLS = OWN + LANES
Q = 256
HALF = Q // 2

epsilon = 1e-05
highest = lax.Precision.HIGHEST
f32 = jnp.float32
bf16 = jnp.bfloat16
LOG2E = 1.4426950408889634


def swap(value, axis, pairs):
    return lax.ppermute(value, axis, pairs)


def xor_seq(value, bits):
    return lax.ppermute(value, "seq", [(s, s ^ bits) for s in range(PART)])


def core_halves(blocks):
    core = lax.axis_index("seq") % 2
    view = blocks.reshape((2, 2) + blocks.shape[1:])
    mine = lax.dynamic_index_in_dim(view, core, 1, False)
    other = lax.dynamic_index_in_dim(view, 1 - core, 1, False)
    return mine, xor_seq(other, 1)


def halves_sum(mine, received):
    row = lax.axis_index("seq") // 2

    def of(which):
        a = lax.dynamic_index_in_dim(mine, which, 0, False)
        return a.astype(f32) + lax.dynamic_index_in_dim(received, which, 0, False).astype(f32)

    return of(row), of(1 - row).astype(bf16)


def seq_scatter_relative(blocks):
    view = blocks.reshape((2, 2) + blocks.shape[1:])
    half = view[:, 0].astype(f32) + xor_seq(view[:, 1], 1).astype(f32)
    return half[0], xor_seq(half[1].astype(bf16), 2)


def by_partner(pieces):
    me = lax.axis_index("seq")
    odd, lower = me % 2 == 1, me >= 2
    a, b, c, d = pieces
    a, b = jnp.where(odd, b, a), jnp.where(odd, a, b)
    c, d = jnp.where(odd, d, c), jnp.where(odd, c, d)
    return (
        jnp.where(lower, c, a),
        jnp.where(lower, d, b),
        jnp.where(lower, a, c),
        jnp.where(lower, b, d),
    )


def seq_exchange(pieces):
    turned = by_partner([pieces[k] for k in range(PART)])
    return [turned[0]] + [xor_seq(turned[k], k) for k in range(1, PART)]


def seq_total(value):
    value = value + xor_seq(value, 1)
    return value + xor_seq(value, 2)


def fast_mesh():
    return lax.axis_size("dp") == 8


def dp_shift_z(value, steps):
    pairs = [(z * 2 + x, (z + steps) % 4 * 2 + x) for z in range(4) for x in range(2)]
    return lax.ppermute(value, "dp", pairs)


def dp_swap_x(value):
    return lax.ppermute(value, "dp", [(d, d ^ 1) for d in range(8)])


def tie_kernel(*refs):
    del refs


def tie(*values):
    anywhere = pl.BlockSpec(memory_space=pl.ANY)
    return pl.pallas_call(
        tie_kernel,
        in_specs=[anywhere] * len(values),
        out_specs=[anywhere] * len(values),
        out_shape=[jax.ShapeDtypeStruct(v.shape, v.dtype) for v in values],
        input_output_aliases={k: k for k in range(len(values))},
        name="tie",
    )(*values)


def after(values, needed):
    anywhere = pl.BlockSpec(memory_space=pl.ANY)
    return pl.pallas_call(
        tie_kernel,
        in_specs=[anywhere] * (len(values) + len(needed)),
        out_specs=[anywhere] * len(values),
        out_shape=[jax.ShapeDtypeStruct(v.shape, v.dtype) for v in values],
        input_output_aliases={k: k for k in range(len(values))},
        name="after",
    )(*values, *needed)


def assemble_kernel(places_ref, *refs):
    rows = refs[0].shape[0]
    for k, piece in enumerate(refs[:-1]):
        refs[-1][pl.ds(pl.multiple_of(places_ref[k] * rows, rows), rows), :] = piece[...]


def assemble(pieces, places, tile):
    rows, columns = pieces[0].shape
    count = len(pieces)
    along = lambda i, places: (0, i)
    return pl.pallas_call(
        assemble_kernel,
        grid_spec=pltpu.PrefetchScalarGridSpec(
            num_scalar_prefetch=1,
            grid=(columns // tile,),
            in_specs=[pl.BlockSpec((rows, tile), along)] * count,
            out_specs=pl.BlockSpec((rows * count, tile), along),
        ),
        out_shape=jax.ShapeDtypeStruct((rows * count, columns), pieces[0].dtype),
        compiler_params=pltpu.CompilerParams(vmem_limit_bytes=24 * 2**20),
        cost_estimate=pl.CostEstimate(
            flops=0, bytes_accessed=4 * rows * count * columns, transcendentals=0
        ),
        name="assemble",
    )(places, *pieces)


def pieces_kernel(w_ref, dt_ref, norm_ref, gate_ref, conv_ref, gates_ref):
    rows = w_ref.shape[0]
    lane = lax.broadcasted_iota(jnp.int32, (1, LANES), 1)
    square = lax.broadcasted_iota(jnp.int32, (rows, rows), 0) == lax.broadcasted_iota(
        jnp.int32, (rows, rows), 1
    )

    def column(values):
        return jnp.sum(jnp.where(square, values, 0.0), axis=1, keepdims=True)

    gain = column(norm_ref[0:1, :].astype(f32))
    gates = [column(gate_ref[k : k + 1, :].astype(f32)) for k in range(2)]
    head = lax.broadcasted_iota(jnp.int32, (HEADS, LANES), 0)
    slot = lax.broadcasted_iota(jnp.int32, (HEADS, LANES), 1)
    for owner in range(PART):
        for strip in range(STRIPS):
            source = (strip * PART + owner) * LANES
            at = slice(strip * LANES, (strip + 1) * LANES)
            gates_ref[owner, :, at] = w_ref[:, source : source + LANES]
            conv_ref[owner, :, at] = w_ref[:, INNER + source : INNER + source + LANES]
        chosen = (slot < OWN_HEADS) & (head == slot // 2 * 2 * PART + 2 * owner + slot % 2)
        steps = dot_nn(dt_ref[...], jnp.where(chosen, 1.0, 0.0).astype(bf16))
        first = 2 * INNER + owner // 2 * LANES
        tile = w_ref[:, first : first + LANES].astype(f32)
        if owner % 2 == 0:
            tile = pltpu.roll(tile, OWN_BC, 1)
        tail = jnp.where(lane < OWN_HEADS, steps, jnp.where(lane == OWN_HEADS, gain, 0.0))
        for k in range(2):
            tail = jnp.where(lane == OWN_HEADS + 1 + k, gates[k], tail)
        tail = jnp.where(lane >= LANES - OWN_BC, tile, tail)
        conv_ref[owner, :, OWN:] = tail.astype(bf16)


def owners_pieces(w_in, w_dt, norm_gain, gate_gain):
    rows = w_in.shape[0]
    whole = lambda *block: pl.BlockSpec(block, lambda i: (0,) * len(block))

    return pl.pallas_call(
        pieces_kernel,
        grid=(1,),
        in_specs=[whole(rows, 2 * INNER + 2 * STATE), whole(rows, HEADS), whole(1, rows), whole(2, rows)],
        out_specs=[whole(PART, rows, CONV_COLS), whole(PART, rows, OWN)],
        out_shape=[
            jax.ShapeDtypeStruct((PART, rows, CONV_COLS), bf16),
            jax.ShapeDtypeStruct((PART, rows, OWN), bf16),
        ],
        compiler_params=pltpu.CompilerParams(vmem_limit_bytes=32 * 2**20),
        name="owners_pieces",
    )(w_in, w_dt, norm_gain[None, :], gate_gain.reshape(2, rows))


def seq_pass(pieces, *beside):
    me = lax.axis_index("seq")
    core, row = me % 2, me // 2
    view = pieces.reshape((2, 2) + pieces.shape[1:])
    give = lax.dynamic_index_in_dim(view, 1 - row, 0, False)
    keep = lax.dynamic_index_in_dim(view, row, 0, False)
    got, *beside = tie(xor_seq(give, 2), *beside)
    lower = jnp.where(row == 0, keep, got)
    upper = jnp.where(row == 0, got, keep)
    both = jnp.stack([lower, upper])
    mine = lax.dynamic_index_in_dim(both, core, 1, False)
    other = xor_seq(lax.dynamic_index_in_dim(both, 1 - core, 1, False), 1)
    first = jnp.where(core == 0, mine, other)
    second = jnp.where(core == 0, other, mine)
    return jnp.stack([first, second], axis=1).reshape((-1,) + pieces.shape[2:]), beside


def seq_pieces(block, after=None):
    source = block if after is None else tie(block, after)[0]
    across = xor_seq(source, 2)
    return block, xor_seq(block, 1), across, xor_seq(across, 1)


def gather_everything(conv_pieces, gate_pieces, o, x_block, cot_block):
    c, (o1,) = seq_pass(conv_pieces, dp_shift_z(o, 1))
    w_conv = lax.all_gather(c, "dp", axis=0, tiled=True)
    x_across, gate_pieces = tie(xor_seq(after([x_block], [c])[0], 2), gate_pieces)
    g, _ = seq_pass(gate_pieces)
    half = cot_block.shape[0] // 2
    cot_a, cot_b = after([cot_block[:half], cot_block[half:]], [g])
    cot_a = xor_seq(cot_a, 2)
    o2, o3, o_x, g, x_across = after(
        [dp_shift_z(o, 2), dp_shift_z(o, 3), dp_swap_x(o), g, x_across], [w_conv]
    )
    x_pieces = (x_block, xor_seq(x_block, 1), x_across, xor_seq(x_across, 1))
    w_gate = lax.all_gather(g, "dp", axis=0, tiled=True)
    return w_conv, w_gate, [o, o1, o2, o3, o_x], x_pieces, (cot_a, cot_b)


def out_places():
    dp = lax.axis_index("dp")
    sources = (dp // 2 - jnp.arange(4, dtype=jnp.int32) + 4) % 4 * 2
    return jnp.concatenate([sources + dp % 2, sources + 1 - dp % 2]).astype(jnp.int32)


def norm_rows(x, gain):
    x = x.astype(f32)
    inverse = lax.rsqrt(jnp.mean(x * x, axis=1, keepdims=True) + epsilon)
    return (x * inverse * gain).astype(bf16)


def positions_kernel(shares, with_norm, order_ref, *refs):
    step = pl.program_id(0)
    first = 0
    for k, share in enumerate(shares):

        @pl.when((step >= first) & (step < first + share))
        def _():
            if with_norm:
                refs[-1][...] = norm_rows(refs[k][...], refs[-2][0:1, :])
            else:
                refs[-1][...] = refs[k][...]

        first += share


def all_positions(pieces, order, gain_rows=None):
    tile = min(256, min(p.shape[0] for p in pieces))
    shares = [p.shape[0] // tile for p in pieces]
    steps = sum(shares)
    each = steps // PART

    def place(first, share):
        return lambda i, order: (jnp.clip(i - first, 0, share - 1), 0)

    specs, first = [], 0
    for share in shares:
        specs.append(pl.BlockSpec((tile, D), place(first, share)))
        first += share
    extra = []
    if gain_rows is not None:
        specs.append(pl.BlockSpec((8, D), lambda i, order: (0, 0)))
        extra.append(gain_rows)
    return pl.pallas_call(
        functools.partial(positions_kernel, shares, gain_rows is not None),
        grid_spec=pltpu.PrefetchScalarGridSpec(
            num_scalar_prefetch=1,
            grid=(steps,),
            in_specs=specs,
            out_specs=pl.BlockSpec((tile, D), lambda i, order: (order[i // each] * each + i % each, 0)),
        ),
        out_shape=jax.ShapeDtypeStruct((tile * steps, D), bf16),
        compiler_params=pltpu.CompilerParams(vmem_limit_bytes=32 * 2**20),
        cost_estimate=pl.CostEstimate(
            flops=4 * tile * steps * D, bytes_accessed=4 * tile * steps * D, transcendentals=0
        ),
        name="all_positions",
    )(order, *pieces, *extra)


def dp_total(value):
    if not fast_mesh():
        return lax.psum(value, "dp")
    value = value + dp_swap_x(value)
    return value + dp_shift_z(value, 1) + dp_shift_z(value, 2) + dp_shift_z(value, 3)


def by_owner(columns):
    rows = columns.shape[0]
    return (
        columns.reshape(rows, STRIPS, PART, LANES).transpose(2, 0, 1, 3).reshape(PART, rows, OWN)
    )


def from_owner(pieces):
    rows = pieces.shape[1]
    return (
        pieces.reshape(PART, rows, STRIPS, LANES).transpose(1, 2, 0, 3).reshape(rows, INNER)
    )


def heads_by_owner(columns):
    rows = columns.shape[0]
    return (
        columns.reshape(rows, STRIPS, PART, 2).transpose(2, 0, 1, 3).reshape(PART, rows, OWN_HEADS)
    )


def heads_from_owner(pieces):
    rows = pieces.shape[1]
    return (
        pieces.reshape(PART, rows, STRIPS, 2).transpose(1, 2, 0, 3).reshape(rows, HEADS)
    )


def gather_in(pieces):
    full = lax.all_gather(pieces, ("dp", "seq"), axis=1, tiled=True)
    return lax.dynamic_index_in_dim(full, lax.axis_index("seq"), 0, False)


def dp_sum(product):
    return lax.psum_scatter(product, "dp", scatter_dimension=0, tiled=True)


def owners_rows(total):
    return seq_exchange(total.reshape(PART, -1, total.shape[1]))


def scatter_in(grads):
    full = jnp.zeros((PART,) + grads.shape, grads.dtype)
    full = lax.dynamic_update_index_in_dim(full, grads, lax.axis_index("seq"), 0)
    return lax.psum_scatter(full, ("dp", "seq"), scatter_dimension=1, tiled=True).astype(f32)


def gather_out(rows):
    full = lax.all_gather(rows, ("dp", "seq"), axis=0, tiled=True)
    full = full.reshape(STRIPS, PART, LANES, -1)
    return lax.dynamic_index_in_dim(full, lax.axis_index("seq"), 1, False).reshape(OWN, -1)


def gather_plainly(conv_pieces, gate_pieces, out_rows, x_block, cot_block):
    return (
        gather_in(conv_pieces),
        gather_in(gate_pieces),
        gather_out(out_rows),
        seq_pieces(x_block),
        jnp.split(cot_block, 2),
    )


def scatter_out(grads):
    full = jnp.zeros((STRIPS, PART, LANES, grads.shape[1]), grads.dtype)
    full = lax.dynamic_update_index_in_dim(
        full, grads.reshape(STRIPS, LANES, -1), lax.axis_index("seq"), 1
    )
    full = full.reshape(INNER, -1)
    return lax.psum_scatter(full, ("dp", "seq"), scatter_dimension=0, tiled=True).astype(f32)


def dot_nn(a, b):
    return lax.dot_general(a, b, (((1,), (0,)), ((), ())), preferred_element_type=f32)


def dot_nt(a, b):
    return lax.dot_general(a, b, (((1,), (1,)), ((), ())), preferred_element_type=f32)


def dot_tn(a, b):
    return lax.dot_general(a, b, (((0,), (0,)), ((), ())), preferred_element_type=f32)


def dot_exact(a, b):
    return lax.dot_general(
        a, b, (((1,), (0,)), ((), ())), precision=highest, preferred_element_type=f32
    )


def sigmoid(v):
    return 0.5 + 0.5 * jnp.tanh(0.5 * v)


def bc_forward_kernel(tile_ref, taps_ref, out_ref, padded):
    length = tile_ref.shape[0]
    padded[0:8, :] = jnp.zeros((8, LANES), f32)
    padded[8 : 8 + length, :] = tile_ref[...].astype(bf16).astype(f32)
    left = lax.broadcasted_iota(jnp.int32, (1, LANES), 1) < OWN_BC
    for block in range(length // Q):
        start = block * Q
        pre = taps_ref[0:1, :] * padded[start + 5 : start + 5 + Q, :]
        for tap in range(1, CONV):
            pre = pre + taps_ref[tap : tap + 1, :] * padded[start + 5 + tap : start + 5 + tap + Q, :]
        act = pre * sigmoid(pre)
        packed = jnp.where(left, pltpu.roll(act[HALF:], OWN_BC, 1), act[:HALF])
        out_ref[block * HALF : (block + 1) * HALF, :] = packed.astype(bf16)


def bc_forward(dt_tile, taps_tile):
    length = dt_tile.shape[0]
    return pl.pallas_call(
        bc_forward_kernel,
        out_shape=jax.ShapeDtypeStruct((length // 2, LANES), bf16),
        scratch_shapes=[pltpu.VMEM((8 + length, LANES), f32)],
        compiler_params=pltpu.CompilerParams(vmem_limit_bytes=16 * 2**20),
        cost_estimate=pl.CostEstimate(
            flops=20 * length * LANES, bytes_accessed=5 * length * LANES, transcendentals=0
        ),
        name="bc_forward",
    )(dt_tile, taps_tile)


def tail_kernel(tile_ref, grad_ref, ddt_ref, taps_ref, into_ref, out_ref, sums_ref, padded, dp):
    del into_ref
    length = tile_ref.shape[0]
    padded[0:8, :] = jnp.zeros((8, LANES), f32)
    padded[8 : 8 + length, :] = tile_ref[...].astype(bf16).astype(f32)
    dp[length : length + 8, :] = jnp.zeros((8, LANES), f32)
    lane = lax.broadcasted_iota(jnp.int32, (1, LANES), 1)
    left = lane < OWN_BC
    sums_ref[...] = jnp.zeros_like(sums_ref)
    for block in reversed(range(length // Q)):
        start = block * Q
        taken = [padded[start + 5 + tap : start + 5 + tap + Q, :] for tap in range(CONV)]
        pre = taps_ref[0:1, :] * taken[0]
        for tap in range(1, CONV):
            pre = pre + taps_ref[tap : tap + 1, :] * taken[tap]
        packed = grad_ref[block * HALF : (block + 1) * HALF, :]
        grad = jnp.concatenate([packed, pltpu.roll(packed, OWN_BC, 1)], axis=0)
        squashed = sigmoid(pre)
        d_pre = jnp.where(left, 0.0, grad * squashed * (1.0 + pre * (1.0 - squashed)))
        dp[start : start + Q, :] = d_pre
        for tap in range(CONV):
            sums_ref[tap : tap + 1, :] += jnp.sum(d_pre * taken[tap], axis=0, keepdims=True)
        d_in = taps_ref[CONV - 1 : CONV, :] * d_pre
        for tap in range(CONV - 1):
            first = start + CONV - 1 - tap
            d_in = d_in + taps_ref[tap : tap + 1, :] * dp[first : first + Q, :]
        d_dt = jnp.where(lane < OWN_HEADS, ddt_ref[start : start + Q, :], 0.0)
        out_ref[start : start + Q, :] = jnp.where(left, d_dt, d_in).astype(bf16)


def tail_backward(dt_tile, grad, d_dt, taps_tile, into):
    length = dt_tile.shape[0]
    whole = lambda i: (0, 0)
    return pl.pallas_call(
        tail_kernel,
        grid=(1,),
        in_specs=[
            pl.BlockSpec((length, LANES), whole),
            pl.BlockSpec((length // 2, LANES), whole),
            pl.BlockSpec((length, LANES), whole),
            pl.BlockSpec((8, LANES), whole),
            pl.BlockSpec(memory_space=pl.ANY),
        ],
        out_specs=[
            pl.BlockSpec((length, LANES), lambda i: (0, STRIPS)),
            pl.BlockSpec((8, LANES), whole),
        ],
        out_shape=[
            jax.ShapeDtypeStruct(into.shape, bf16),
            jax.ShapeDtypeStruct((8, LANES), f32),
        ],
        input_output_aliases={4: 0},
        scratch_shapes=[pltpu.VMEM((8 + length, LANES), f32), pltpu.VMEM((8 + length, LANES), f32)],
        compiler_params=pltpu.CompilerParams(vmem_limit_bytes=60 * 2**20),
        cost_estimate=pl.CostEstimate(
            flops=40 * length * LANES, bytes_accessed=14 * length * LANES, transcendentals=0
        ),
        name="tail_backward",
    )(dt_tile, grad, d_dt, taps_tile, into)


def keys_and_reads(me, refs):
    odd, lower = me % 2 == 1, me >= 2
    p = [ref[...].astype(f32) for ref in refs]
    r0, r1 = jnp.where(odd, p[1], p[0]), jnp.where(odd, p[0], p[1])
    r2, r3 = jnp.where(odd, p[3], p[2]), jnp.where(odd, p[2], p[3])
    q = (
        jnp.where(lower, r2, r0),
        jnp.where(lower, r3, r1),
        jnp.where(lower, r0, r2),
        jnp.where(lower, r1, r3),
    )
    left = lax.broadcasted_iota(jnp.int32, (1, LANES), 1) < OWN_BC

    def join(a, b):
        top = jnp.where(left, pltpu.roll(a, OWN_BC, 1), b)
        bottom = jnp.where(left, a, pltpu.roll(b, OWN_BC, 1))
        return jnp.concatenate([top, bottom], axis=0).astype(bf16)

    return join(q[0], q[1]), join(q[2], q[3])


def give_back(me, d_keys, d_reads, out_ref):
    left = lax.broadcasted_iota(jnp.int32, (1, LANES), 1) < OWN_BC
    for pair, array in enumerate((d_keys, d_reads)):
        top, bottom = array[:HALF], array[HALF:]
        low = jnp.where(left, bottom, pltpu.roll(top, OWN_BC, 1))
        high = jnp.where(left, pltpu.roll(bottom, OWN_BC, 1), top)
        out_ref[jnp.bitwise_xor(me, 2 * pair)] = low.astype(bf16)
        out_ref[jnp.bitwise_xor(me, 2 * pair + 1)] = high.astype(bf16)


def decay_terms(dt_ref, rows_ref):
    v = dt_ref[...] * rows_ref[2:3, :] + rows_ref[0:1, :]
    steps = jnp.maximum(v, 0.0) + jnp.log1p(jnp.exp(-jnp.abs(v)))
    log2_decay = rows_ref[1:2, :] * LOG2E * steps
    row = lax.broadcasted_iota(jnp.int32, (Q, Q), 0)
    column = lax.broadcasted_iota(jnp.int32, (Q, Q), 1)
    lower = jnp.where(row >= column, 1.0, 0.0)
    running = dot_exact(lower, log2_decay)
    shifted = running - jnp.log(steps) * LOG2E
    end = running[Q - 1 : Q, :]
    return v, steps, running, shifted, end


def forward_kernel(
    me_ref, ci_ref, b0, b1, b2, b3, dt_ref, cw_ref, rows_ref, skip_ref, y_ref, act_ref, s_ref, state, xf
):
    @pl.when(pl.program_id(0) == 0)
    def _():
        state[...] = jnp.zeros_like(state)
        xf[0:8, :] = jnp.zeros((8, OWN), f32)

    @pl.when(pl.program_id(0) > 0)
    def _():
        xf[0:8, :] = xf[Q : Q + 8, :]

    xf[8 : Q + 8, :] = ci_ref[...].astype(f32)
    _, _, running, shifted, end = decay_terms(dt_ref, rows_ref)
    shifted_t = shifted.T
    e_run = jnp.exp2(running)
    w_end = jnp.exp2(end - shifted)
    e_end = jnp.exp2(end)
    keys, reads = keys_and_reads(me_ref[0], (b0, b1, b2, b3))
    keys_t = keys.T
    cb = dot_nt(reads, keys)
    causal = lax.broadcasted_iota(jnp.int32, (HALF, HALF), 0) >= lax.broadcasted_iota(
        jnp.int32, (HALF, HALF), 1
    )
    left = lax.broadcasted_iota(jnp.int32, (1, LANES), 1) < HEAD_DIM
    s_ref[0] = state[...].astype(bf16)
    for strip in range(STRIPS):
        at = slice(strip * LANES, (strip + 1) * LANES)
        h0, h1 = 2 * strip, 2 * strip + 1
        pre = cw_ref[0:1, at] * xf[5 : 5 + Q, at]
        for tap in range(1, CONV):
            pre = pre + cw_ref[tap : tap + 1, at] * xf[5 + tap : 5 + tap + Q, at]
        act = (pre * sigmoid(pre)).astype(bf16)
        act_ref[:, at] = act
        actf = act.astype(f32)
        inter = dot_nn(reads, s_ref[0, :, at]) * jnp.where(
            left, e_run[:, h0 : h0 + 1], e_run[:, h1 : h1 + 1]
        )
        inter = inter + skip_ref[0:1, at] * actf
        top, bottom = inter[:HALF], inter[HALF:]
        for h, side in ((h0, left), (h1, jnp.logical_not(left))):
            x_h = jnp.where(side, actf, 0.0).astype(bf16)
            m00 = jnp.where(
                causal,
                jnp.exp2(running[:HALF, h : h + 1] - shifted_t[h : h + 1, :HALF]) * cb[:HALF, :HALF],
                0.0,
            )
            m10 = jnp.exp2(running[HALF:, h : h + 1] - shifted_t[h : h + 1, :HALF]) * cb[HALF:, :HALF]
            m11 = jnp.where(
                causal,
                jnp.exp2(running[HALF:, h : h + 1] - shifted_t[h : h + 1, HALF:]) * cb[HALF:, HALF:],
                0.0,
            )
            top = top + dot_nn(m00.astype(bf16), x_h[:HALF])
            bottom = bottom + dot_nn(
                jnp.concatenate([m10.astype(bf16), m11.astype(bf16)], axis=1), x_h
            )
        y_ref[:HALF, at] = top
        y_ref[HALF:, at] = bottom
        weighted = (actf * jnp.where(left, w_end[:, h0 : h0 + 1], w_end[:, h1 : h1 + 1])).astype(bf16)
        state[:, at] = state[:, at] * jnp.where(
            left, e_end[:, h0 : h0 + 1], e_end[:, h1 : h1 + 1]
        ) + dot_nn(keys_t, weighted)


def recurrence_forward(me, conv_in, bc, dt_tile, taps, rows, skip_row):
    length = conv_in.shape[0]
    blocks = length // Q
    whole = lambda i, me: (0, 0)
    along = lambda i, me: (i, 0)
    return pl.pallas_call(
        forward_kernel,
        grid_spec=pltpu.PrefetchScalarGridSpec(
            num_scalar_prefetch=1,
            grid=(blocks,),
            in_specs=[pl.BlockSpec((Q, OWN), along)]
            + [pl.BlockSpec((HALF, LANES), along)] * PART
            + [
                pl.BlockSpec((Q, LANES), along),
                pl.BlockSpec((8, OWN), whole),
                pl.BlockSpec((8, LANES), whole),
                pl.BlockSpec((8, OWN), whole),
            ],
            out_specs=[
                pl.BlockSpec((Q, OWN), along),
                pl.BlockSpec((Q, OWN), along),
                pl.BlockSpec((1, STATE, OWN), lambda i, me: (i, 0, 0)),
            ],
            scratch_shapes=[pltpu.VMEM((STATE, OWN), f32), pltpu.VMEM((Q + 8, OWN), f32)],
        ),
        out_shape=[
            jax.ShapeDtypeStruct((length, OWN), f32),
            jax.ShapeDtypeStruct((length, OWN), bf16),
            jax.ShapeDtypeStruct((blocks, STATE, OWN), bf16),
        ],
        compiler_params=pltpu.CompilerParams(
            dimension_semantics=("arbitrary",), vmem_limit_bytes=60 * 2**20
        ),
        cost_estimate=pl.CostEstimate(
            flops=60 * 10**9, bytes_accessed=2**24, transcendentals=10**7
        ),
        name="recurrence_forward",
    )(me, conv_in, *bc, dt_tile, taps, rows, skip_row)


def backward_kernel(
    me_ref,
    ci_ref,
    prev_ref,
    act_ref,
    dy_ref,
    y_ref,
    b0,
    b1,
    b2,
    b3,
    dt_ref,
    s_ref,
    cw_ref,
    rows_ref,
    skip_ref,
    dci_ref,
    dbc_ref,
    ddt_ref,
    gconv_ref,
    grow_ref,
    back,
    back16,
    dp,
    xf,
    edy,
    wx,
    dcb,
    p12h,
    p12l,
    p3,
    p23,
    cross,
):
    step = pl.program_id(0)
    last = pl.num_programs(0) - 1

    @pl.when(step == 0)
    def _():
        back[...] = jnp.zeros_like(back)
        dp[Q : Q + 8, :] = jnp.zeros((8, OWN), f32)
        gconv_ref[...] = jnp.zeros_like(gconv_ref)
        grow_ref[...] = jnp.zeros_like(grow_ref)
        cross[...] = jnp.zeros_like(cross)

    @pl.when(step > 0)
    def _():
        dp[Q : Q + 8, :] = dp[0:8, :]

    before = prev_ref[8:16, :].astype(f32)
    xf[0:8, :] = jnp.where(step == last, 0.0, before)
    xf[8 : Q + 8, :] = ci_ref[...].astype(f32)
    v, steps, running, shifted, end = decay_terms(dt_ref, rows_ref)
    running_t = running.T
    e_run = jnp.exp2(running)
    w_end = jnp.exp2(end - shifted)
    e_end = jnp.exp2(end)
    keys, reads = keys_and_reads(me_ref[0], (b0, b1, b2, b3))
    reads_t = reads.T
    cbt = dot_nt(keys, reads)
    ahead = lax.broadcasted_iota(jnp.int32, (HALF, HALF), 0) <= lax.broadcasted_iota(
        jnp.int32, (HALF, HALF), 1
    )
    left = lax.broadcasted_iota(jnp.int32, (1, LANES), 1) < HEAD_DIM
    back16[...] = back[...].astype(bf16)
    dcb[...] = jnp.zeros_like(dcb)
    for strip in range(STRIPS):
        at = slice(strip * LANES, (strip + 1) * LANES)
        h0, h1 = 2 * strip, 2 * strip + 1
        act = act_ref[:, at]
        dy = dy_ref[:, at]
        actf = act.astype(f32)
        dyf = dy.astype(f32)
        skip = skip_ref[0:1, at]
        w_pair = jnp.where(left, w_end[:, h0 : h0 + 1], w_end[:, h1 : h1 + 1])
        e_pair = jnp.where(left, e_run[:, h0 : h0 + 1], e_run[:, h1 : h1 + 1])
        decayed = (dyf * e_pair).astype(bf16)
        edy[:, at] = decayed
        wx[:, at] = (actf * w_pair).astype(bf16)
        inter = dot_nn(keys, back16[:, at]) * w_pair
        top = jnp.zeros((HALF, LANES), f32)
        bottom = jnp.zeros((HALF, LANES), f32)
        for h, side in ((h0, left), (h1, jnp.logical_not(left))):
            x_h = jnp.where(side, actf, 0.0).astype(bf16)
            dy_h = jnp.where(side, dyf, 0.0).astype(bf16)
            g_top = dot_nt(x_h[:HALF], dy)
            g_bottom = dot_nt(x_h[HALF:], dy[HALF:])
            l00 = jnp.exp2(running_t[h : h + 1, :HALF] - shifted[:HALF, h : h + 1])
            l01 = jnp.exp2(running_t[h : h + 1, HALF:] - shifted[:HALF, h : h + 1])
            l11 = jnp.exp2(running_t[h : h + 1, HALF:] - shifted[HALF:, h : h + 1])
            m00 = jnp.where(ahead, l00 * cbt[:HALF, :HALF], 0.0).astype(bf16)
            m01 = (l01 * cbt[:HALF, HALF:]).astype(bf16)
            m11 = jnp.where(ahead, l11 * cbt[HALF:, HALF:], 0.0).astype(bf16)
            top = top + dot_nn(jnp.concatenate([m00, m01], axis=1), dy_h)
            bottom = bottom + dot_nn(m11, dy_h[HALF:])
            dcb[:HALF, :HALF] += jnp.where(ahead, l00 * g_top[:, :HALF], 0.0)
            dcb[:HALF, HALF:] += l01 * g_top[:, HALF:]
            dcb[HALF:, HALF:] += jnp.where(ahead, l11 * g_bottom, 0.0)
        intra = jnp.concatenate([top, bottom], axis=0)
        d_values = intra + inter
        p_12 = dyf * (y_ref[:, at] - skip * actf) - actf * intra
        p_12h = p_12.astype(bf16)
        p12h[:, at] = p_12h
        p12l[:, at] = (p_12 - p_12h.astype(f32)).astype(bf16)
        p3[:, at] = (actf * inter).astype(bf16)
        p23[:, at] = (actf * d_values).astype(bf16)
        d_act = d_values + skip * dyf
        pre = cw_ref[0:1, at] * xf[5 : 5 + Q, at]
        for tap in range(1, CONV):
            pre = pre + cw_ref[tap : tap + 1, at] * xf[5 + tap : 5 + tap + Q, at]
        squashed = sigmoid(pre)
        d_pre = d_act * squashed * (1.0 + pre * (1.0 - squashed))
        dp[0:Q, at] = d_pre
        sums = [
            jnp.sum(d_pre * xf[5 + tap : 5 + tap + Q, at], axis=0, keepdims=True)
            for tap in range(CONV)
        ]
        sums.append(jnp.sum(dyf * actf, axis=0, keepdims=True))
        for place, total in enumerate(sums):
            gconv_ref[place : place + 1, at] += total
        d_in = cw_ref[CONV - 1 : CONV, at] * d_pre
        for tap in range(CONV - 1):
            d_in = d_in + cw_ref[tap : tap + 1, at] * dp[CONV - 1 - tap : CONV - 1 - tap + Q, at]
        dci_ref[:, at] = d_in.astype(bf16)
        kept = back[:, at] * jnp.where(left, e_end[:, h0 : h0 + 1], e_end[:, h1 : h1 + 1])
        cross[0:1, at] = jnp.sum(kept * s_ref[0, :, at].astype(f32), axis=0, keepdims=True)
        back[:, at] = kept + dot_nn(reads_t, decayed)
    dcb_t = dcb[...]
    d_keys = dot_nn(dcb_t.astype(bf16), reads) + dot_nt(wx[...], back16[...])
    d_reads = dot_nn(dcb_t.T.astype(bf16), keys) + dot_nt(edy[...], s_ref[0])
    give_back(me_ref[0], d_keys, d_reads, dbc_ref)
    unit = lax.broadcasted_iota(jnp.int32, (OWN, LANES), 0)
    head = lax.broadcasted_iota(jnp.int32, (OWN, LANES), 1)
    member = jnp.where(unit // HEAD_DIM == head, 1.0, 0.0)
    member16 = member.astype(bf16)
    s_12 = dot_nn(p12h[...], member16) + dot_nn(p12l[...], member16)
    s_3 = dot_nn(p3[...], member16)
    s_23 = dot_nn(p23[...], member16)
    through = dot_exact(cross[...], member)[0:1, :]
    row = lax.broadcasted_iota(jnp.int32, (Q, Q), 0)
    column = lax.broadcasted_iota(jnp.int32, (Q, Q), 1)
    suffix = jnp.where(column >= row, 1.0, 0.0)
    prefix = jnp.where(column < row, 1.0, 0.0)
    d_log = dot_exact(suffix, s_12) + dot_exact(prefix, s_3) + through
    slope = sigmoid(v)
    ratio = jnp.where(steps > 0.0, slope / steps, 0.0)
    rate = rows_ref[1:2, :]
    d_sum = s_23 * ratio + rate * d_log * slope
    ddt_ref[...] = d_sum * rows_ref[2:3, :]
    grow_ref[0:1, :] += jnp.sum(d_sum, axis=0, keepdims=True)
    grow_ref[1:2, :] += jnp.sum(d_log * rate * steps, axis=0, keepdims=True)


def recurrence_backward(me, conv_in, act, dy, y, bc, dt_tile, entry, taps, rows, skip_row):
    length = conv_in.shape[0]
    blocks = length // Q
    whole = lambda i, me: (0, 0)
    along = lambda i, me: (blocks - 1 - i, 0)
    previous = lambda i, me: (jnp.maximum((blocks - 1 - i) * (Q // 16) - 1, 0), 0)
    return pl.pallas_call(
        backward_kernel,
        grid_spec=pltpu.PrefetchScalarGridSpec(
            num_scalar_prefetch=1,
            grid=(blocks,),
            in_specs=[
                pl.BlockSpec((Q, OWN), along),
                pl.BlockSpec((16, OWN), previous),
                pl.BlockSpec((Q, OWN), along),
                pl.BlockSpec((Q, OWN), along),
                pl.BlockSpec((Q, OWN), along),
            ]
            + [pl.BlockSpec((HALF, LANES), along)] * PART
            + [
                pl.BlockSpec((Q, LANES), along),
                pl.BlockSpec((1, STATE, OWN), lambda i, me: (blocks - 1 - i, 0, 0)),
                pl.BlockSpec((8, OWN), whole),
                pl.BlockSpec((8, LANES), whole),
                pl.BlockSpec((8, OWN), whole),
            ],
            out_specs=[
                pl.BlockSpec((Q, OWN), along),
                pl.BlockSpec((PART, HALF, LANES), lambda i, me: (0, blocks - 1 - i, 0)),
                pl.BlockSpec((Q, LANES), along),
                pl.BlockSpec((8, OWN), whole),
                pl.BlockSpec((8, LANES), whole),
            ],
            scratch_shapes=[
                pltpu.VMEM((STATE, OWN), f32),
                pltpu.VMEM((STATE, OWN), bf16),
                pltpu.VMEM((Q + 8, OWN), f32),
                pltpu.VMEM((Q + 8, OWN), f32),
                pltpu.VMEM((Q, OWN), bf16),
                pltpu.VMEM((Q, OWN), bf16),
                pltpu.VMEM((Q, Q), f32),
                pltpu.VMEM((Q, OWN), bf16),
                pltpu.VMEM((Q, OWN), bf16),
                pltpu.VMEM((Q, OWN), bf16),
                pltpu.VMEM((Q, OWN), bf16),
                pltpu.VMEM((8, OWN), f32),
            ],
        ),
        out_shape=[
            jax.ShapeDtypeStruct((length, CONV_COLS), bf16),
            jax.ShapeDtypeStruct((PART, length // 2, LANES), bf16),
            jax.ShapeDtypeStruct((length, LANES), f32),
            jax.ShapeDtypeStruct((8, OWN), f32),
            jax.ShapeDtypeStruct((8, LANES), f32),
        ],
        compiler_params=pltpu.CompilerParams(
            dimension_semantics=("arbitrary",), vmem_limit_bytes=60 * 2**20
        ),
        cost_estimate=pl.CostEstimate(
            flops=70 * 10**9, bytes_accessed=2**24, transcendentals=10**7
        ),
        name="recurrence_backward",
    )(me, conv_in, conv_in, act, dy, y, *bc, dt_tile, entry, taps, rows, skip_row)


def gate_forward_kernel(n_ref, t_ref, y_ref, wg_ref, wo_ref, row_ref, z_ref, d_ref, sums_ref):
    z = dot_nn(n_ref[...], wg_ref[...]) * row_ref[1:2, :]
    d = dot_nt(t_ref[...], wo_ref[...])
    z_ref[...] = z
    d_ref[...] = d
    gated = y_ref[...] * (z * sigmoid(z))
    squares = jnp.sum(gated * gated, axis=1, keepdims=True)
    cross = jnp.sum(d * row_ref[0:1, :] * gated, axis=1, keepdims=True)
    lane = lax.broadcasted_iota(jnp.int32, (1, LANES), 1)
    both = jnp.where(lane == 0, squares, jnp.where(lane == 1, cross, 0.0))
    sums_ref[...] = both.T[0:8, :]


def gate_forward(normed, cot, y, w_gate, w_o, row):
    length = normed.shape[0]
    whole = lambda i: (0, 0)
    along = lambda i: (i, 0)
    return pl.pallas_call(
        gate_forward_kernel,
        grid=(length // Q,),
        in_specs=[
            pl.BlockSpec((Q, D), along),
            pl.BlockSpec((Q, D), along),
            pl.BlockSpec((Q, OWN), along),
            pl.BlockSpec((D, OWN), whole),
            pl.BlockSpec((OWN, D), whole),
            pl.BlockSpec((8, OWN), whole),
        ],
        out_specs=[
            pl.BlockSpec((Q, OWN), along),
            pl.BlockSpec((Q, OWN), along),
            pl.BlockSpec((8, Q), lambda i: (0, i)),
        ],
        out_shape=[
            jax.ShapeDtypeStruct((length, OWN), f32),
            jax.ShapeDtypeStruct((length, OWN), f32),
            jax.ShapeDtypeStruct((8, length), f32),
        ],
        compiler_params=pltpu.CompilerParams(vmem_limit_bytes=48 * 2**20),
        cost_estimate=pl.CostEstimate(
            flops=4 * length * D * OWN, bytes_accessed=2**25, transcendentals=length * OWN
        ),
        name="gate_forward",
    )(normed, cot, y, w_gate, w_o, row)


def gate_backward_kernel(y_ref, z_ref, d_ref, sums_ref, row_ref, out_ref, dy_ref, dz_ref, gain_ref):
    @pl.when(pl.program_id(0) == 0)
    def _():
        gain_ref[...] = jnp.zeros_like(gain_ref)

    units = row_ref[2:3, 0:1]
    sums = sums_ref[...]
    inverse = lax.rsqrt(sums[0:1, :] / units + epsilon)
    pull = inverse * inverse * inverse * sums[1:2, :] / units
    row = lax.broadcasted_iota(jnp.int32, (LANES, 1), 0)
    columns = jnp.where(row == 0, inverse, jnp.where(row == 1, pull, 0.0)).T
    inverse, pull = columns[:, 0:1], columns[:, 1:2]
    for strip in range(STRIPS):
        at = slice(strip * LANES, (strip + 1) * LANES)
        y, z, d = y_ref[:, at], z_ref[:, at], d_ref[:, at]
        gain = row_ref[0:1, at]
        squashed = sigmoid(z)
        act = z * squashed
        gated = y * act
        normalized = gated * inverse
        out_ref[:, at] = (normalized * gain).astype(bf16)
        gain_ref[0:1, at] += jnp.sum(d * normalized, axis=0, keepdims=True)
        d_gated = inverse * (d * gain) - gated * pull
        dy_ref[:, at] = (d_gated * act).astype(bf16)
        dz_ref[:, at] = (d_gated * y * squashed * (1.0 + z * (1.0 - squashed))).astype(bf16)


def gate_backward(y, z, d, sums, row):
    length = y.shape[0]
    whole = lambda i: (0, 0)
    along = lambda i: (i, 0)
    return pl.pallas_call(
        gate_backward_kernel,
        grid=(length // Q,),
        in_specs=[pl.BlockSpec((Q, OWN), along)] * 3
        + [pl.BlockSpec((8, Q), lambda i: (0, i)), pl.BlockSpec((8, OWN), whole)],
        out_specs=[pl.BlockSpec((Q, OWN), along)] * 3 + [pl.BlockSpec((8, OWN), whole)],
        out_shape=[jax.ShapeDtypeStruct((length, OWN), bf16)] * 3
        + [jax.ShapeDtypeStruct((8, OWN), f32)],
        compiler_params=pltpu.CompilerParams(vmem_limit_bytes=32 * 2**20),
        cost_estimate=pl.CostEstimate(
            flops=30 * length * OWN, bytes_accessed=18 * length * OWN, transcendentals=length * OWN
        ),
        name="gate_backward",
    )(y, z, d, sums, row)


def input_gradient_kernel(z_ref, p_ref, wg_ref, wc_ref, out_ref):
    out_ref[...] = (dot_nt(z_ref[...], wg_ref[...]) + dot_nt(p_ref[...], wc_ref[...])).astype(bf16)


def input_gradient(d_z, d_project, w_gate, w_conv):
    length = d_z.shape[0]
    whole = lambda i: (0, 0)
    along = lambda i: (i, 0)
    return pl.pallas_call(
        input_gradient_kernel,
        grid=(length // Q,),
        in_specs=[
            pl.BlockSpec((Q, OWN), along),
            pl.BlockSpec((Q, CONV_COLS), along),
            pl.BlockSpec((D, OWN), whole),
            pl.BlockSpec((D, CONV_COLS), whole),
        ],
        out_specs=pl.BlockSpec((Q, D), along),
        out_shape=jax.ShapeDtypeStruct((length, D), bf16),
        compiler_params=pltpu.CompilerParams(vmem_limit_bytes=60 * 2**20),
        cost_estimate=pl.CostEstimate(
            flops=10**10, bytes_accessed=2**22, transcendentals=0
        ),
        name="input_gradient",
    )(d_z, d_project, w_gate, w_conv)


def products_kernel(n_ref, z_ref, r_ref, t_ref, out_ref):
    rows = n_ref.shape[1]
    half = r_ref.shape[1]
    out_ref[0, :rows, :] = dot_nn(n_ref[...].T, z_ref[...]).astype(bf16)
    product = dot_nn(r_ref[...].T, t_ref[...]).astype(bf16)
    out_ref[0, rows : rows + half, :] = product[:, :OWN]
    out_ref[0, rows + half :, :] = product[:, OWN:]


def products(normed, d_z, rounded_out, cot):
    length = normed.shape[0]
    count = STRIPS
    whole = lambda i: (0, 0)
    across = lambda i: (0, i)
    return pl.pallas_call(
        products_kernel,
        grid=(count,),
        in_specs=[
            pl.BlockSpec((length, D // count), across),
            pl.BlockSpec((length, OWN), whole),
            pl.BlockSpec((length, LANES), across),
            pl.BlockSpec((length, D), whole),
        ],
        out_specs=pl.BlockSpec((1, D // count + 2 * LANES, OWN), lambda i: (i, 0, 0)),
        out_shape=jax.ShapeDtypeStruct((count, D // count + 2 * LANES, OWN), bf16),
        compiler_params=pltpu.CompilerParams(vmem_limit_bytes=48 * 2**20),
        cost_estimate=pl.CostEstimate(
            flops=4 * length * D * OWN, bytes_accessed=2**25, transcendentals=0
        ),
        name="products",
    )(normed, d_z, rounded_out, cot)


def rows_kernel(me_ref, *refs):
    gates, convs = refs[:PART], refs[PART : 2 * PART]
    w_ref, wdt_ref, gain_ref, grad_ref, gdt_ref, gnorm_ref = refs[2 * PART :]
    me = me_ref[0]
    rows = w_ref.shape[0]
    for k in range(PART):
        owner = jnp.bitwise_xor(me, k)
        for strip in range(STRIPS):
            at = slice(strip * LANES, (strip + 1) * LANES)
            first = pl.multiple_of((strip * PART + owner) * LANES, LANES)
            grad_ref[:, pl.ds(first, LANES)] = gates[k][:, at].astype(f32)
            grad_ref[:, pl.ds(INNER + first, LANES)] = convs[k][:, at].astype(f32)
    odd, lower = me % 2 == 1, me >= 2
    p = [convs[k][:, OWN:].astype(f32) for k in range(PART)]
    r0, r1 = jnp.where(odd, p[1], p[0]), jnp.where(odd, p[0], p[1])
    r2, r3 = jnp.where(odd, p[3], p[2]), jnp.where(odd, p[2], p[3])
    tails = (
        jnp.where(lower, r2, r0),
        jnp.where(lower, r3, r1),
        jnp.where(lower, r0, r2),
        jnp.where(lower, r1, r3),
    )
    left = lax.broadcasted_iota(jnp.int32, (1, LANES), 1) < OWN_BC
    for pair in range(2):
        low, high = tails[2 * pair], tails[2 * pair + 1]
        first = 2 * INNER + pair * LANES
        grad_ref[:, first : first + LANES] = jnp.where(left, pltpu.roll(low, OWN_BC, 1), high)
    slot = lax.broadcasted_iota(jnp.int32, (LANES, HEADS), 0)
    head = lax.broadcasted_iota(jnp.int32, (LANES, HEADS), 1)
    d_dt = jnp.zeros((rows, HEADS), f32)
    for owner in range(PART):
        chosen = (slot < OWN_HEADS) & (head == slot // 2 * 2 * PART + 2 * owner + slot % 2)
        d_dt = d_dt + dot_nn(tails[owner].astype(bf16), jnp.where(chosen, 1.0, 0.0).astype(bf16))
    gdt_ref[...] = d_dt
    total = jnp.sum(wdt_ref[...].astype(f32) * d_dt, axis=1, keepdims=True)
    for strip in range(2 * STRIPS * PART + 2):
        at = slice(strip * LANES, (strip + 1) * LANES)
        total = total + jnp.sum(w_ref[:, at].astype(f32) * grad_ref[:, at], axis=1, keepdims=True)
    square = lax.broadcasted_iota(jnp.int32, (rows, rows), 0) == lax.broadcasted_iota(
        jnp.int32, (rows, rows), 1
    )
    flat = jnp.sum(jnp.where(square, total, 0.0), axis=0, keepdims=True)
    gnorm_ref[...] = flat / gain_ref[...].astype(f32)


def projection_rows(me, gates, convs, w_in, w_dt, norm_gain):
    rows = w_in.shape[0]
    whole = lambda *block: pl.BlockSpec(block, lambda i, me: (0,) * len(block))
    columns = w_in.shape[1]
    return pl.pallas_call(
        rows_kernel,
        grid_spec=pltpu.PrefetchScalarGridSpec(
            num_scalar_prefetch=1,
            grid=(1,),
            in_specs=[whole(rows, OWN)] * PART
            + [whole(rows, CONV_COLS)] * PART
            + [whole(rows, columns), whole(rows, HEADS), whole(1, rows)],
            out_specs=[whole(rows, columns), whole(rows, HEADS), whole(1, rows)],
        ),
        out_shape=[
            jax.ShapeDtypeStruct((rows, columns), f32),
            jax.ShapeDtypeStruct((rows, HEADS), f32),
            jax.ShapeDtypeStruct((1, rows), f32),
        ],
        compiler_params=pltpu.CompilerParams(vmem_limit_bytes=32 * 2**20),
        name="projection_rows",
    )(me, *gates, *convs, w_in, w_dt, norm_gain[None, :])


def per_device(
    hidden_in,
    widths,
    norm_gain,
    w_in,
    w_dt,
    conv_weight,
    dt_bias,
    a_log,
    skip_gain,
    gate_gain,
    w_out,
    grad_out,
):
    me = lax.axis_index("seq")
    tokens = hidden_in.shape[1]
    length = tokens * PART
    rows_in = w_in.shape[0]
    used_units = INNER // 8 * jnp.left_shift(jnp.int32(1), widths[0])
    units_float = used_units.astype(f32)
    block = jnp.arange(OWN) // LANES * PART + me
    unit_used = block * LANES < used_units
    head_used = ((jnp.arange(OWN_HEADS) // 2 * PART + me) * LANES < used_units).astype(f32)

    if fast_mesh():
        conv_pieces, gate_pieces = owners_pieces(w_in, w_dt, norm_gain, gate_gain)
    else:
        every = lambda a: jnp.broadcast_to(a[None], (PART,) + a.shape)
        tail = jnp.concatenate(
            [
                heads_by_owner(w_dt),
                every(norm_gain[:, None]),
                every(gate_gain.reshape(2, rows_in).T),
                jnp.zeros((PART, rows_in, LANES - OWN_HEADS - 3 - OWN_BC), bf16),
                w_in[:, 2 * INNER :].reshape(rows_in, PART, OWN_BC).transpose(1, 0, 2),
            ],
            axis=2,
        )
        conv_pieces = jnp.concatenate([by_owner(w_in[:, INNER : 2 * INNER]), tail], axis=2)
        gate_pieces = by_owner(w_in[:, :INNER])

    gather = gather_everything if fast_mesh() else gather_plainly
    w_conv, w_gate, w_o, x_pieces, (cot_a, cot_b) = gather(
        conv_pieces, gate_pieces, w_out, hidden_in[0], grad_out[0]
    )
    order = jnp.stack([me, me ^ 1, me ^ 2, me ^ 3]).astype(jnp.int32)
    gate_all = w_conv[:, OWN + OWN_HEADS + 1 : OWN + OWN_HEADS + 3]
    gate_all = gate_all.reshape(D // rows_in, rows_in, 2).transpose(0, 2, 1)
    gate_row = lax.dynamic_index_in_dim(gate_all.reshape(STRIPS, PART, LANES), me, 1, False)
    gate_row = gate_row.reshape(1, OWN).astype(f32)
    gain_row = w_conv[:, OWN + OWN_HEADS].astype(f32)[None, :]

    def own_heads(array):
        return lax.dynamic_index_in_dim(array.reshape(STRIPS, PART, 2), me, 1, False).reshape(-1)

    bias = own_heads(dt_bias)
    rate = -jnp.exp(own_heads(a_log))
    skip = own_heads(skip_gain)
    pad_heads = lambda a: jnp.pad(a, (0, LANES - OWN_HEADS))
    rows = jnp.stack(
        [pad_heads(bias), pad_heads(rate), pad_heads(head_used)] + [jnp.zeros((LANES,), f32)] * 5
    )
    skip_row = jnp.broadcast_to(jnp.repeat(skip, HEAD_DIM)[None, :], (8, OWN))
    taps = lax.dynamic_index_in_dim(
        conv_weight[:, :INNER].reshape(CONV, STRIPS, PART, LANES), me, 2, False
    ).reshape(CONV, OWN)
    taps = jnp.pad(taps.astype(f32), ((0, 8 - CONV), (0, 0)))
    taps_bc = lax.dynamic_slice_in_dim(conv_weight[:, INNER:], me * OWN_BC, OWN_BC, 1).astype(f32)
    taps_tile = jnp.pad(taps_bc, ((0, 8 - CONV), (LANES - OWN_BC, 0)))
    place_me = me.astype(jnp.int32).reshape(1)

    normed = all_positions(x_pieces, order, jnp.broadcast_to(gain_row, (8, D)))
    dt_tile = dot_nn(normed, w_conv[:, OWN:])
    bc = seq_pieces(bc_forward(dt_tile, taps_tile))
    conv_in = jnp.where(unit_used, dot_nn(normed, w_conv[:, :OWN]), 0.0).astype(bf16)
    if fast_mesh():
        w_o += [dp_swap_x(piece) for piece in w_o[1:4]]
    if not fast_mesh():
        cot_a = xor_seq(cot_a, 2)
    cot_a, cot_b, conv_in = tie(cot_a, cot_b, conv_in)
    cot_b = xor_seq(cot_b, 2)
    y, act, entry = recurrence_forward(place_me, conv_in, bc, dt_tile, taps, rows, skip_row)
    if fast_mesh():
        cot_b, *w_o[5:] = after([cot_b, *w_o[5:]], [entry])
    cot_pieces = (
        grad_out[0], xor_seq(grad_out[0], 1), cot_a, cot_b, xor_seq(cot_a, 1), xor_seq(cot_b, 1)
    )
    cot_all = all_positions(cot_pieces, order)
    if fast_mesh():
        w_o = assemble(w_o, out_places(), 512)
    row = jnp.concatenate(
        [
            gate_row,
            unit_used.astype(f32)[None, :],
            jnp.full((6, OWN), units_float),
        ],
        axis=0,
    )
    z, d_rounded, sums = gate_forward(normed, cot_all, y, w_gate, w_o, row)
    rounded_out, d_y, d_z, grad_gate_rows = gate_backward(y, z, d_rounded, seq_total(sums), row)
    grad_gate_local = grad_gate_rows[0]

    if fast_mesh():
        both = products(normed, d_z, rounded_out, cot_all)
        d_y, both = tie(d_y, both)
        both_total = dp_sum(both.reshape(-1, OWN))

    d_values, d_bc, d_dt, g_conv, g_rows = recurrence_backward(
        place_me, conv_in, act, d_y, y, bc, dt_tile, entry, taps, rows, skip_row
    )
    if fast_mesh():
        d_values, d_bc, rounded_out = tie(d_values, d_bc, rounded_out)
    branch = dot_nn(rounded_out, w_o).astype(bf16).reshape(PART, tokens, D)
    branch_mine, branch_got = core_halves(branch)
    d_bc_mine, d_bc_got = seq_scatter_relative(d_bc)
    branch_keep, branch_give = halves_sum(branch_mine, branch_got)
    d_bc_got, branch_give = tie(d_bc_got, branch_give)
    d_project, g_tail = tail_backward(
        dt_tile, d_bc_mine + d_bc_got.astype(f32), d_dt, taps_tile, d_values
    )
    g_skip = jnp.sum(g_conv[4].reshape(OWN_HEADS, HEAD_DIM), axis=1)
    small = jnp.concatenate(
        [
            g_conv[:CONV].reshape(-1),
            g_tail[:CONV, LANES - OWN_BC :].reshape(-1),
            pad_heads(g_rows[0, :OWN_HEADS]),
            pad_heads(g_rows[1, :OWN_HEADS]),
            pad_heads(g_skip),
            grad_gate_local,
        ]
    )
    count = small.shape[0]
    padded = -(-count // (8 * LANES)) * 8 * LANES
    small = jnp.pad(small, (0, padded - count)).reshape(-1, LANES)
    if fast_mesh():
        conv_product = dot_tn(normed, d_project).astype(bf16)
        d_project, conv_product = tie(d_project, conv_product)
        (conv_product,) = after([conv_product], [both_total])
        conv_total = dp_sum(conv_product)
    branch_across = xor_seq(branch_give, 2)
    d_normed = input_gradient(d_z, d_project, w_gate, w_conv)
    if fast_mesh():
        branch_across, d_normed = tie(branch_across, d_normed)
    mine, got = core_halves(d_normed.reshape(PART, tokens, D))
    keep, give = halves_sum(mine, got)
    small, give = tie(small, give)
    across = xor_seq(give, 2)
    small, across = tie(dp_total(small), across)
    d_own = keep + across.astype(f32)
    if fast_mesh():
        both_total = after([both_total], [across])[0]
        small_pieces = seq_pieces(small)
        gate_rows, out_left, out_right = jnp.split(both_total, [rows_in * PART, rows_in * PART + LANES])
        grad_w_out = jnp.concatenate([out_left, out_right], axis=1).astype(f32)
        gate_rows = owners_rows(gate_rows)
        (conv_total,) = after([conv_total], [small_pieces[3], *gate_rows[1:]])
        grad_w_in, grad_w_dt, grad_norm_gain = projection_rows(
            place_me, gate_rows, owners_rows(conv_total), w_in, w_dt, norm_gain
        )
        grad_norm_gain = grad_norm_gain[0]
    else:
        small_pieces = seq_pieces(small)
        grad_w_out = scatter_out(dot_tn(rounded_out, cot_all).astype(bf16))
        grad_gate_in = scatter_in(dot_tn(normed, d_z).astype(bf16))
        grad_conv_in = scatter_in(dot_tn(normed, d_project).astype(bf16))
        grad_w_in = jnp.concatenate(
            [
                from_owner(grad_gate_in),
                from_owner(grad_conv_in[:, :, :OWN]),
                grad_conv_in[:, :, CONV_COLS - OWN_BC :].transpose(1, 0, 2).reshape(rows_in, 2 * STATE),
            ],
            axis=1,
        )
        grad_w_dt = heads_from_owner(grad_conv_in[:, :, OWN : OWN + OWN_HEADS])
        grad_norm_gain = (
            jnp.sum(w_in.astype(f32) * grad_w_in, axis=1)
            + jnp.sum(w_dt.astype(f32) * grad_w_dt, axis=1)
        ) / norm_gain.astype(f32)
    x_own = hidden_in[0].astype(f32)
    hidden_out = (x_own + branch_keep + branch_across.astype(f32)).astype(bf16)[None]
    own_rms = lax.rsqrt(jnp.mean(x_own * x_own, axis=1, keepdims=True) + epsilon)
    d_scaled = d_own * gain_row
    d_input = own_rms * d_scaled - x_own * own_rms**3 * jnp.mean(
        d_scaled * x_own, axis=1, keepdims=True
    )
    grad_in = (grad_out[0].astype(f32) + d_input).astype(bf16)[None]

    every = jnp.stack(by_partner(small_pieces)).reshape(PART, padded)
    start = 0

    def take(size):
        nonlocal start
        start += size
        return every[:, start - size : start]

    all_conv = take(CONV * OWN).reshape(PART, CONV, OWN)
    all_conv_bc = take(CONV * OWN_BC).reshape(PART, CONV, OWN_BC)
    head_sums = [heads_from_owner(take(LANES)[:, None, :OWN_HEADS]).reshape(HEADS) for _ in range(3)]
    grad_gate = lax.dynamic_index_in_dim(take(OWN), me, 0, False)
    grad_conv = jnp.concatenate(
        [from_owner(all_conv), all_conv_bc.transpose(1, 0, 2).reshape(CONV, 2 * STATE)], axis=1
    )
    place = lax.axis_index(("dp", "seq"))
    gain_rows = gate_gain.shape[0]
    if gain_rows == LANES:
        grad_gate_gain = lax.dynamic_slice_in_dim(
            grad_gate, lax.axis_index("dp") * gain_rows, gain_rows, 0
        )
    else:
        start = CONV * OWN + CONV * OWN_BC + 3 * LANES
        whole_gate = from_owner(take(OWN)[:, None, :]).reshape(INNER)
        grad_gate_gain = lax.dynamic_slice_in_dim(whole_gate, place * gain_rows, gain_rows, 0)

    return (
        hidden_out,
        grad_in,
        grad_norm_gain,
        grad_w_in,
        grad_w_dt,
        grad_conv,
        head_sums[0],
        head_sums[1],
        head_sums[2],
        grad_gate_gain,
        grad_w_out,
    )


def solution(mesh):
    return jax.shard_map(
        per_device,
        mesh=mesh,
        in_specs=(
            P("dp", "seq", None),
            P("dp"),
            P(("dp", "seq")),
            P(("dp", "seq"), None),
            P(("dp", "seq"), None),
            P(),
            P(),
            P(),
            P(),
            P(("dp", "seq")),
            P(("dp", "seq"), None),
            P("dp", "seq", None),
        ),
        out_specs=(
            P("dp", "seq", None),
            P("dp", "seq", None),
            P(("dp", "seq")),
            P(("dp", "seq"), None),
            P(("dp", "seq"), None),
            P(),
            P(),
            P(),
            P(),
            P(("dp", "seq")),
            P(("dp", "seq"), None),
        ),
        check_vma=False,
    )
```

```python
import functools

import jax
import jax.numpy as jnp
from jax import lax
from jax.experimental import pallas as pl
from jax.experimental.pallas import tpu as pltpu
from jax.sharding import PartitionSpec as P

D = 2048
INNER = 4096
HEAD_DIM = 64
STATE = 128
CONV = 4
HEADS = 64
CHANNELS = 4352

PART = 4
LANES = 128
STRIPS = INNER // LANES // PART
OWN = STRIPS * LANES
OWN_HEADS = OWN // HEAD_DIM
OWN_BC = 2 * STATE // PART
CONV_COLS = OWN + LANES
Q = 256
HALF = Q // 2
WIDE = 512

epsilon = 1e-05
highest = lax.Precision.HIGHEST
f32 = jnp.float32
bf16 = jnp.bfloat16
LOG2E = 1.4426950408889634


def swap(value, axis, pairs):
    return lax.ppermute(value, axis, pairs)


def xor_seq(value, bits):
    return lax.ppermute(value, "seq", [(s, s ^ bits) for s in range(PART)])


def core_halves(blocks):
    core = lax.axis_index("seq") % 2
    view = blocks.reshape((2, 2) + blocks.shape[1:])
    mine = lax.dynamic_index_in_dim(view, core, 1, False)
    other = lax.dynamic_index_in_dim(view, 1 - core, 1, False)
    return mine, xor_seq(other, 1)


def halves_sum(mine, received):
    row = lax.axis_index("seq") // 2

    def of(which):
        a = lax.dynamic_index_in_dim(mine, which, 0, False)
        return a.astype(f32) + lax.dynamic_index_in_dim(received, which, 0, False).astype(f32)

    return of(row), of(1 - row).astype(bf16)


def seq_scatter_relative(blocks):
    view = blocks.reshape((2, 2) + blocks.shape[1:])
    half = view[:, 0].astype(f32) + xor_seq(view[:, 1], 1).astype(f32)
    return half[0], xor_seq(half[1].astype(bf16), 2)


def by_partner(pieces):
    me = lax.axis_index("seq")
    odd, lower = me % 2 == 1, me >= 2
    a, b, c, d = pieces
    a, b = jnp.where(odd, b, a), jnp.where(odd, a, b)
    c, d = jnp.where(odd, d, c), jnp.where(odd, c, d)
    return (
        jnp.where(lower, c, a),
        jnp.where(lower, d, b),
        jnp.where(lower, a, c),
        jnp.where(lower, b, d),
    )


def seq_exchange(pieces):
    turned = by_partner([pieces[k] for k in range(PART)])
    return [turned[0]] + [xor_seq(turned[k], k) for k in range(1, PART)]


def seq_total(value):
    return value + xor_seq(value, 1) + xor_seq(value, 2) + xor_seq(value, 3)


def fast_mesh():
    return lax.axis_size("dp") == 8


def dp_shift_z(value, steps):
    pairs = [(z * 2 + x, (z + steps) % 4 * 2 + x) for z in range(4) for x in range(2)]
    return lax.ppermute(value, "dp", pairs)


def dp_swap_x(value):
    return lax.ppermute(value, "dp", [(d, d ^ 1) for d in range(8)])


def tie_kernel(*refs):
    del refs


def tie(*values):
    anywhere = pl.BlockSpec(memory_space=pl.ANY)
    return pl.pallas_call(
        tie_kernel,
        in_specs=[anywhere] * len(values),
        out_specs=[anywhere] * len(values),
        out_shape=[jax.ShapeDtypeStruct(v.shape, v.dtype) for v in values],
        input_output_aliases={k: k for k in range(len(values))},
        name="tie",
    )(*values)


def after(values, needed):
    anywhere = pl.BlockSpec(memory_space=pl.ANY)
    return pl.pallas_call(
        tie_kernel,
        in_specs=[anywhere] * (len(values) + len(needed)),
        out_specs=[anywhere] * len(values),
        out_shape=[jax.ShapeDtypeStruct(v.shape, v.dtype) for v in values],
        input_output_aliases={k: k for k in range(len(values))},
        name="after",
    )(*values, *needed)


def assemble_kernel(places_ref, *refs):
    rows = refs[0].shape[0]
    for k, piece in enumerate(refs[:-1]):
        refs[-1][pl.ds(pl.multiple_of(places_ref[k] * rows, rows), rows), :] = piece[...]


def assemble(pieces, places, tile):
    rows, columns = pieces[0].shape
    count = len(pieces)
    along = lambda i, places: (0, i)
    return pl.pallas_call(
        assemble_kernel,
        grid_spec=pltpu.PrefetchScalarGridSpec(
            num_scalar_prefetch=1,
            grid=(columns // tile,),
            in_specs=[pl.BlockSpec((rows, tile), along)] * count,
            out_specs=pl.BlockSpec((rows * count, tile), along),
        ),
        out_shape=jax.ShapeDtypeStruct((rows * count, columns), pieces[0].dtype),
        compiler_params=pltpu.CompilerParams(vmem_limit_bytes=24 * 2**20),
        cost_estimate=pl.CostEstimate(
            flops=0, bytes_accessed=4 * rows * count * columns, transcendentals=0
        ),
        name="assemble",
    )(places, *pieces)


def pieces_kernel(w_ref, dt_ref, norm_ref, gate_ref, conv_ref, gates_ref):
    rows = w_ref.shape[0]
    lane = lax.broadcasted_iota(jnp.int32, (1, LANES), 1)
    square = lax.broadcasted_iota(jnp.int32, (rows, rows), 0) == lax.broadcasted_iota(
        jnp.int32, (rows, rows), 1
    )

    def column(values):
        return jnp.sum(jnp.where(square, values, 0.0), axis=1, keepdims=True)

    gain = column(norm_ref[0:1, :].astype(f32))
    gates = [column(gate_ref[k : k + 1, :].astype(f32)) for k in range(2)]
    head = lax.broadcasted_iota(jnp.int32, (HEADS, LANES), 0)
    slot = lax.broadcasted_iota(jnp.int32, (HEADS, LANES), 1)
    for owner in range(PART):
        for strip in range(STRIPS):
            source = (strip * PART + owner) * LANES
            at = slice(strip * LANES, (strip + 1) * LANES)
            gates_ref[owner, :, at] = w_ref[:, source : source + LANES]
            conv_ref[owner, :, at] = w_ref[:, INNER + source : INNER + source + LANES]
        chosen = (slot < OWN_HEADS) & (head == slot // 2 * 2 * PART + 2 * owner + slot % 2)
        steps = dot_nn(dt_ref[...], jnp.where(chosen, 1.0, 0.0).astype(bf16))
        first = 2 * INNER + owner // 2 * LANES
        tile = w_ref[:, first : first + LANES].astype(f32)
        if owner % 2 == 0:
            tile = pltpu.roll(tile, OWN_BC, 1)
        tail = jnp.where(lane < OWN_HEADS, steps, jnp.where(lane == OWN_HEADS, gain, 0.0))
        for k in range(2):
            tail = jnp.where(lane == OWN_HEADS + 1 + k, gates[k], tail)
        tail = jnp.where(lane >= LANES - OWN_BC, tile, tail)
        conv_ref[owner, :, OWN:] = tail.astype(bf16)


def owners_pieces(w_in, w_dt, norm_gain, gate_gain):
    rows = w_in.shape[0]
    whole = lambda *block: pl.BlockSpec(block, lambda i: (0,) * len(block))

    return pl.pallas_call(
        pieces_kernel,
        grid=(1,),
        in_specs=[whole(rows, 2 * INNER + 2 * STATE), whole(rows, HEADS), whole(1, rows), whole(2, rows)],
        out_specs=[whole(PART, rows, CONV_COLS), whole(PART, rows, OWN)],
        out_shape=[
            jax.ShapeDtypeStruct((PART, rows, CONV_COLS), bf16),
            jax.ShapeDtypeStruct((PART, rows, OWN), bf16),
        ],
        compiler_params=pltpu.CompilerParams(vmem_limit_bytes=32 * 2**20),
        name="owners_pieces",
    )(w_in, w_dt, norm_gain[None, :], gate_gain.reshape(2, rows))


def seq_pass(pieces, *beside):
    me = lax.axis_index("seq")
    core, row = me % 2, me // 2
    view = pieces.reshape((2, 2) + pieces.shape[1:])
    give = lax.dynamic_index_in_dim(view, 1 - row, 0, False)
    keep = lax.dynamic_index_in_dim(view, row, 0, False)
    got, *beside = tie(xor_seq(give, 2), *beside)
    lower = jnp.where(row == 0, keep, got)
    upper = jnp.where(row == 0, got, keep)
    both = jnp.stack([lower, upper])
    mine = lax.dynamic_index_in_dim(both, core, 1, False)
    other = xor_seq(lax.dynamic_index_in_dim(both, 1 - core, 1, False), 1)
    first = jnp.where(core == 0, mine, other)
    second = jnp.where(core == 0, other, mine)
    return jnp.stack([first, second], axis=1).reshape((-1,) + pieces.shape[2:]), beside


def seq_pieces(block, after=None):
    source = block if after is None else tie(block, after)[0]
    across = xor_seq(source, 2)
    return block, xor_seq(block, 1), across, xor_seq(across, 1)


def gather_everything(conv_pieces, gate_pieces, o, x_block, cot_block):
    c, (o1,) = seq_pass(conv_pieces, dp_shift_z(o, 1))
    w_conv = lax.all_gather(c, "dp", axis=0, tiled=True)
    x_across, gate_pieces, o2, o3, o_x = tie(
        xor_seq(after([x_block], [c])[0], 2),
        gate_pieces,
        dp_shift_z(o, 2),
        dp_shift_z(o, 3),
        dp_swap_x(o),
    )
    g, _ = seq_pass(gate_pieces)
    half = cot_block.shape[0] // 2
    cot_a, cot_b = after([cot_block[:half], cot_block[half:]], [g])
    g, x_across, cot_a = after([g, x_across, xor_seq(cot_a, 2)], [w_conv])
    x_pieces = (x_block, xor_seq(x_block, 1), x_across, xor_seq(x_across, 1))
    w_gate = lax.all_gather(g, "dp", axis=0, tiled=True)
    return w_conv, w_gate, [o, o1, o2, o3, o_x], x_pieces, (cot_a, cot_b)


def out_places():
    dp = lax.axis_index("dp")
    sources = (dp // 2 - jnp.arange(4, dtype=jnp.int32) + 4) % 4 * 2
    return jnp.concatenate([sources + dp % 2, sources + 1 - dp % 2]).astype(jnp.int32)


def norm_rows(x, gain):
    x = x.astype(f32)
    inverse = lax.rsqrt(jnp.mean(x * x, axis=1, keepdims=True) + epsilon)
    return (x * inverse * gain).astype(bf16)


def positions_kernel(shares, with_norm, order_ref, *refs):
    step = pl.program_id(0)
    first = 0
    for k, share in enumerate(shares):

        @pl.when((step >= first) & (step < first + share))
        def _():
            if with_norm:
                refs[-1][...] = norm_rows(refs[k][...], refs[-2][0:1, :])
            else:
                refs[-1][...] = refs[k][...]

        first += share


def all_positions(pieces, order, gain_rows=None):
    tile = min(256, min(p.shape[0] for p in pieces))
    shares = [p.shape[0] // tile for p in pieces]
    steps = sum(shares)
    each = steps // PART

    def place(first, share):
        return lambda i, order: (jnp.clip(i - first, 0, share - 1), 0)

    specs, first = [], 0
    for share in shares:
        specs.append(pl.BlockSpec((tile, D), place(first, share)))
        first += share
    extra = []
    if gain_rows is not None:
        specs.append(pl.BlockSpec((8, D), lambda i, order: (0, 0)))
        extra.append(gain_rows)
    return pl.pallas_call(
        functools.partial(positions_kernel, shares, gain_rows is not None),
        grid_spec=pltpu.PrefetchScalarGridSpec(
            num_scalar_prefetch=1,
            grid=(steps,),
            in_specs=specs,
            out_specs=pl.BlockSpec((tile, D), lambda i, order: (order[i // each] * each + i % each, 0)),
        ),
        out_shape=jax.ShapeDtypeStruct((tile * steps, D), bf16),
        compiler_params=pltpu.CompilerParams(vmem_limit_bytes=32 * 2**20),
        cost_estimate=pl.CostEstimate(
            flops=4 * tile * steps * D, bytes_accessed=4 * tile * steps * D, transcendentals=0
        ),
        name="all_positions",
    )(order, *pieces, *extra)


def dp_total(value):
    if not fast_mesh():
        return lax.psum(value, "dp")
    value = value + dp_swap_x(value)
    return value + dp_shift_z(value, 1) + dp_shift_z(value, 2) + dp_shift_z(value, 3)


def by_owner(columns):
    rows = columns.shape[0]
    return (
        columns.reshape(rows, STRIPS, PART, LANES).transpose(2, 0, 1, 3).reshape(PART, rows, OWN)
    )


def from_owner(pieces):
    rows = pieces.shape[1]
    return (
        pieces.reshape(PART, rows, STRIPS, LANES).transpose(1, 2, 0, 3).reshape(rows, INNER)
    )


def heads_by_owner(columns):
    rows = columns.shape[0]
    return (
        columns.reshape(rows, STRIPS, PART, 2).transpose(2, 0, 1, 3).reshape(PART, rows, OWN_HEADS)
    )


def heads_from_owner(pieces):
    rows = pieces.shape[1]
    return (
        pieces.reshape(PART, rows, STRIPS, 2).transpose(1, 2, 0, 3).reshape(rows, HEADS)
    )


def gather_in(pieces):
    full = lax.all_gather(pieces, ("dp", "seq"), axis=1, tiled=True)
    return lax.dynamic_index_in_dim(full, lax.axis_index("seq"), 0, False)


def dp_sum(product):
    return lax.psum_scatter(product, "dp", scatter_dimension=0, tiled=True)


def owners_rows(total):
    return seq_exchange(total.reshape(PART, -1, total.shape[1]))


def scatter_in(grads):
    full = jnp.zeros((PART,) + grads.shape, grads.dtype)
    full = lax.dynamic_update_index_in_dim(full, grads, lax.axis_index("seq"), 0)
    return lax.psum_scatter(full, ("dp", "seq"), scatter_dimension=1, tiled=True).astype(f32)


def gather_out(rows):
    full = lax.all_gather(rows, ("dp", "seq"), axis=0, tiled=True)
    full = full.reshape(STRIPS, PART, LANES, -1)
    return lax.dynamic_index_in_dim(full, lax.axis_index("seq"), 1, False).reshape(OWN, -1)


def gather_plainly(conv_pieces, gate_pieces, out_rows, x_block, cot_block):
    return (
        gather_in(conv_pieces),
        gather_in(gate_pieces),
        gather_out(out_rows),
        seq_pieces(x_block),
        jnp.split(cot_block, 2),
    )


def scatter_out(grads):
    full = jnp.zeros((STRIPS, PART, LANES, grads.shape[1]), grads.dtype)
    full = lax.dynamic_update_index_in_dim(
        full, grads.reshape(STRIPS, LANES, -1), lax.axis_index("seq"), 1
    )
    full = full.reshape(INNER, -1)
    return lax.psum_scatter(full, ("dp", "seq"), scatter_dimension=0, tiled=True).astype(f32)


def dot_nn(a, b):
    return lax.dot_general(a, b, (((1,), (0,)), ((), ())), preferred_element_type=f32)


def dot_nt(a, b):
    return lax.dot_general(a, b, (((1,), (1,)), ((), ())), preferred_element_type=f32)


def dot_tn(a, b):
    return lax.dot_general(a, b, (((0,), (0,)), ((), ())), preferred_element_type=f32)


def dot_exact(a, b):
    return lax.dot_general(
        a, b, (((1,), (0,)), ((), ())), precision=highest, preferred_element_type=f32
    )


def sigmoid(v):
    return 0.5 + 0.5 * jnp.tanh(0.5 * v)


def bc_forward_kernel(tile_ref, taps_ref, out_ref, padded):
    length = tile_ref.shape[0]
    padded[0:8, :] = jnp.zeros((8, LANES), f32)
    padded[8 : 8 + length, :] = tile_ref[...].astype(bf16).astype(f32)
    left = lax.broadcasted_iota(jnp.int32, (1, LANES), 1) < OWN_BC
    for block in range(length // Q):
        start = block * Q
        pre = taps_ref[0:1, :] * padded[start + 5 : start + 5 + Q, :]
        for tap in range(1, CONV):
            pre = pre + taps_ref[tap : tap + 1, :] * padded[start + 5 + tap : start + 5 + tap + Q, :]
        act = pre * sigmoid(pre)
        packed = jnp.where(left, pltpu.roll(act[HALF:], OWN_BC, 1), act[:HALF])
        out_ref[block * HALF : (block + 1) * HALF, :] = packed.astype(bf16)


def bc_forward(dt_tile, taps_tile):
    length = dt_tile.shape[0]
    return pl.pallas_call(
        bc_forward_kernel,
        out_shape=jax.ShapeDtypeStruct((length // 2, LANES), bf16),
        scratch_shapes=[pltpu.VMEM((8 + length, LANES), f32)],
        compiler_params=pltpu.CompilerParams(vmem_limit_bytes=16 * 2**20),
        cost_estimate=pl.CostEstimate(
            flops=20 * length * LANES, bytes_accessed=5 * length * LANES, transcendentals=0
        ),
        name="bc_forward",
    )(dt_tile, taps_tile)


def tail_kernel(tile_ref, grad_ref, ddt_ref, taps_ref, into_ref, out_ref, sums_ref, padded, dp):
    del into_ref
    length = tile_ref.shape[0]
    padded[0:8, :] = jnp.zeros((8, LANES), f32)
    padded[8 : 8 + length, :] = tile_ref[...].astype(bf16).astype(f32)
    dp[length : length + 8, :] = jnp.zeros((8, LANES), f32)
    lane = lax.broadcasted_iota(jnp.int32, (1, LANES), 1)
    left = lane < OWN_BC
    sums_ref[...] = jnp.zeros_like(sums_ref)
    for block in reversed(range(length // Q)):
        start = block * Q
        taken = [padded[start + 5 + tap : start + 5 + tap + Q, :] for tap in range(CONV)]
        pre = taps_ref[0:1, :] * taken[0]
        for tap in range(1, CONV):
            pre = pre + taps_ref[tap : tap + 1, :] * taken[tap]
        packed = grad_ref[block * HALF : (block + 1) * HALF, :]
        grad = jnp.concatenate([packed, pltpu.roll(packed, OWN_BC, 1)], axis=0)
        squashed = sigmoid(pre)
        d_pre = jnp.where(left, 0.0, grad * squashed * (1.0 + pre * (1.0 - squashed)))
        dp[start : start + Q, :] = d_pre
        for tap in range(CONV):
            sums_ref[tap : tap + 1, :] += jnp.sum(d_pre * taken[tap], axis=0, keepdims=True)
        d_in = taps_ref[CONV - 1 : CONV, :] * d_pre
        for tap in range(CONV - 1):
            first = start + CONV - 1 - tap
            d_in = d_in + taps_ref[tap : tap + 1, :] * dp[first : first + Q, :]
        d_dt = jnp.where(lane < OWN_HEADS, ddt_ref[start : start + Q, :], 0.0)
        out_ref[start : start + Q, :] = jnp.where(left, d_dt, d_in).astype(bf16)


def tail_backward(dt_tile, grad, d_dt, taps_tile, into):
    length = dt_tile.shape[0]
    whole = lambda i: (0, 0)
    return pl.pallas_call(
        tail_kernel,
        grid=(1,),
        in_specs=[
            pl.BlockSpec((length, LANES), whole),
            pl.BlockSpec((length // 2, LANES), whole),
            pl.BlockSpec((length, LANES), whole),
            pl.BlockSpec((8, LANES), whole),
            pl.BlockSpec(memory_space=pl.ANY),
        ],
        out_specs=[
            pl.BlockSpec((length, LANES), lambda i: (0, STRIPS)),
            pl.BlockSpec((8, LANES), whole),
        ],
        out_shape=[
            jax.ShapeDtypeStruct(into.shape, bf16),
            jax.ShapeDtypeStruct((8, LANES), f32),
        ],
        input_output_aliases={4: 0},
        scratch_shapes=[pltpu.VMEM((8 + length, LANES), f32), pltpu.VMEM((8 + length, LANES), f32)],
        compiler_params=pltpu.CompilerParams(vmem_limit_bytes=60 * 2**20),
        cost_estimate=pl.CostEstimate(
            flops=40 * length * LANES, bytes_accessed=14 * length * LANES, transcendentals=0
        ),
        name="tail_backward",
    )(dt_tile, grad, d_dt, taps_tile, into)


def keys_and_reads(me, refs):
    odd, lower = me % 2 == 1, me >= 2
    p = [ref[...].astype(f32) for ref in refs]
    r0, r1 = jnp.where(odd, p[1], p[0]), jnp.where(odd, p[0], p[1])
    r2, r3 = jnp.where(odd, p[3], p[2]), jnp.where(odd, p[2], p[3])
    q = (
        jnp.where(lower, r2, r0),
        jnp.where(lower, r3, r1),
        jnp.where(lower, r0, r2),
        jnp.where(lower, r1, r3),
    )
    left = lax.broadcasted_iota(jnp.int32, (1, LANES), 1) < OWN_BC

    def join(a, b):
        top = jnp.where(left, pltpu.roll(a, OWN_BC, 1), b)
        bottom = jnp.where(left, a, pltpu.roll(b, OWN_BC, 1))
        return jnp.concatenate([top, bottom], axis=0).astype(bf16)

    return join(q[0], q[1]), join(q[2], q[3])


def give_back(me, d_keys, d_reads, out_ref):
    left = lax.broadcasted_iota(jnp.int32, (1, LANES), 1) < OWN_BC
    for pair, array in enumerate((d_keys, d_reads)):
        top, bottom = array[:HALF], array[HALF:]
        low = jnp.where(left, bottom, pltpu.roll(top, OWN_BC, 1))
        high = jnp.where(left, pltpu.roll(bottom, OWN_BC, 1), top)
        out_ref[jnp.bitwise_xor(me, 2 * pair)] = low.astype(bf16)
        out_ref[jnp.bitwise_xor(me, 2 * pair + 1)] = high.astype(bf16)


def decay_terms(dt_ref, rows_ref):
    v = dt_ref[...] * rows_ref[2:3, :] + rows_ref[0:1, :]
    steps = jnp.maximum(v, 0.0) + jnp.log1p(jnp.exp(-jnp.abs(v)))
    log2_decay = rows_ref[1:2, :] * LOG2E * steps
    row = lax.broadcasted_iota(jnp.int32, (Q, Q), 0)
    column = lax.broadcasted_iota(jnp.int32, (Q, Q), 1)
    lower = jnp.where(row >= column, 1.0, 0.0)
    running = dot_exact(lower, log2_decay)
    shifted = running - jnp.log(steps) * LOG2E
    end = running[Q - 1 : Q, :]
    return v, steps, running, shifted, end


def spread_heads(values, spread):
    high = values.astype(bf16)
    low = (values - high.astype(f32)).astype(bf16)
    return dot_nn(high, spread) + dot_nn(low, spread)


def forward_kernel(
    me_ref, ci_ref, b0, b1, b2, b3, dt_ref, cw_ref, rows_ref, skip_ref, y_ref, act_ref, s_ref, state, xf,
    e_wide, w_wide
):
    @pl.when(pl.program_id(0) == 0)
    def _():
        state[...] = jnp.zeros_like(state)
        xf[0:8, :] = jnp.zeros((8, OWN), f32)

    @pl.when(pl.program_id(0) > 0)
    def _():
        xf[0:8, :] = xf[Q : Q + 8, :]

    xf[8 : Q + 8, :] = ci_ref[...].astype(f32)
    _, _, running, shifted, end = decay_terms(dt_ref, rows_ref)
    shifted_t = shifted.T
    e_run = jnp.exp2(running)
    w_end = jnp.exp2(end - shifted)
    e_end = jnp.exp2(end)
    keys, reads = keys_and_reads(me_ref[0], (b0, b1, b2, b3))
    keys_t = keys.T
    cb = dot_nt(reads, keys)
    causal = lax.broadcasted_iota(jnp.int32, (HALF, HALF), 0) >= lax.broadcasted_iota(
        jnp.int32, (HALF, HALF), 1
    )
    left = lax.broadcasted_iota(jnp.int32, (1, LANES), 1) < HEAD_DIM
    spread = lax.broadcasted_iota(jnp.int32, (LANES, OWN), 0) == (
        lax.broadcasted_iota(jnp.int32, (LANES, OWN), 1) // HEAD_DIM
    )
    spread = jnp.where(spread, 1.0, 0.0).astype(bf16)
    e_wide[...] = spread_heads(e_run, spread)
    w_wide[...] = spread_heads(w_end, spread)
    s_ref[0] = state[...].astype(bf16)
    for strip in range(STRIPS):
        at = slice(strip * LANES, (strip + 1) * LANES)
        h0, h1 = 2 * strip, 2 * strip + 1
        pre = cw_ref[0:1, at] * xf[5 : 5 + Q, at]
        for tap in range(1, CONV):
            pre = pre + cw_ref[tap : tap + 1, at] * xf[5 + tap : 5 + tap + Q, at]
        act = (pre * sigmoid(pre)).astype(bf16)
        act_ref[:, at] = act
        actf = act.astype(f32)
        inter = dot_nn(reads, s_ref[0, :, at]) * e_wide[:, at]
        inter = inter + skip_ref[0:1, at] * actf
        top, bottom = inter[:HALF], inter[HALF:]
        for h, side in ((h0, left), (h1, jnp.logical_not(left))):
            x_h = jnp.where(side, act, jnp.zeros_like(act))
            m00 = jnp.where(
                causal,
                jnp.exp2(running[:HALF, h : h + 1] - shifted_t[h : h + 1, :HALF]) * cb[:HALF, :HALF],
                0.0,
            )
            m10 = jnp.exp2(running[HALF:, h : h + 1] - shifted_t[h : h + 1, :HALF]) * cb[HALF:, :HALF]
            m11 = jnp.where(
                causal,
                jnp.exp2(running[HALF:, h : h + 1] - shifted_t[h : h + 1, HALF:]) * cb[HALF:, HALF:],
                0.0,
            )
            top = top + dot_nn(m00.astype(bf16), x_h[:HALF])
            bottom = bottom + dot_nn(
                jnp.concatenate([m10.astype(bf16), m11.astype(bf16)], axis=1), x_h
            )
        y_ref[:HALF, at] = top
        y_ref[HALF:, at] = bottom
        weighted = (actf * w_wide[:, at]).astype(bf16)
        state[:, at] = state[:, at] * jnp.where(
            left, e_end[:, h0 : h0 + 1], e_end[:, h1 : h1 + 1]
        ) + dot_nn(keys_t, weighted)


def recurrence_forward(me, conv_in, bc, dt_tile, taps, rows, skip_row):
    length = conv_in.shape[0]
    blocks = length // Q
    whole = lambda i, me: (0, 0)
    along = lambda i, me: (i, 0)
    return pl.pallas_call(
        forward_kernel,
        grid_spec=pltpu.PrefetchScalarGridSpec(
            num_scalar_prefetch=1,
            grid=(blocks,),
            in_specs=[pl.BlockSpec((Q, OWN), along)]
            + [pl.BlockSpec((HALF, LANES), along)] * PART
            + [
                pl.BlockSpec((Q, LANES), along),
                pl.BlockSpec((8, OWN), whole),
                pl.BlockSpec((8, LANES), whole),
                pl.BlockSpec((8, OWN), whole),
            ],
            out_specs=[
                pl.BlockSpec((Q, OWN), along),
                pl.BlockSpec((Q, OWN), along),
                pl.BlockSpec((1, STATE, OWN), lambda i, me: (i, 0, 0)),
            ],
            scratch_shapes=[
                pltpu.VMEM((STATE, OWN), f32),
                pltpu.VMEM((Q + 8, OWN), f32),
                pltpu.VMEM((Q, OWN), f32),
                pltpu.VMEM((Q, OWN), f32),
            ],
        ),
        out_shape=[
            jax.ShapeDtypeStruct((length, OWN), f32),
            jax.ShapeDtypeStruct((length, OWN), bf16),
            jax.ShapeDtypeStruct((blocks, STATE, OWN), bf16),
        ],
        compiler_params=pltpu.CompilerParams(
            dimension_semantics=("arbitrary",), vmem_limit_bytes=60 * 2**20
        ),
        cost_estimate=pl.CostEstimate(
            flops=40 * 10**9, bytes_accessed=2**24, transcendentals=10**7
        ),
        name="recurrence_forward",
    )(me, conv_in, *bc, dt_tile, taps, rows, skip_row)


def backward_kernel(
    me_ref,
    ci_ref,
    prev_ref,
    act_ref,
    dy_ref,
    y_ref,
    b0,
    b1,
    b2,
    b3,
    dt_ref,
    s_ref,
    cw_ref,
    rows_ref,
    skip_ref,
    dci_ref,
    dbc_ref,
    ddt_ref,
    gconv_ref,
    grow_ref,
    back,
    back16,
    dp,
    xf,
    edy,
    wx,
    dcb,
    p12h,
    p12l,
    p3,
    p23,
    cross,
):
    step = pl.program_id(0)
    last = pl.num_programs(0) - 1

    @pl.when(step == 0)
    def _():
        back[...] = jnp.zeros_like(back)
        dp[Q : Q + 8, :] = jnp.zeros((8, OWN), f32)
        gconv_ref[...] = jnp.zeros_like(gconv_ref)
        grow_ref[...] = jnp.zeros_like(grow_ref)
        cross[...] = jnp.zeros_like(cross)

    @pl.when(step > 0)
    def _():
        dp[Q : Q + 8, :] = dp[0:8, :]

    before = prev_ref[8:16, :].astype(f32)
    xf[0:8, :] = jnp.where(step == last, 0.0, before)
    xf[8 : Q + 8, :] = ci_ref[...].astype(f32)
    v, steps, running, shifted, end = decay_terms(dt_ref, rows_ref)
    running_t = running.T
    e_run = jnp.exp2(running)
    w_end = jnp.exp2(end - shifted)
    e_end = jnp.exp2(end)
    keys, reads = keys_and_reads(me_ref[0], (b0, b1, b2, b3))
    reads_t = reads.T
    cbt = dot_nt(keys, reads)
    ahead = lax.broadcasted_iota(jnp.int32, (HALF, HALF), 0) <= lax.broadcasted_iota(
        jnp.int32, (HALF, HALF), 1
    )
    left = lax.broadcasted_iota(jnp.int32, (1, LANES), 1) < HEAD_DIM
    back16[...] = back[...].astype(bf16)
    dcb[...] = jnp.zeros_like(dcb)
    for strip in range(STRIPS):
        at = slice(strip * LANES, (strip + 1) * LANES)
        h0, h1 = 2 * strip, 2 * strip + 1
        act = act_ref[:, at]
        dy = dy_ref[:, at]
        actf = act.astype(f32)
        dyf = dy.astype(f32)
        skip = skip_ref[0:1, at]
        w_pair = jnp.where(left, w_end[:, h0 : h0 + 1], w_end[:, h1 : h1 + 1])
        e_pair = jnp.where(left, e_run[:, h0 : h0 + 1], e_run[:, h1 : h1 + 1])
        decayed = (dyf * e_pair).astype(bf16)
        edy[:, at] = decayed
        wx[:, at] = (actf * w_pair).astype(bf16)
        inter = dot_nn(keys, back16[:, at]) * w_pair
        top = jnp.zeros((HALF, LANES), f32)
        bottom = jnp.zeros((HALF, LANES), f32)
        for h, side in ((h0, left), (h1, jnp.logical_not(left))):
            x_h = jnp.where(side, actf, 0.0).astype(bf16)
            dy_h = jnp.where(side, dyf, 0.0).astype(bf16)
            g_top = dot_nt(x_h[:HALF], dy)
            g_bottom = dot_nt(x_h[HALF:], dy[HALF:])
            l00 = jnp.exp2(running_t[h : h + 1, :HALF] - shifted[:HALF, h : h + 1])
            l01 = jnp.exp2(running_t[h : h + 1, HALF:] - shifted[:HALF, h : h + 1])
            l11 = jnp.exp2(running_t[h : h + 1, HALF:] - shifted[HALF:, h : h + 1])
            m00 = jnp.where(ahead, l00 * cbt[:HALF, :HALF], 0.0).astype(bf16)
            m01 = (l01 * cbt[:HALF, HALF:]).astype(bf16)
            m11 = jnp.where(ahead, l11 * cbt[HALF:, HALF:], 0.0).astype(bf16)
            top = top + dot_nn(jnp.concatenate([m00, m01], axis=1), dy_h)
            bottom = bottom + dot_nn(m11, dy_h[HALF:])
            dcb[:HALF, :HALF] += jnp.where(ahead, l00 * g_top[:, :HALF], 0.0)
            dcb[:HALF, HALF:] += l01 * g_top[:, HALF:]
            dcb[HALF:, HALF:] += jnp.where(ahead, l11 * g_bottom, 0.0)
        intra = jnp.concatenate([top, bottom], axis=0)
        d_values = intra + inter
        p_12 = dyf * (y_ref[:, at] - skip * actf) - actf * intra
        p_12h = p_12.astype(bf16)
        p12h[:, at] = p_12h
        p12l[:, at] = (p_12 - p_12h.astype(f32)).astype(bf16)
        p3[:, at] = (actf * inter).astype(bf16)
        p23[:, at] = (actf * d_values).astype(bf16)
        d_act = d_values + skip * dyf
        pre = cw_ref[0:1, at] * xf[5 : 5 + Q, at]
        for tap in range(1, CONV):
            pre = pre + cw_ref[tap : tap + 1, at] * xf[5 + tap : 5 + tap + Q, at]
        squashed = sigmoid(pre)
        d_pre = d_act * squashed * (1.0 + pre * (1.0 - squashed))
        dp[0:Q, at] = d_pre
        sums = [
            jnp.sum(d_pre * xf[5 + tap : 5 + tap + Q, at], axis=0, keepdims=True)
            for tap in range(CONV)
        ]
        sums.append(jnp.sum(dyf * actf, axis=0, keepdims=True))
        for place, total in enumerate(sums):
            gconv_ref[place : place + 1, at] += total
        d_in = cw_ref[CONV - 1 : CONV, at] * d_pre
        for tap in range(CONV - 1):
            d_in = d_in + cw_ref[tap : tap + 1, at] * dp[CONV - 1 - tap : CONV - 1 - tap + Q, at]
        dci_ref[:, at] = d_in.astype(bf16)
        kept = back[:, at] * jnp.where(left, e_end[:, h0 : h0 + 1], e_end[:, h1 : h1 + 1])
        cross[0:1, at] = jnp.sum(kept * s_ref[0, :, at].astype(f32), axis=0, keepdims=True)
        back[:, at] = kept + dot_nn(reads_t, decayed)
    dcb_t = dcb[...]
    d_keys = dot_nn(dcb_t.astype(bf16), reads) + dot_nt(wx[...], back16[...])
    d_reads = dot_nn(dcb_t.T.astype(bf16), keys) + dot_nt(edy[...], s_ref[0])
    give_back(me_ref[0], d_keys, d_reads, dbc_ref)
    unit = lax.broadcasted_iota(jnp.int32, (OWN, LANES), 0)
    head = lax.broadcasted_iota(jnp.int32, (OWN, LANES), 1)
    member = jnp.where(unit // HEAD_DIM == head, 1.0, 0.0)
    member16 = member.astype(bf16)
    s_12 = dot_nn(p12h[...], member16) + dot_nn(p12l[...], member16)
    s_3 = dot_nn(p3[...], member16)
    s_23 = dot_nn(p23[...], member16)
    through = dot_exact(cross[...], member)[0:1, :]
    row = lax.broadcasted_iota(jnp.int32, (Q, Q), 0)
    column = lax.broadcasted_iota(jnp.int32, (Q, Q), 1)
    suffix = jnp.where(column >= row, 1.0, 0.0)
    prefix = jnp.where(column < row, 1.0, 0.0)
    d_log = dot_exact(suffix, s_12) + dot_exact(prefix, s_3) + through
    slope = sigmoid(v)
    ratio = jnp.where(steps > 0.0, slope / steps, 0.0)
    rate = rows_ref[1:2, :]
    d_sum = s_23 * ratio + rate * d_log * slope
    ddt_ref[...] = d_sum * rows_ref[2:3, :]
    grow_ref[0:1, :] += jnp.sum(d_sum, axis=0, keepdims=True)
    grow_ref[1:2, :] += jnp.sum(d_log * rate * steps, axis=0, keepdims=True)


def recurrence_backward(me, conv_in, act, dy, y, bc, dt_tile, entry, taps, rows, skip_row):
    length = conv_in.shape[0]
    blocks = length // Q
    whole = lambda i, me: (0, 0)
    along = lambda i, me: (blocks - 1 - i, 0)
    previous = lambda i, me: (jnp.maximum((blocks - 1 - i) * (Q // 16) - 1, 0), 0)
    return pl.pallas_call(
        backward_kernel,
        grid_spec=pltpu.PrefetchScalarGridSpec(
            num_scalar_prefetch=1,
            grid=(blocks,),
            in_specs=[
                pl.BlockSpec((Q, OWN), along),
                pl.BlockSpec((16, OWN), previous),
                pl.BlockSpec((Q, OWN), along),
                pl.BlockSpec((Q, OWN), along),
                pl.BlockSpec((Q, OWN), along),
            ]
            + [pl.BlockSpec((HALF, LANES), along)] * PART
            + [
                pl.BlockSpec((Q, LANES), along),
                pl.BlockSpec((1, STATE, OWN), lambda i, me: (blocks - 1 - i, 0, 0)),
                pl.BlockSpec((8, OWN), whole),
                pl.BlockSpec((8, LANES), whole),
                pl.BlockSpec((8, OWN), whole),
            ],
            out_specs=[
                pl.BlockSpec((Q, OWN), along),
                pl.BlockSpec((PART, HALF, LANES), lambda i, me: (0, blocks - 1 - i, 0)),
                pl.BlockSpec((Q, LANES), along),
                pl.BlockSpec((8, OWN), whole),
                pl.BlockSpec((8, LANES), whole),
            ],
            scratch_shapes=[
                pltpu.VMEM((STATE, OWN), f32),
                pltpu.VMEM((STATE, OWN), bf16),
                pltpu.VMEM((Q + 8, OWN), f32),
                pltpu.VMEM((Q + 8, OWN), f32),
                pltpu.VMEM((Q, OWN), bf16),
                pltpu.VMEM((Q, OWN), bf16),
                pltpu.VMEM((Q, Q), f32),
                pltpu.VMEM((Q, OWN), bf16),
                pltpu.VMEM((Q, OWN), bf16),
                pltpu.VMEM((Q, OWN), bf16),
                pltpu.VMEM((Q, OWN), bf16),
                pltpu.VMEM((8, OWN), f32),
            ],
        ),
        out_shape=[
            jax.ShapeDtypeStruct((length, CONV_COLS), bf16),
            jax.ShapeDtypeStruct((PART, length // 2, LANES), bf16),
            jax.ShapeDtypeStruct((length, LANES), f32),
            jax.ShapeDtypeStruct((8, OWN), f32),
            jax.ShapeDtypeStruct((8, LANES), f32),
        ],
        compiler_params=pltpu.CompilerParams(
            dimension_semantics=("arbitrary",), vmem_limit_bytes=60 * 2**20
        ),
        cost_estimate=pl.CostEstimate(
            flops=70 * 10**9, bytes_accessed=2**24, transcendentals=10**7
        ),
        name="recurrence_backward",
    )(me, conv_in, conv_in, act, dy, y, *bc, dt_tile, entry, taps, rows, skip_row)


def pull_out_kernel(order_ref, own, sibling, across_a, across_b, corner_a, corner_b, wo_ref, cot_ref, d_ref):
    del order_ref
    step = pl.program_id(0)
    half = across_a.shape[0]
    for k, ref in enumerate((own, sibling)):

        @pl.when(step == k)
        def _():
            cot_ref[...] = ref[...]

    for k, (first, second) in enumerate(((across_a, across_b), (corner_a, corner_b))):

        @pl.when(step == 2 + k)
        def _():
            cot_ref[:half, :] = first[...]
            cot_ref[half:, :] = second[...]

    d_ref[...] = dot_nt(cot_ref[...], wo_ref[...])


def pull_out(pieces, order, w_o):
    tile = pieces[0].shape[0]
    whole = lambda i, order: (0, 0)
    there = lambda i, order: (order[i], 0)
    length = tile * PART
    return pl.pallas_call(
        pull_out_kernel,
        grid_spec=pltpu.PrefetchScalarGridSpec(
            num_scalar_prefetch=1,
            grid=(PART,),
            in_specs=[pl.BlockSpec(piece.shape, whole) for piece in pieces]
            + [pl.BlockSpec((OWN, D), whole)],
            out_specs=[pl.BlockSpec((tile, D), there), pl.BlockSpec((tile, OWN), there)],
        ),
        out_shape=[
            jax.ShapeDtypeStruct((length, D), bf16),
            jax.ShapeDtypeStruct((length, OWN), f32),
        ],
        compiler_params=pltpu.CompilerParams(vmem_limit_bytes=52 * 2**20),
        cost_estimate=pl.CostEstimate(
            flops=2 * length * D * OWN, bytes_accessed=2**25, transcendentals=0
        ),
        name="pull_out",
    )(order, *pieces, w_o)


def gate_forward_kernel(n_ref, y_ref, d_ref, wg_ref, row_ref, z_ref, sums_ref):
    z = dot_nn(n_ref[...], wg_ref[...]) * row_ref[1:2, :]
    z_ref[...] = z
    gated = y_ref[...] * (z * sigmoid(z))
    squares = jnp.sum(gated * gated, axis=1, keepdims=True)
    cross = jnp.sum(d_ref[...] * row_ref[0:1, :] * gated, axis=1, keepdims=True)
    lane = lax.broadcasted_iota(jnp.int32, (1, LANES), 1)
    both = jnp.where(lane == 0, squares, jnp.where(lane == 1, cross, 0.0))
    sums_ref[...] = both.T[0:8, :]


def gate_forward(normed, y, d, w_gate, row):
    length = normed.shape[0]
    whole = lambda i: (0, 0)
    along = lambda i: (i, 0)
    return pl.pallas_call(
        gate_forward_kernel,
        grid=(length // WIDE,),
        in_specs=[
            pl.BlockSpec((WIDE, D), along),
            pl.BlockSpec((WIDE, OWN), along),
            pl.BlockSpec((WIDE, OWN), along),
            pl.BlockSpec((D, OWN), whole),
            pl.BlockSpec((8, OWN), whole),
        ],
        out_specs=[
            pl.BlockSpec((WIDE, OWN), along),
            pl.BlockSpec((8, WIDE), lambda i: (0, i)),
        ],
        out_shape=[
            jax.ShapeDtypeStruct((length, OWN), f32),
            jax.ShapeDtypeStruct((8, length), f32),
        ],
        compiler_params=pltpu.CompilerParams(vmem_limit_bytes=52 * 2**20),
        cost_estimate=pl.CostEstimate(
            flops=2 * length * D * OWN, bytes_accessed=2**25, transcendentals=length * OWN
        ),
        name="gate_forward",
    )(normed, y, d, w_gate, row)


def gate_backward_kernel(y_ref, z_ref, d_ref, sums_ref, row_ref, out_ref, dy_ref, dz_ref, gain_ref):
    @pl.when(pl.program_id(0) == 0)
    def _():
        gain_ref[...] = jnp.zeros_like(gain_ref)

    units = row_ref[2:3, 0:1]
    sums = sums_ref[...]
    inverse = lax.rsqrt(sums[0:1, :] / units + epsilon)
    pull = inverse * inverse * inverse * sums[1:2, :] / units
    row = lax.broadcasted_iota(jnp.int32, (LANES, 1), 0)
    columns = jnp.where(row == 0, inverse, jnp.where(row == 1, pull, 0.0)).T
    inverse, pull = columns[:, 0:1], columns[:, 1:2]
    for strip in range(STRIPS):
        at = slice(strip * LANES, (strip + 1) * LANES)
        y, z, d = y_ref[:, at], z_ref[:, at], d_ref[:, at]
        gain = row_ref[0:1, at]
        squashed = sigmoid(z)
        act = z * squashed
        gated = y * act
        normalized = gated * inverse
        out_ref[:, at] = (normalized * gain).astype(bf16)
        gain_ref[0:1, at] += jnp.sum(d * normalized, axis=0, keepdims=True)
        d_gated = inverse * (d * gain) - gated * pull
        dy_ref[:, at] = (d_gated * act).astype(bf16)
        dz_ref[:, at] = (d_gated * y * squashed * (1.0 + z * (1.0 - squashed))).astype(bf16)


def gate_backward(y, z, d, sums, row):
    length = y.shape[0]
    whole = lambda i: (0, 0)
    along = lambda i: (i, 0)
    return pl.pallas_call(
        gate_backward_kernel,
        grid=(length // Q,),
        in_specs=[pl.BlockSpec((Q, OWN), along)] * 3
        + [pl.BlockSpec((8, Q), lambda i: (0, i)), pl.BlockSpec((8, OWN), whole)],
        out_specs=[pl.BlockSpec((Q, OWN), along)] * 3 + [pl.BlockSpec((8, OWN), whole)],
        out_shape=[jax.ShapeDtypeStruct((length, OWN), bf16)] * 3
        + [jax.ShapeDtypeStruct((8, OWN), f32)],
        compiler_params=pltpu.CompilerParams(vmem_limit_bytes=32 * 2**20),
        cost_estimate=pl.CostEstimate(
            flops=30 * length * OWN, bytes_accessed=18 * length * OWN, transcendentals=length * OWN
        ),
        name="gate_backward",
    )(y, z, d, sums, row)


def input_gradient_kernel(z_ref, p_ref, wg_ref, wc_ref, out_ref):
    out_ref[...] = (dot_nt(z_ref[...], wg_ref[...]) + dot_nt(p_ref[...], wc_ref[...])).astype(bf16)


def input_gradient(d_z, d_project, w_gate, w_conv):
    length = d_z.shape[0]
    whole = lambda i: (0, 0)
    along = lambda i: (i, 0)
    return pl.pallas_call(
        input_gradient_kernel,
        grid=(length // WIDE,),
        in_specs=[
            pl.BlockSpec((WIDE, OWN), along),
            pl.BlockSpec((WIDE, CONV_COLS), along),
            pl.BlockSpec((D, OWN), whole),
            pl.BlockSpec((D, CONV_COLS), whole),
        ],
        out_specs=pl.BlockSpec((WIDE, D), along),
        out_shape=jax.ShapeDtypeStruct((length, D), bf16),
        compiler_params=pltpu.CompilerParams(vmem_limit_bytes=60 * 2**20),
        cost_estimate=pl.CostEstimate(
            flops=10**10, bytes_accessed=2**22, transcendentals=0
        ),
        name="input_gradient",
    )(d_z, d_project, w_gate, w_conv)


def products_kernel(n_ref, z_ref, r_ref, t_ref, out_ref):
    rows = D // STRIPS
    gate = dot_nn(n_ref[...].T, z_ref[...]).astype(bf16)
    rest = dot_nn(r_ref[...].T, t_ref[...]).astype(bf16)
    for k in range(out_ref.shape[0]):
        out_ref[k, :rows, :] = gate[k * rows : (k + 1) * rows]
        product = rest[k * LANES : (k + 1) * LANES]
        out_ref[k, rows : rows + LANES, :] = product[:, :OWN]
        out_ref[k, rows + LANES :, :] = product[:, OWN:]


def products(normed, d_z, rounded_out, cot):
    length = normed.shape[0]
    rows = D // STRIPS
    each = 2
    whole = lambda i: (0, 0)
    across = lambda i: (0, i)
    return pl.pallas_call(
        products_kernel,
        grid=(STRIPS // each,),
        in_specs=[
            pl.BlockSpec((length, each * rows), across),
            pl.BlockSpec((length, OWN), whole),
            pl.BlockSpec((length, each * LANES), across),
            pl.BlockSpec((length, D), whole),
        ],
        out_specs=pl.BlockSpec((each, rows + 2 * LANES, OWN), lambda i: (i, 0, 0)),
        out_shape=jax.ShapeDtypeStruct((STRIPS, rows + 2 * LANES, OWN), bf16),
        compiler_params=pltpu.CompilerParams(vmem_limit_bytes=56 * 2**20),
        cost_estimate=pl.CostEstimate(
            flops=4 * length * D * OWN, bytes_accessed=2**25, transcendentals=0
        ),
        name="products",
    )(normed, d_z, rounded_out, cot)


def rows_kernel(me_ref, *refs):
    gates, convs = refs[:PART], refs[PART : 2 * PART]
    w_ref, wdt_ref, gain_ref, grad_ref, gdt_ref, gnorm_ref = refs[2 * PART :]
    me = me_ref[0]
    rows = w_ref.shape[0]
    for k in range(PART):
        owner = jnp.bitwise_xor(me, k)
        for strip in range(STRIPS):
            at = slice(strip * LANES, (strip + 1) * LANES)
            first = pl.multiple_of((strip * PART + owner) * LANES, LANES)
            grad_ref[:, pl.ds(first, LANES)] = gates[k][:, at].astype(f32)
            grad_ref[:, pl.ds(INNER + first, LANES)] = convs[k][:, at].astype(f32)
    odd, lower = me % 2 == 1, me >= 2
    p = [convs[k][:, OWN:].astype(f32) for k in range(PART)]
    r0, r1 = jnp.where(odd, p[1], p[0]), jnp.where(odd, p[0], p[1])
    r2, r3 = jnp.where(odd, p[3], p[2]), jnp.where(odd, p[2], p[3])
    tails = (
        jnp.where(lower, r2, r0),
        jnp.where(lower, r3, r1),
        jnp.where(lower, r0, r2),
        jnp.where(lower, r1, r3),
    )
    left = lax.broadcasted_iota(jnp.int32, (1, LANES), 1) < OWN_BC
    for pair in range(2):
        low, high = tails[2 * pair], tails[2 * pair + 1]
        first = 2 * INNER + pair * LANES
        grad_ref[:, first : first + LANES] = jnp.where(left, pltpu.roll(low, OWN_BC, 1), high)
    slot = lax.broadcasted_iota(jnp.int32, (LANES, HEADS), 0)
    head = lax.broadcasted_iota(jnp.int32, (LANES, HEADS), 1)
    d_dt = jnp.zeros((rows, HEADS), f32)
    for owner in range(PART):
        chosen = (slot < OWN_HEADS) & (head == slot // 2 * 2 * PART + 2 * owner + slot % 2)
        d_dt = d_dt + dot_nn(tails[owner].astype(bf16), jnp.where(chosen, 1.0, 0.0).astype(bf16))
    gdt_ref[...] = d_dt
    total = jnp.sum(wdt_ref[...].astype(f32) * d_dt, axis=1, keepdims=True)
    for strip in range(2 * STRIPS * PART + 2):
        at = slice(strip * LANES, (strip + 1) * LANES)
        total = total + jnp.sum(w_ref[:, at].astype(f32) * grad_ref[:, at], axis=1, keepdims=True)
    square = lax.broadcasted_iota(jnp.int32, (rows, rows), 0) == lax.broadcasted_iota(
        jnp.int32, (rows, rows), 1
    )
    flat = jnp.sum(jnp.where(square, total, 0.0), axis=0, keepdims=True)
    gnorm_ref[...] = flat / gain_ref[...].astype(f32)


def projection_rows(me, gates, convs, w_in, w_dt, norm_gain):
    rows = w_in.shape[0]
    whole = lambda *block: pl.BlockSpec(block, lambda i, me: (0,) * len(block))
    columns = w_in.shape[1]
    return pl.pallas_call(
        rows_kernel,
        grid_spec=pltpu.PrefetchScalarGridSpec(
            num_scalar_prefetch=1,
            grid=(1,),
            in_specs=[whole(rows, OWN)] * PART
            + [whole(rows, CONV_COLS)] * PART
            + [whole(rows, columns), whole(rows, HEADS), whole(1, rows)],
            out_specs=[whole(rows, columns), whole(rows, HEADS), whole(1, rows)],
        ),
        out_shape=[
            jax.ShapeDtypeStruct((rows, columns), f32),
            jax.ShapeDtypeStruct((rows, HEADS), f32),
            jax.ShapeDtypeStruct((1, rows), f32),
        ],
        compiler_params=pltpu.CompilerParams(vmem_limit_bytes=32 * 2**20),
        name="projection_rows",
    )(me, *gates, *convs, w_in, w_dt, norm_gain[None, :])


def per_device(
    hidden_in,
    widths,
    norm_gain,
    w_in,
    w_dt,
    conv_weight,
    dt_bias,
    a_log,
    skip_gain,
    gate_gain,
    w_out,
    grad_out,
):
    me = lax.axis_index("seq")
    tokens = hidden_in.shape[1]
    length = tokens * PART
    rows_in = w_in.shape[0]
    used_units = INNER // 8 * jnp.left_shift(jnp.int32(1), widths[0])
    units_float = used_units.astype(f32)
    block = jnp.arange(OWN) // LANES * PART + me
    unit_used = block * LANES < used_units
    head_used = ((jnp.arange(OWN_HEADS) // 2 * PART + me) * LANES < used_units).astype(f32)

    if fast_mesh():
        conv_pieces, gate_pieces = owners_pieces(w_in, w_dt, norm_gain, gate_gain)
    else:
        every = lambda a: jnp.broadcast_to(a[None], (PART,) + a.shape)
        tail = jnp.concatenate(
            [
                heads_by_owner(w_dt),
                every(norm_gain[:, None]),
                every(gate_gain.reshape(2, rows_in).T),
                jnp.zeros((PART, rows_in, LANES - OWN_HEADS - 3 - OWN_BC), bf16),
                w_in[:, 2 * INNER :].reshape(rows_in, PART, OWN_BC).transpose(1, 0, 2),
            ],
            axis=2,
        )
        conv_pieces = jnp.concatenate([by_owner(w_in[:, INNER : 2 * INNER]), tail], axis=2)
        gate_pieces = by_owner(w_in[:, :INNER])

    gather = gather_everything if fast_mesh() else gather_plainly
    w_conv, w_gate, w_o, x_pieces, (cot_a, cot_b) = gather(
        conv_pieces, gate_pieces, w_out, hidden_in[0], grad_out[0]
    )
    order = jnp.stack([me, me ^ 1, me ^ 2, me ^ 3]).astype(jnp.int32)
    gate_all = w_conv[:, OWN + OWN_HEADS + 1 : OWN + OWN_HEADS + 3]
    gate_all = gate_all.reshape(D // rows_in, rows_in, 2).transpose(0, 2, 1)
    gate_row = lax.dynamic_index_in_dim(gate_all.reshape(STRIPS, PART, LANES), me, 1, False)
    gate_row = gate_row.reshape(1, OWN).astype(f32)
    gain_row = w_conv[:, OWN + OWN_HEADS].astype(f32)[None, :]

    def own_heads(array):
        return lax.dynamic_index_in_dim(array.reshape(STRIPS, PART, 2), me, 1, False).reshape(-1)

    bias = own_heads(dt_bias)
    rate = -jnp.exp(own_heads(a_log))
    skip = own_heads(skip_gain)
    pad_heads = lambda a: jnp.pad(a, (0, LANES - OWN_HEADS))
    rows = jnp.stack(
        [pad_heads(bias), pad_heads(rate), pad_heads(head_used)] + [jnp.zeros((LANES,), f32)] * 5
    )
    skip_row = jnp.broadcast_to(jnp.repeat(skip, HEAD_DIM)[None, :], (8, OWN))
    taps = lax.dynamic_index_in_dim(
        conv_weight[:, :INNER].reshape(CONV, STRIPS, PART, LANES), me, 2, False
    ).reshape(CONV, OWN)
    taps = jnp.pad(taps.astype(f32), ((0, 8 - CONV), (0, 0)))
    taps_bc = lax.dynamic_slice_in_dim(conv_weight[:, INNER:], me * OWN_BC, OWN_BC, 1).astype(f32)
    taps_tile = jnp.pad(taps_bc, ((0, 8 - CONV), (LANES - OWN_BC, 0)))
    place_me = me.astype(jnp.int32).reshape(1)

    normed = all_positions(x_pieces, order, jnp.broadcast_to(gain_row, (8, D)))
    dt_tile = dot_nn(normed, w_conv[:, OWN:])
    bc = bc_forward(dt_tile, taps_tile)
    bc = [bc] + [xor_seq(bc, bits) for bits in range(1, PART)]
    conv_in = jnp.where(unit_used, dot_nn(normed, w_conv[:, :OWN]), 0.0).astype(bf16)
    if fast_mesh():
        w_o += [dp_swap_x(piece) for piece in w_o[1:4]]
    else:
        cot_a = xor_seq(cot_a, 2)
    cot_b, conv_in, *bc[1:] = tie(cot_b, conv_in, *bc[1:])
    cot_b = xor_seq(cot_b, 2)
    y, act, entry = recurrence_forward(place_me, conv_in, bc, dt_tile, taps, rows, skip_row)
    if fast_mesh():
        cot_b, *w_o[5:] = after([cot_b, *w_o[5:]], [entry])
        w_o = assemble(w_o, out_places(), 512)
    else:
        (cot_b,) = after([cot_b], [entry])
    cot_pieces = (
        grad_out[0], xor_seq(grad_out[0], 1), cot_a, cot_b, xor_seq(cot_a, 1), xor_seq(cot_b, 1)
    )
    cot_all, d_rounded = pull_out(cot_pieces, order, w_o)
    row = jnp.concatenate(
        [
            gate_row,
            unit_used.astype(f32)[None, :],
            jnp.full((6, OWN), units_float),
        ],
        axis=0,
    )
    z, sums = gate_forward(normed, y, d_rounded, w_gate, row)
    rounded_out, d_y, d_z, grad_gate_rows = gate_backward(y, z, d_rounded, seq_total(sums), row)
    grad_gate_local = grad_gate_rows[0]

    if fast_mesh():
        both = products(normed, d_z, rounded_out, cot_all)
        d_y, both = tie(d_y, both)
        both_total = dp_sum(both.reshape(-1, OWN))

    d_values, d_bc, d_dt, g_conv, g_rows = recurrence_backward(
        place_me, conv_in, act, d_y, y, bc, dt_tile, entry, taps, rows, skip_row
    )
    if fast_mesh():
        d_values, d_bc, rounded_out = tie(d_values, d_bc, rounded_out)
    branch = dot_nn(rounded_out, w_o).astype(bf16).reshape(PART, tokens, D)
    branch_mine, branch_got = core_halves(branch)
    d_bc_mine, d_bc_got = seq_scatter_relative(d_bc)
    branch_keep, branch_give = halves_sum(branch_mine, branch_got)
    d_bc_got, branch_give = tie(d_bc_got, branch_give)
    d_project, g_tail = tail_backward(
        dt_tile, d_bc_mine + d_bc_got.astype(f32), d_dt, taps_tile, d_values
    )
    g_skip = jnp.sum(g_conv[4].reshape(OWN_HEADS, HEAD_DIM), axis=1)
    small = jnp.concatenate(
        [
            g_conv[:CONV].reshape(-1),
            g_tail[:CONV, LANES - OWN_BC :].reshape(-1),
            pad_heads(g_rows[0, :OWN_HEADS]),
            pad_heads(g_rows[1, :OWN_HEADS]),
            pad_heads(g_skip),
            grad_gate_local,
        ]
    )
    count = small.shape[0]
    padded = -(-count // (8 * LANES)) * 8 * LANES
    small = jnp.pad(small, (0, padded - count)).reshape(-1, LANES)
    if fast_mesh():
        conv_product = dot_tn(normed, d_project).astype(bf16)
        d_project, conv_product = tie(d_project, conv_product)
        (conv_product,) = after([conv_product], [both_total])
        conv_total = dp_sum(conv_product)
    branch_across = xor_seq(branch_give, 2)
    d_normed = input_gradient(d_z, d_project, w_gate, w_conv)
    if fast_mesh():
        branch_across, d_normed = tie(branch_across, d_normed)
    mine, got = core_halves(d_normed.reshape(PART, tokens, D))
    keep, give = halves_sum(mine, got)
    small, give = tie(small, give)
    across = xor_seq(give, 2)
    small, across = tie(dp_total(small), across)
    d_own = keep + across.astype(f32)
    if fast_mesh():
        both_total = after([both_total], [across])[0]
        small_pieces = seq_pieces(small)
        gate_rows, out_left, out_right = jnp.split(both_total, [rows_in * PART, rows_in * PART + LANES])
        grad_w_out = jnp.concatenate([out_left, out_right], axis=1).astype(f32)
        gate_rows = owners_rows(gate_rows)
        (conv_total,) = after([conv_total], [small_pieces[3], *gate_rows[1:]])
        grad_w_in, grad_w_dt, grad_norm_gain = projection_rows(
            place_me, gate_rows, owners_rows(conv_total), w_in, w_dt, norm_gain
        )
        grad_norm_gain = grad_norm_gain[0]
    else:
        small_pieces = seq_pieces(small)
        grad_w_out = scatter_out(dot_tn(rounded_out, cot_all).astype(bf16))
        grad_gate_in = scatter_in(dot_tn(normed, d_z).astype(bf16))
        grad_conv_in = scatter_in(dot_tn(normed, d_project).astype(bf16))
        grad_w_in = jnp.concatenate(
            [
                from_owner(grad_gate_in),
                from_owner(grad_conv_in[:, :, :OWN]),
                grad_conv_in[:, :, CONV_COLS - OWN_BC :].transpose(1, 0, 2).reshape(rows_in, 2 * STATE),
            ],
            axis=1,
        )
        grad_w_dt = heads_from_owner(grad_conv_in[:, :, OWN : OWN + OWN_HEADS])
        grad_norm_gain = (
            jnp.sum(w_in.astype(f32) * grad_w_in, axis=1)
            + jnp.sum(w_dt.astype(f32) * grad_w_dt, axis=1)
        ) / norm_gain.astype(f32)
    x_own = hidden_in[0].astype(f32)
    hidden_out = (x_own + branch_keep + branch_across.astype(f32)).astype(bf16)[None]
    own_rms = lax.rsqrt(jnp.mean(x_own * x_own, axis=1, keepdims=True) + epsilon)
    d_scaled = d_own * gain_row
    d_input = own_rms * d_scaled - x_own * own_rms**3 * jnp.mean(
        d_scaled * x_own, axis=1, keepdims=True
    )
    grad_in = (grad_out[0].astype(f32) + d_input).astype(bf16)[None]

    every = jnp.stack(by_partner(small_pieces)).reshape(PART, padded)
    start = 0

    def take(size):
        nonlocal start
        start += size
        return every[:, start - size : start]

    all_conv = take(CONV * OWN).reshape(PART, CONV, OWN)
    all_conv_bc = take(CONV * OWN_BC).reshape(PART, CONV, OWN_BC)
    head_sums = [heads_from_owner(take(LANES)[:, None, :OWN_HEADS]).reshape(HEADS) for _ in range(3)]
    grad_gate = lax.dynamic_index_in_dim(take(OWN), me, 0, False)
    grad_conv = jnp.concatenate(
        [from_owner(all_conv), all_conv_bc.transpose(1, 0, 2).reshape(CONV, 2 * STATE)], axis=1
    )
    place = lax.axis_index(("dp", "seq"))
    gain_rows = gate_gain.shape[0]
    if gain_rows == LANES:
        grad_gate_gain = lax.dynamic_slice_in_dim(
            grad_gate, lax.axis_index("dp") * gain_rows, gain_rows, 0
        )
    else:
        start = CONV * OWN + CONV * OWN_BC + 3 * LANES
        whole_gate = from_owner(take(OWN)[:, None, :]).reshape(INNER)
        grad_gate_gain = lax.dynamic_slice_in_dim(whole_gate, place * gain_rows, gain_rows, 0)

    return (
        hidden_out,
        grad_in,
        grad_norm_gain,
        grad_w_in,
        grad_w_dt,
        grad_conv,
        head_sums[0],
        head_sums[1],
        head_sums[2],
        grad_gate_gain,
        grad_w_out,
    )


def solution(mesh):
    return jax.shard_map(
        per_device,
        mesh=mesh,
        in_specs=(
            P("dp", "seq", None),
            P("dp"),
            P(("dp", "seq")),
            P(("dp", "seq"), None),
            P(("dp", "seq"), None),
            P(),
            P(),
            P(),
            P(),
            P(("dp", "seq")),
            P(("dp", "seq"), None),
            P("dp", "seq", None),
        ),
        out_specs=(
            P("dp", "seq", None),
            P("dp", "seq", None),
            P(("dp", "seq")),
            P(("dp", "seq"), None),
            P(("dp", "seq"), None),
            P(),
            P(),
            P(),
            P(),
            P(("dp", "seq")),
            P(("dp", "seq"), None),
        ),
        check_vma=False,
    )
```

```python
import functools

import jax
import jax.numpy as jnp
from jax import lax
from jax.experimental import pallas as pl
from jax.experimental.pallas import tpu as pltpu
from jax.sharding import PartitionSpec as P

D = 2048
INNER = 4096
HEAD_DIM = 64
STATE = 128
CONV = 4
HEADS = 64
CHANNELS = 4352

PART = 4
LANES = 128
STRIPS = INNER // LANES // PART
OWN = STRIPS * LANES
OWN_HEADS = OWN // HEAD_DIM
OWN_BC = 2 * STATE // PART
CONV_COLS = OWN + LANES
Q = 256
HALF = Q // 2
WIDE = 512

epsilon = 1e-05
highest = lax.Precision.HIGHEST
f32 = jnp.float32
bf16 = jnp.bfloat16
LOG2E = 1.4426950408889634


def swap(value, axis, pairs):
    return lax.ppermute(value, axis, pairs)


def xor_seq(value, bits):
    return lax.ppermute(value, "seq", [(s, s ^ bits) for s in range(PART)])


def core_halves(blocks):
    core = lax.axis_index("seq") % 2
    view = blocks.reshape((2, 2) + blocks.shape[1:])
    mine = lax.dynamic_index_in_dim(view, core, 1, False)
    other = lax.dynamic_index_in_dim(view, 1 - core, 1, False)
    return mine, xor_seq(other, 1)


def halves_sum(mine, received):
    row = lax.axis_index("seq") // 2

    def of(which):
        a = lax.dynamic_index_in_dim(mine, which, 0, False)
        return a.astype(f32) + lax.dynamic_index_in_dim(received, which, 0, False).astype(f32)

    return of(row), of(1 - row).astype(bf16)


def seq_scatter_relative(blocks):
    view = blocks.reshape((2, 2) + blocks.shape[1:])
    half = view[:, 0].astype(f32) + xor_seq(view[:, 1], 1).astype(f32)
    return half[0], xor_seq(half[1].astype(bf16), 2)


def by_partner(pieces):
    me = lax.axis_index("seq")
    odd, lower = me % 2 == 1, me >= 2
    a, b, c, d = pieces
    a, b = jnp.where(odd, b, a), jnp.where(odd, a, b)
    c, d = jnp.where(odd, d, c), jnp.where(odd, c, d)
    return (
        jnp.where(lower, c, a),
        jnp.where(lower, d, b),
        jnp.where(lower, a, c),
        jnp.where(lower, b, d),
    )


def seq_exchange(pieces):
    turned = by_partner([pieces[k] for k in range(PART)])
    return [turned[0]] + [xor_seq(turned[k], k) for k in range(1, PART)]


def seq_total(value):
    return value + xor_seq(value, 1) + xor_seq(value, 2) + xor_seq(value, 3)


def fast_mesh():
    return lax.axis_size("dp") == 8


def dp_shift_z(value, steps):
    pairs = [(z * 2 + x, (z + steps) % 4 * 2 + x) for z in range(4) for x in range(2)]
    return lax.ppermute(value, "dp", pairs)


def dp_swap_x(value):
    return lax.ppermute(value, "dp", [(d, d ^ 1) for d in range(8)])


def tie_kernel(*refs):
    del refs


def tie(*values):
    anywhere = pl.BlockSpec(memory_space=pl.ANY)
    return pl.pallas_call(
        tie_kernel,
        in_specs=[anywhere] * len(values),
        out_specs=[anywhere] * len(values),
        out_shape=[jax.ShapeDtypeStruct(v.shape, v.dtype) for v in values],
        input_output_aliases={k: k for k in range(len(values))},
        name="tie",
    )(*values)


def after(values, needed):
    anywhere = pl.BlockSpec(memory_space=pl.ANY)
    return pl.pallas_call(
        tie_kernel,
        in_specs=[anywhere] * (len(values) + len(needed)),
        out_specs=[anywhere] * len(values),
        out_shape=[jax.ShapeDtypeStruct(v.shape, v.dtype) for v in values],
        input_output_aliases={k: k for k in range(len(values))},
        name="after",
    )(*values, *needed)


def assemble_kernel(places_ref, *refs):
    rows = refs[0].shape[0]
    for k, piece in enumerate(refs[:-1]):
        refs[-1][pl.ds(pl.multiple_of(places_ref[k] * rows, rows), rows), :] = piece[...]


def assemble(pieces, places, tile):
    rows, columns = pieces[0].shape
    count = len(pieces)
    along = lambda i, places: (0, i)
    return pl.pallas_call(
        assemble_kernel,
        grid_spec=pltpu.PrefetchScalarGridSpec(
            num_scalar_prefetch=1,
            grid=(columns // tile,),
            in_specs=[pl.BlockSpec((rows, tile), along)] * count,
            out_specs=pl.BlockSpec((rows * count, tile), along),
        ),
        out_shape=jax.ShapeDtypeStruct((rows * count, columns), pieces[0].dtype),
        compiler_params=pltpu.CompilerParams(vmem_limit_bytes=60 * 2**20),
        cost_estimate=pl.CostEstimate(
            flops=0, bytes_accessed=4 * rows * count * columns, transcendentals=0
        ),
        name="assemble",
    )(places, *pieces)


def pieces_kernel(w_ref, dt_ref, norm_ref, gate_ref, conv_ref, gates_ref):
    rows = w_ref.shape[0]
    lane = lax.broadcasted_iota(jnp.int32, (1, LANES), 1)
    square = lax.broadcasted_iota(jnp.int32, (rows, rows), 0) == lax.broadcasted_iota(
        jnp.int32, (rows, rows), 1
    )

    def column(values):
        return jnp.sum(jnp.where(square, values, 0.0), axis=1, keepdims=True)

    gain = column(norm_ref[0:1, :].astype(f32))
    gates = [column(gate_ref[k : k + 1, :].astype(f32)) for k in range(2)]
    head = lax.broadcasted_iota(jnp.int32, (HEADS, LANES), 0)
    slot = lax.broadcasted_iota(jnp.int32, (HEADS, LANES), 1)
    for owner in range(PART):
        for strip in range(STRIPS):
            source = (strip * PART + owner) * LANES
            at = slice(strip * LANES, (strip + 1) * LANES)
            gates_ref[owner, :, at] = w_ref[:, source : source + LANES]
            conv_ref[owner, :, at] = w_ref[:, INNER + source : INNER + source + LANES]
        chosen = (slot < OWN_HEADS) & (head == slot // 2 * 2 * PART + 2 * owner + slot % 2)
        steps = dot_nn(dt_ref[...], jnp.where(chosen, 1.0, 0.0).astype(bf16))
        first = 2 * INNER + owner // 2 * LANES
        tile = w_ref[:, first : first + LANES].astype(f32)
        if owner % 2 == 0:
            tile = pltpu.roll(tile, OWN_BC, 1)
        tail = jnp.where(lane < OWN_HEADS, steps, jnp.where(lane == OWN_HEADS, gain, 0.0))
        for k in range(2):
            tail = jnp.where(lane == OWN_HEADS + 1 + k, gates[k], tail)
        tail = jnp.where(lane >= LANES - OWN_BC, tile, tail)
        conv_ref[owner, :, OWN:] = tail.astype(bf16)


def owners_pieces(w_in, w_dt, norm_gain, gate_gain):
    rows = w_in.shape[0]
    whole = lambda *block: pl.BlockSpec(block, lambda i: (0,) * len(block))

    return pl.pallas_call(
        pieces_kernel,
        grid=(1,),
        in_specs=[whole(rows, 2 * INNER + 2 * STATE), whole(rows, HEADS), whole(1, rows), whole(2, rows)],
        out_specs=[whole(PART, rows, CONV_COLS), whole(PART, rows, OWN)],
        out_shape=[
            jax.ShapeDtypeStruct((PART, rows, CONV_COLS), bf16),
            jax.ShapeDtypeStruct((PART, rows, OWN), bf16),
        ],
        compiler_params=pltpu.CompilerParams(vmem_limit_bytes=32 * 2**20),
        name="owners_pieces",
    )(w_in, w_dt, norm_gain[None, :], gate_gain.reshape(2, rows))


def seq_pass(pieces, *beside):
    me = lax.axis_index("seq")
    core, row = me % 2, me // 2
    view = pieces.reshape((2, 2) + pieces.shape[1:])
    give = lax.dynamic_index_in_dim(view, 1 - row, 0, False)
    keep = lax.dynamic_index_in_dim(view, row, 0, False)
    got, *beside = tie(xor_seq(give, 2), *beside)
    lower = jnp.where(row == 0, keep, got)
    upper = jnp.where(row == 0, got, keep)
    both = jnp.stack([lower, upper])
    mine = lax.dynamic_index_in_dim(both, core, 1, False)
    other = xor_seq(lax.dynamic_index_in_dim(both, 1 - core, 1, False), 1)
    first = jnp.where(core == 0, mine, other)
    second = jnp.where(core == 0, other, mine)
    return jnp.stack([first, second], axis=1).reshape((-1,) + pieces.shape[2:]), beside


def seq_pieces(block, after=None):
    source = block if after is None else tie(block, after)[0]
    across = xor_seq(source, 2)
    return block, xor_seq(block, 1), across, xor_seq(across, 1)


def gather_everything(conv_pieces, gate_pieces, o, x_block, cot_block):
    c, (o1,) = seq_pass(conv_pieces, dp_shift_z(o, 1))
    w_conv = lax.all_gather(c, "dp", axis=0, tiled=True)
    x_across, gate_pieces, o2, o3, o_x = tie(
        xor_seq(after([x_block], [c])[0], 2),
        gate_pieces,
        dp_shift_z(o, 2),
        dp_shift_z(o, 3),
        dp_swap_x(o),
    )
    g, _ = seq_pass(gate_pieces)
    half = cot_block.shape[0] // 2
    cot_a, cot_b = after([cot_block[:half], cot_block[half:]], [g])
    g, x_across, cot_a = after([g, x_across, xor_seq(cot_a, 2)], [w_conv])
    x_pieces = (x_block, xor_seq(x_block, 1), x_across, xor_seq(x_across, 1))
    w_gate = lax.all_gather(g, "dp", axis=0, tiled=True)
    return w_conv, w_gate, [o, o1, o2, o3, o_x], x_pieces, (cot_a, cot_b)


def out_places():
    dp = lax.axis_index("dp")
    sources = (dp // 2 - jnp.arange(4, dtype=jnp.int32) + 4) % 4 * 2
    return jnp.concatenate([sources + dp % 2, sources + 1 - dp % 2]).astype(jnp.int32)


def norm_rows(x, gain):
    x = x.astype(f32)
    inverse = lax.rsqrt(jnp.mean(x * x, axis=1, keepdims=True) + epsilon)
    return (x * inverse * gain).astype(bf16)


def positions_kernel(shares, with_norm, order_ref, *refs):
    step = pl.program_id(0)
    first = 0
    for k, share in enumerate(shares):

        @pl.when((step >= first) & (step < first + share))
        def _():
            if with_norm:
                refs[-1][...] = norm_rows(refs[k][...], refs[-2][0:1, :])
            else:
                refs[-1][...] = refs[k][...]

        first += share


def all_positions(pieces, order, gain_rows=None):
    tile = min(256, min(p.shape[0] for p in pieces))
    shares = [p.shape[0] // tile for p in pieces]
    steps = sum(shares)
    each = steps // PART

    def place(first, share):
        return lambda i, order: (jnp.clip(i - first, 0, share - 1), 0)

    specs, first = [], 0
    for share in shares:
        specs.append(pl.BlockSpec((tile, D), place(first, share)))
        first += share
    extra = []
    if gain_rows is not None:
        specs.append(pl.BlockSpec((8, D), lambda i, order: (0, 0)))
        extra.append(gain_rows)
    return pl.pallas_call(
        functools.partial(positions_kernel, shares, gain_rows is not None),
        grid_spec=pltpu.PrefetchScalarGridSpec(
            num_scalar_prefetch=1,
            grid=(steps,),
            in_specs=specs,
            out_specs=pl.BlockSpec((tile, D), lambda i, order: (order[i // each] * each + i % each, 0)),
        ),
        out_shape=jax.ShapeDtypeStruct((tile * steps, D), bf16),
        compiler_params=pltpu.CompilerParams(vmem_limit_bytes=32 * 2**20),
        cost_estimate=pl.CostEstimate(
            flops=4 * tile * steps * D, bytes_accessed=4 * tile * steps * D, transcendentals=0
        ),
        name="all_positions",
    )(order, *pieces, *extra)


def dp_total(value):
    if not fast_mesh():
        return lax.psum(value, "dp")
    value = value + dp_swap_x(value)
    return value + dp_shift_z(value, 1) + dp_shift_z(value, 2) + dp_shift_z(value, 3)


def by_owner(columns):
    rows = columns.shape[0]
    return (
        columns.reshape(rows, STRIPS, PART, LANES).transpose(2, 0, 1, 3).reshape(PART, rows, OWN)
    )


def from_owner(pieces):
    rows = pieces.shape[1]
    return (
        pieces.reshape(PART, rows, STRIPS, LANES).transpose(1, 2, 0, 3).reshape(rows, INNER)
    )


def heads_by_owner(columns):
    rows = columns.shape[0]
    return (
        columns.reshape(rows, STRIPS, PART, 2).transpose(2, 0, 1, 3).reshape(PART, rows, OWN_HEADS)
    )


def heads_from_owner(pieces):
    rows = pieces.shape[1]
    return (
        pieces.reshape(PART, rows, STRIPS, 2).transpose(1, 2, 0, 3).reshape(rows, HEADS)
    )


def gather_in(pieces):
    full = lax.all_gather(pieces, ("dp", "seq"), axis=1, tiled=True)
    return lax.dynamic_index_in_dim(full, lax.axis_index("seq"), 0, False)


def dp_sum(product):
    return lax.psum_scatter(product, "dp", scatter_dimension=0, tiled=True)


def owners_rows(total):
    return seq_exchange(total.reshape(PART, -1, total.shape[1]))


def scatter_in(grads):
    full = jnp.zeros((PART,) + grads.shape, grads.dtype)
    full = lax.dynamic_update_index_in_dim(full, grads, lax.axis_index("seq"), 0)
    return lax.psum_scatter(full, ("dp", "seq"), scatter_dimension=1, tiled=True).astype(f32)


def gather_out(rows):
    full = lax.all_gather(rows, ("dp", "seq"), axis=0, tiled=True)
    full = full.reshape(STRIPS, PART, LANES, -1)
    return lax.dynamic_index_in_dim(full, lax.axis_index("seq"), 1, False).reshape(OWN, -1)


def gather_plainly(conv_pieces, gate_pieces, out_rows, x_block, cot_block):
    return (
        gather_in(conv_pieces),
        gather_in(gate_pieces),
        gather_out(out_rows),
        seq_pieces(x_block),
        jnp.split(cot_block, 2),
    )


def scatter_out(grads):
    full = jnp.zeros((STRIPS, PART, LANES, grads.shape[1]), grads.dtype)
    full = lax.dynamic_update_index_in_dim(
        full, grads.reshape(STRIPS, LANES, -1), lax.axis_index("seq"), 1
    )
    full = full.reshape(INNER, -1)
    return lax.psum_scatter(full, ("dp", "seq"), scatter_dimension=0, tiled=True).astype(f32)


def dot_nn(a, b):
    return lax.dot_general(a, b, (((1,), (0,)), ((), ())), preferred_element_type=f32)


def dot_nt(a, b):
    return lax.dot_general(a, b, (((1,), (1,)), ((), ())), preferred_element_type=f32)


def dot_tn(a, b):
    return lax.dot_general(a, b, (((0,), (0,)), ((), ())), preferred_element_type=f32)


def dot_exact(a, b):
    return lax.dot_general(
        a, b, (((1,), (0,)), ((), ())), precision=highest, preferred_element_type=f32
    )


def sigmoid(v):
    return 0.5 + 0.5 * jnp.tanh(0.5 * v)


def bc_forward_kernel(tile_ref, taps_ref, out_ref, padded):
    length = tile_ref.shape[0]
    padded[0:8, :] = jnp.zeros((8, LANES), f32)
    padded[8 : 8 + length, :] = tile_ref[...].astype(bf16).astype(f32)
    left = lax.broadcasted_iota(jnp.int32, (1, LANES), 1) < OWN_BC
    for block in range(length // Q):
        start = block * Q
        pre = taps_ref[0:1, :] * padded[start + 5 : start + 5 + Q, :]
        for tap in range(1, CONV):
            pre = pre + taps_ref[tap : tap + 1, :] * padded[start + 5 + tap : start + 5 + tap + Q, :]
        act = pre * sigmoid(pre)
        packed = jnp.where(left, pltpu.roll(act[HALF:], OWN_BC, 1), act[:HALF])
        out_ref[block * HALF : (block + 1) * HALF, :] = packed.astype(bf16)


def bc_forward(dt_tile, taps_tile):
    length = dt_tile.shape[0]
    return pl.pallas_call(
        bc_forward_kernel,
        out_shape=jax.ShapeDtypeStruct((length // 2, LANES), bf16),
        scratch_shapes=[pltpu.VMEM((8 + length, LANES), f32)],
        compiler_params=pltpu.CompilerParams(vmem_limit_bytes=16 * 2**20),
        cost_estimate=pl.CostEstimate(
            flops=20 * length * LANES, bytes_accessed=5 * length * LANES, transcendentals=0
        ),
        name="bc_forward",
    )(dt_tile, taps_tile)


def tail_kernel(tile_ref, grad_ref, ddt_ref, taps_ref, into_ref, out_ref, sums_ref, padded, dp):
    del into_ref
    length = tile_ref.shape[0]
    padded[0:8, :] = jnp.zeros((8, LANES), f32)
    padded[8 : 8 + length, :] = tile_ref[...].astype(bf16).astype(f32)
    dp[length : length + 8, :] = jnp.zeros((8, LANES), f32)
    lane = lax.broadcasted_iota(jnp.int32, (1, LANES), 1)
    left = lane < OWN_BC
    sums_ref[...] = jnp.zeros_like(sums_ref)
    for block in reversed(range(length // Q)):
        start = block * Q
        taken = [padded[start + 5 + tap : start + 5 + tap + Q, :] for tap in range(CONV)]
        pre = taps_ref[0:1, :] * taken[0]
        for tap in range(1, CONV):
            pre = pre + taps_ref[tap : tap + 1, :] * taken[tap]
        packed = grad_ref[block * HALF : (block + 1) * HALF, :]
        grad = jnp.concatenate([packed, pltpu.roll(packed, OWN_BC, 1)], axis=0)
        squashed = sigmoid(pre)
        d_pre = jnp.where(left, 0.0, grad * squashed * (1.0 + pre * (1.0 - squashed)))
        dp[start : start + Q, :] = d_pre
        for tap in range(CONV):
            sums_ref[tap : tap + 1, :] += jnp.sum(d_pre * taken[tap], axis=0, keepdims=True)
        d_in = taps_ref[CONV - 1 : CONV, :] * d_pre
        for tap in range(CONV - 1):
            first = start + CONV - 1 - tap
            d_in = d_in + taps_ref[tap : tap + 1, :] * dp[first : first + Q, :]
        d_dt = jnp.where(lane < OWN_HEADS, ddt_ref[start : start + Q, :], 0.0)
        out_ref[start : start + Q, :] = jnp.where(left, d_dt, d_in).astype(bf16)


def tail_backward(dt_tile, grad, d_dt, taps_tile, into):
    length = dt_tile.shape[0]
    whole = lambda i: (0, 0)
    return pl.pallas_call(
        tail_kernel,
        grid=(1,),
        in_specs=[
            pl.BlockSpec((length, LANES), whole),
            pl.BlockSpec((length // 2, LANES), whole),
            pl.BlockSpec((length, LANES), whole),
            pl.BlockSpec((8, LANES), whole),
            pl.BlockSpec(memory_space=pl.ANY),
        ],
        out_specs=[
            pl.BlockSpec((length, LANES), lambda i: (0, STRIPS)),
            pl.BlockSpec((8, LANES), whole),
        ],
        out_shape=[
            jax.ShapeDtypeStruct(into.shape, bf16),
            jax.ShapeDtypeStruct((8, LANES), f32),
        ],
        input_output_aliases={4: 0},
        scratch_shapes=[pltpu.VMEM((8 + length, LANES), f32), pltpu.VMEM((8 + length, LANES), f32)],
        compiler_params=pltpu.CompilerParams(vmem_limit_bytes=60 * 2**20),
        cost_estimate=pl.CostEstimate(
            flops=40 * length * LANES, bytes_accessed=14 * length * LANES, transcendentals=0
        ),
        name="tail_backward",
    )(dt_tile, grad, d_dt, taps_tile, into)


def keys_and_reads(me, refs):
    odd, lower = me % 2 == 1, me >= 2
    p = [ref[...].astype(f32) for ref in refs]
    r0, r1 = jnp.where(odd, p[1], p[0]), jnp.where(odd, p[0], p[1])
    r2, r3 = jnp.where(odd, p[3], p[2]), jnp.where(odd, p[2], p[3])
    q = (
        jnp.where(lower, r2, r0),
        jnp.where(lower, r3, r1),
        jnp.where(lower, r0, r2),
        jnp.where(lower, r1, r3),
    )
    left = lax.broadcasted_iota(jnp.int32, (1, LANES), 1) < OWN_BC

    def join(a, b):
        top = jnp.where(left, pltpu.roll(a, OWN_BC, 1), b)
        bottom = jnp.where(left, a, pltpu.roll(b, OWN_BC, 1))
        return jnp.concatenate([top, bottom], axis=0).astype(bf16)

    return join(q[0], q[1]), join(q[2], q[3])


def give_back(me, d_keys, d_reads, out_ref):
    left = lax.broadcasted_iota(jnp.int32, (1, LANES), 1) < OWN_BC
    for pair, array in enumerate((d_keys, d_reads)):
        top, bottom = array[:HALF], array[HALF:]
        low = jnp.where(left, bottom, pltpu.roll(top, OWN_BC, 1))
        high = jnp.where(left, pltpu.roll(bottom, OWN_BC, 1), top)
        out_ref[jnp.bitwise_xor(me, 2 * pair)] = low.astype(bf16)
        out_ref[jnp.bitwise_xor(me, 2 * pair + 1)] = high.astype(bf16)


def decay_terms(dt_ref, rows_ref):
    v = dt_ref[...] * rows_ref[2:3, :] + rows_ref[0:1, :]
    steps = jnp.maximum(v, 0.0) + jnp.log1p(jnp.exp(-jnp.abs(v)))
    log2_decay = rows_ref[1:2, :] * LOG2E * steps
    row = lax.broadcasted_iota(jnp.int32, (Q, Q), 0)
    column = lax.broadcasted_iota(jnp.int32, (Q, Q), 1)
    lower = jnp.where(row >= column, 1.0, 0.0)
    running = dot_exact(lower, log2_decay)
    shifted = running - jnp.log(steps) * LOG2E
    end = running[Q - 1 : Q, :]
    return v, steps, running, shifted, end


def spread_heads(values, spread):
    high = values.astype(bf16)
    low = (values - high.astype(f32)).astype(bf16)
    return dot_nn(high, spread) + dot_nn(low, spread)


def forward_kernel(
    me_ref, ci_ref, b0, b1, b2, b3, dt_ref, cw_ref, rows_ref, skip_ref, y_ref, act_ref, s_ref, state, xf,
    e_wide, w_wide
):
    @pl.when(pl.program_id(0) == 0)
    def _():
        state[...] = jnp.zeros_like(state)
        xf[0:8, :] = jnp.zeros((8, OWN), f32)

    @pl.when(pl.program_id(0) > 0)
    def _():
        xf[0:8, :] = xf[Q : Q + 8, :]

    xf[8 : Q + 8, :] = ci_ref[...].astype(f32)
    _, _, running, shifted, end = decay_terms(dt_ref, rows_ref)
    shifted_t = shifted.T
    e_run = jnp.exp2(running)
    w_end = jnp.exp2(end - shifted)
    e_end = jnp.exp2(end)
    keys, reads = keys_and_reads(me_ref[0], (b0, b1, b2, b3))
    keys_t = keys.T
    cb = dot_nt(reads, keys)
    causal = lax.broadcasted_iota(jnp.int32, (HALF, HALF), 0) >= lax.broadcasted_iota(
        jnp.int32, (HALF, HALF), 1
    )
    left = lax.broadcasted_iota(jnp.int32, (1, LANES), 1) < HEAD_DIM
    spread = lax.broadcasted_iota(jnp.int32, (LANES, OWN), 0) == (
        lax.broadcasted_iota(jnp.int32, (LANES, OWN), 1) // HEAD_DIM
    )
    spread = jnp.where(spread, 1.0, 0.0).astype(bf16)
    e_wide[...] = spread_heads(e_run, spread)
    w_wide[...] = spread_heads(w_end, spread)
    s_ref[0] = state[...].astype(bf16)
    for strip in range(STRIPS):
        at = slice(strip * LANES, (strip + 1) * LANES)
        h0, h1 = 2 * strip, 2 * strip + 1
        pre = cw_ref[0:1, at] * xf[5 : 5 + Q, at]
        for tap in range(1, CONV):
            pre = pre + cw_ref[tap : tap + 1, at] * xf[5 + tap : 5 + tap + Q, at]
        act = (pre * sigmoid(pre)).astype(bf16)
        act_ref[:, at] = act
        actf = act.astype(f32)
        inter = dot_nn(reads, s_ref[0, :, at]) * e_wide[:, at]
        inter = inter + skip_ref[0:1, at] * actf
        top, bottom = inter[:HALF], inter[HALF:]
        for h, side in ((h0, left), (h1, jnp.logical_not(left))):
            x_h = jnp.where(side, act, jnp.zeros_like(act))
            m00 = jnp.where(
                causal,
                jnp.exp2(running[:HALF, h : h + 1] - shifted_t[h : h + 1, :HALF]) * cb[:HALF, :HALF],
                0.0,
            )
            m10 = jnp.exp2(running[HALF:, h : h + 1] - shifted_t[h : h + 1, :HALF]) * cb[HALF:, :HALF]
            m11 = jnp.where(
                causal,
                jnp.exp2(running[HALF:, h : h + 1] - shifted_t[h : h + 1, HALF:]) * cb[HALF:, HALF:],
                0.0,
            )
            top = top + dot_nn(m00.astype(bf16), x_h[:HALF])
            bottom = bottom + dot_nn(
                jnp.concatenate([m10.astype(bf16), m11.astype(bf16)], axis=1), x_h
            )
        y_ref[:HALF, at] = top
        y_ref[HALF:, at] = bottom
        weighted = (actf * w_wide[:, at]).astype(bf16)
        state[:, at] = state[:, at] * jnp.where(
            left, e_end[:, h0 : h0 + 1], e_end[:, h1 : h1 + 1]
        ) + dot_nn(keys_t, weighted)


def recurrence_forward(me, conv_in, bc, dt_tile, taps, rows, skip_row):
    length = conv_in.shape[0]
    blocks = length // Q
    whole = lambda i, me: (0, 0)
    along = lambda i, me: (i, 0)
    return pl.pallas_call(
        forward_kernel,
        grid_spec=pltpu.PrefetchScalarGridSpec(
            num_scalar_prefetch=1,
            grid=(blocks,),
            in_specs=[pl.BlockSpec((Q, OWN), along)]
            + [pl.BlockSpec((HALF, LANES), along)] * PART
            + [
                pl.BlockSpec((Q, LANES), along),
                pl.BlockSpec((8, OWN), whole),
                pl.BlockSpec((8, LANES), whole),
                pl.BlockSpec((8, OWN), whole),
            ],
            out_specs=[
                pl.BlockSpec((Q, OWN), along),
                pl.BlockSpec((Q, OWN), along),
                pl.BlockSpec((1, STATE, OWN), lambda i, me: (i, 0, 0)),
            ],
            scratch_shapes=[
                pltpu.VMEM((STATE, OWN), f32),
                pltpu.VMEM((Q + 8, OWN), f32),
                pltpu.VMEM((Q, OWN), f32),
                pltpu.VMEM((Q, OWN), f32),
            ],
        ),
        out_shape=[
            jax.ShapeDtypeStruct((length, OWN), f32),
            jax.ShapeDtypeStruct((length, OWN), bf16),
            jax.ShapeDtypeStruct((blocks, STATE, OWN), bf16),
        ],
        compiler_params=pltpu.CompilerParams(
            dimension_semantics=("arbitrary",), vmem_limit_bytes=60 * 2**20
        ),
        cost_estimate=pl.CostEstimate(
            flops=40 * 10**9, bytes_accessed=2**24, transcendentals=10**7
        ),
        name="recurrence_forward",
    )(me, conv_in, *bc, dt_tile, taps, rows, skip_row)


def backward_kernel(
    me_ref,
    ci_ref,
    prev_ref,
    act_ref,
    dy_ref,
    y_ref,
    b0,
    b1,
    b2,
    b3,
    dt_ref,
    s_ref,
    cw_ref,
    rows_ref,
    skip_ref,
    dci_ref,
    dbc_ref,
    ddt_ref,
    gconv_ref,
    grow_ref,
    back,
    back16,
    dp,
    xf,
    edy,
    wx,
    dcb,
    p12h,
    p12l,
    p3,
    p23,
    cross,
):
    step = pl.program_id(0)
    last = pl.num_programs(0) - 1

    @pl.when(step == 0)
    def _():
        back[...] = jnp.zeros_like(back)
        dp[Q : Q + 8, :] = jnp.zeros((8, OWN), f32)
        gconv_ref[...] = jnp.zeros_like(gconv_ref)
        grow_ref[...] = jnp.zeros_like(grow_ref)
        cross[...] = jnp.zeros_like(cross)

    @pl.when(step > 0)
    def _():
        dp[Q : Q + 8, :] = dp[0:8, :]

    before = prev_ref[8:16, :].astype(f32)
    xf[0:8, :] = jnp.where(step == last, 0.0, before)
    xf[8 : Q + 8, :] = ci_ref[...].astype(f32)
    v, steps, running, shifted, end = decay_terms(dt_ref, rows_ref)
    running_t = running.T
    e_run = jnp.exp2(running)
    w_end = jnp.exp2(end - shifted)
    e_end = jnp.exp2(end)
    keys, reads = keys_and_reads(me_ref[0], (b0, b1, b2, b3))
    reads_t = reads.T
    cbt = dot_nt(keys, reads)
    ahead = lax.broadcasted_iota(jnp.int32, (HALF, HALF), 0) <= lax.broadcasted_iota(
        jnp.int32, (HALF, HALF), 1
    )
    left = lax.broadcasted_iota(jnp.int32, (1, LANES), 1) < HEAD_DIM
    back16[...] = back[...].astype(bf16)
    dcb[...] = jnp.zeros_like(dcb)
    for strip in range(STRIPS):
        at = slice(strip * LANES, (strip + 1) * LANES)
        h0, h1 = 2 * strip, 2 * strip + 1
        act = act_ref[:, at]
        dy = dy_ref[:, at]
        actf = act.astype(f32)
        dyf = dy.astype(f32)
        skip = skip_ref[0:1, at]
        w_pair = jnp.where(left, w_end[:, h0 : h0 + 1], w_end[:, h1 : h1 + 1])
        e_pair = jnp.where(left, e_run[:, h0 : h0 + 1], e_run[:, h1 : h1 + 1])
        decayed = (dyf * e_pair).astype(bf16)
        edy[:, at] = decayed
        wx[:, at] = (actf * w_pair).astype(bf16)
        inter = dot_nn(keys, back16[:, at]) * w_pair
        top = jnp.zeros((HALF, LANES), f32)
        bottom = jnp.zeros((HALF, LANES), f32)
        for h, side in ((h0, left), (h1, jnp.logical_not(left))):
            x_h = jnp.where(side, actf, 0.0).astype(bf16)
            dy_h = jnp.where(side, dyf, 0.0).astype(bf16)
            g_top = dot_nt(x_h[:HALF], dy)
            g_bottom = dot_nt(x_h[HALF:], dy[HALF:])
            l00 = jnp.exp2(running_t[h : h + 1, :HALF] - shifted[:HALF, h : h + 1])
            l01 = jnp.exp2(running_t[h : h + 1, HALF:] - shifted[:HALF, h : h + 1])
            l11 = jnp.exp2(running_t[h : h + 1, HALF:] - shifted[HALF:, h : h + 1])
            m00 = jnp.where(ahead, l00 * cbt[:HALF, :HALF], 0.0).astype(bf16)
            m01 = (l01 * cbt[:HALF, HALF:]).astype(bf16)
            m11 = jnp.where(ahead, l11 * cbt[HALF:, HALF:], 0.0).astype(bf16)
            top = top + dot_nn(jnp.concatenate([m00, m01], axis=1), dy_h)
            bottom = bottom + dot_nn(m11, dy_h[HALF:])
            dcb[:HALF, :HALF] += jnp.where(ahead, l00 * g_top[:, :HALF], 0.0)
            dcb[:HALF, HALF:] += l01 * g_top[:, HALF:]
            dcb[HALF:, HALF:] += jnp.where(ahead, l11 * g_bottom, 0.0)
        intra = jnp.concatenate([top, bottom], axis=0)
        d_values = intra + inter
        p_12 = dyf * (y_ref[:, at] - skip * actf) - actf * intra
        p_12h = p_12.astype(bf16)
        p12h[:, at] = p_12h
        p12l[:, at] = (p_12 - p_12h.astype(f32)).astype(bf16)
        p3[:, at] = (actf * inter).astype(bf16)
        p23[:, at] = (actf * d_values).astype(bf16)
        d_act = d_values + skip * dyf
        pre = cw_ref[0:1, at] * xf[5 : 5 + Q, at]
        for tap in range(1, CONV):
            pre = pre + cw_ref[tap : tap + 1, at] * xf[5 + tap : 5 + tap + Q, at]
        squashed = sigmoid(pre)
        d_pre = d_act * squashed * (1.0 + pre * (1.0 - squashed))
        dp[0:Q, at] = d_pre
        sums = [
            jnp.sum(d_pre * xf[5 + tap : 5 + tap + Q, at], axis=0, keepdims=True)
            for tap in range(CONV)
        ]
        sums.append(jnp.sum(dyf * actf, axis=0, keepdims=True))
        for place, total in enumerate(sums):
            gconv_ref[place : place + 1, at] += total
        d_in = cw_ref[CONV - 1 : CONV, at] * d_pre
        for tap in range(CONV - 1):
            d_in = d_in + cw_ref[tap : tap + 1, at] * dp[CONV - 1 - tap : CONV - 1 - tap + Q, at]
        dci_ref[:, at] = d_in.astype(bf16)
        kept = back[:, at] * jnp.where(left, e_end[:, h0 : h0 + 1], e_end[:, h1 : h1 + 1])
        cross[0:1, at] = jnp.sum(kept * s_ref[0, :, at].astype(f32), axis=0, keepdims=True)
        back[:, at] = kept + dot_nn(reads_t, decayed)
    dcb_t = dcb[...]
    d_keys = dot_nn(dcb_t.astype(bf16), reads) + dot_nt(wx[...], back16[...])
    d_reads = dot_nn(dcb_t.T.astype(bf16), keys) + dot_nt(edy[...], s_ref[0])
    give_back(me_ref[0], d_keys, d_reads, dbc_ref)
    unit = lax.broadcasted_iota(jnp.int32, (OWN, LANES), 0)
    head = lax.broadcasted_iota(jnp.int32, (OWN, LANES), 1)
    member = jnp.where(unit // HEAD_DIM == head, 1.0, 0.0)
    member16 = member.astype(bf16)
    s_12 = dot_nn(p12h[...], member16) + dot_nn(p12l[...], member16)
    s_3 = dot_nn(p3[...], member16)
    s_23 = dot_nn(p23[...], member16)
    through = dot_exact(cross[...], member)[0:1, :]
    row = lax.broadcasted_iota(jnp.int32, (Q, Q), 0)
    column = lax.broadcasted_iota(jnp.int32, (Q, Q), 1)
    suffix = jnp.where(column >= row, 1.0, 0.0)
    prefix = jnp.where(column < row, 1.0, 0.0)
    d_log = dot_exact(suffix, s_12) + dot_exact(prefix, s_3) + through
    slope = sigmoid(v)
    ratio = jnp.where(steps > 0.0, slope / steps, 0.0)
    rate = rows_ref[1:2, :]
    d_sum = s_23 * ratio + rate * d_log * slope
    ddt_ref[...] = d_sum * rows_ref[2:3, :]
    grow_ref[0:1, :] += jnp.sum(d_sum, axis=0, keepdims=True)
    grow_ref[1:2, :] += jnp.sum(d_log * rate * steps, axis=0, keepdims=True)


def recurrence_backward(me, conv_in, act, dy, y, bc, dt_tile, entry, taps, rows, skip_row):
    length = conv_in.shape[0]
    blocks = length // Q
    whole = lambda i, me: (0, 0)
    along = lambda i, me: (blocks - 1 - i, 0)
    previous = lambda i, me: (jnp.maximum((blocks - 1 - i) * (Q // 16) - 1, 0), 0)
    return pl.pallas_call(
        backward_kernel,
        grid_spec=pltpu.PrefetchScalarGridSpec(
            num_scalar_prefetch=1,
            grid=(blocks,),
            in_specs=[
                pl.BlockSpec((Q, OWN), along),
                pl.BlockSpec((16, OWN), previous),
                pl.BlockSpec((Q, OWN), along),
                pl.BlockSpec((Q, OWN), along),
                pl.BlockSpec((Q, OWN), along),
            ]
            + [pl.BlockSpec((HALF, LANES), along)] * PART
            + [
                pl.BlockSpec((Q, LANES), along),
                pl.BlockSpec((1, STATE, OWN), lambda i, me: (blocks - 1 - i, 0, 0)),
                pl.BlockSpec((8, OWN), whole),
                pl.BlockSpec((8, LANES), whole),
                pl.BlockSpec((8, OWN), whole),
            ],
            out_specs=[
                pl.BlockSpec((Q, OWN), along),
                pl.BlockSpec((PART, HALF, LANES), lambda i, me: (0, blocks - 1 - i, 0)),
                pl.BlockSpec((Q, LANES), along),
                pl.BlockSpec((8, OWN), whole),
                pl.BlockSpec((8, LANES), whole),
            ],
            scratch_shapes=[
                pltpu.VMEM((STATE, OWN), f32),
                pltpu.VMEM((STATE, OWN), bf16),
                pltpu.VMEM((Q + 8, OWN), f32),
                pltpu.VMEM((Q + 8, OWN), f32),
                pltpu.VMEM((Q, OWN), bf16),
                pltpu.VMEM((Q, OWN), bf16),
                pltpu.VMEM((Q, Q), f32),
                pltpu.VMEM((Q, OWN), bf16),
                pltpu.VMEM((Q, OWN), bf16),
                pltpu.VMEM((Q, OWN), bf16),
                pltpu.VMEM((Q, OWN), bf16),
                pltpu.VMEM((8, OWN), f32),
            ],
        ),
        out_shape=[
            jax.ShapeDtypeStruct((length, CONV_COLS), bf16),
            jax.ShapeDtypeStruct((PART, length // 2, LANES), bf16),
            jax.ShapeDtypeStruct((length, LANES), f32),
            jax.ShapeDtypeStruct((8, OWN), f32),
            jax.ShapeDtypeStruct((8, LANES), f32),
        ],
        compiler_params=pltpu.CompilerParams(
            dimension_semantics=("arbitrary",), vmem_limit_bytes=60 * 2**20
        ),
        cost_estimate=pl.CostEstimate(
            flops=70 * 10**9, bytes_accessed=2**24, transcendentals=10**7
        ),
        name="recurrence_backward",
    )(me, conv_in, conv_in, act, dy, y, *bc, dt_tile, entry, taps, rows, skip_row)


def pull_out_kernel(order_ref, own, sibling, across_a, across_b, corner_a, corner_b, wo_ref, cot_ref, d_ref):
    del order_ref
    step = pl.program_id(0)
    half = across_a.shape[0]
    for k, ref in enumerate((own, sibling)):

        @pl.when(step == k)
        def _():
            cot_ref[...] = ref[...]

    for k, (first, second) in enumerate(((across_a, across_b), (corner_a, corner_b))):

        @pl.when(step == 2 + k)
        def _():
            cot_ref[:half, :] = first[...]
            cot_ref[half:, :] = second[...]

    d_ref[...] = dot_nt(cot_ref[...], wo_ref[...])


def pull_out(pieces, order, w_o):
    tile = pieces[0].shape[0]
    whole = lambda i, order: (0, 0)
    there = lambda i, order: (order[i], 0)
    length = tile * PART
    return pl.pallas_call(
        pull_out_kernel,
        grid_spec=pltpu.PrefetchScalarGridSpec(
            num_scalar_prefetch=1,
            grid=(PART,),
            in_specs=[pl.BlockSpec(piece.shape, whole) for piece in pieces]
            + [pl.BlockSpec((OWN, D), whole)],
            out_specs=[pl.BlockSpec((tile, D), there), pl.BlockSpec((tile, OWN), there)],
        ),
        out_shape=[
            jax.ShapeDtypeStruct((length, D), bf16),
            jax.ShapeDtypeStruct((length, OWN), f32),
        ],
        compiler_params=pltpu.CompilerParams(vmem_limit_bytes=52 * 2**20),
        cost_estimate=pl.CostEstimate(
            flops=2 * length * D * OWN, bytes_accessed=2**25, transcendentals=0
        ),
        name="pull_out",
    )(order, *pieces, w_o)


def gate_forward_kernel(n_ref, y_ref, d_ref, wg_ref, row_ref, z_ref, sums_ref):
    z = dot_nn(n_ref[...], wg_ref[...]) * row_ref[1:2, :]
    z_ref[...] = z
    gated = y_ref[...] * (z * sigmoid(z))
    squares = jnp.sum(gated * gated, axis=1, keepdims=True)
    cross = jnp.sum(d_ref[...] * row_ref[0:1, :] * gated, axis=1, keepdims=True)
    lane = lax.broadcasted_iota(jnp.int32, (1, LANES), 1)
    both = jnp.where(lane == 0, squares, jnp.where(lane == 1, cross, 0.0))
    sums_ref[...] = both.T[0:8, :]


def gate_forward(normed, y, d, w_gate, row):
    length = normed.shape[0]
    whole = lambda i: (0, 0)
    along = lambda i: (i, 0)
    return pl.pallas_call(
        gate_forward_kernel,
        grid=(length // WIDE,),
        in_specs=[
            pl.BlockSpec((WIDE, D), along),
            pl.BlockSpec((WIDE, OWN), along),
            pl.BlockSpec((WIDE, OWN), along),
            pl.BlockSpec((D, OWN), whole),
            pl.BlockSpec((8, OWN), whole),
        ],
        out_specs=[
            pl.BlockSpec((WIDE, OWN), along),
            pl.BlockSpec((8, WIDE), lambda i: (0, i)),
        ],
        out_shape=[
            jax.ShapeDtypeStruct((length, OWN), f32),
            jax.ShapeDtypeStruct((8, length), f32),
        ],
        compiler_params=pltpu.CompilerParams(vmem_limit_bytes=52 * 2**20),
        cost_estimate=pl.CostEstimate(
            flops=2 * length * D * OWN, bytes_accessed=2**25, transcendentals=length * OWN
        ),
        name="gate_forward",
    )(normed, y, d, w_gate, row)


def gate_backward_kernel(y_ref, z_ref, d_ref, sums_ref, row_ref, out_ref, dy_ref, dz_ref, gain_ref):
    @pl.when(pl.program_id(0) == 0)
    def _():
        gain_ref[...] = jnp.zeros_like(gain_ref)

    units = row_ref[2:3, 0:1]
    sums = sums_ref[...]
    inverse = lax.rsqrt(sums[0:1, :] / units + epsilon)
    pull = inverse * inverse * inverse * sums[1:2, :] / units
    row = lax.broadcasted_iota(jnp.int32, (LANES, 1), 0)
    columns = jnp.where(row == 0, inverse, jnp.where(row == 1, pull, 0.0)).T
    inverse, pull = columns[:, 0:1], columns[:, 1:2]
    for strip in range(STRIPS):
        at = slice(strip * LANES, (strip + 1) * LANES)
        y, z, d = y_ref[:, at], z_ref[:, at], d_ref[:, at]
        gain = row_ref[0:1, at]
        squashed = sigmoid(z)
        act = z * squashed
        gated = y * act
        normalized = gated * inverse
        out_ref[:, at] = (normalized * gain).astype(bf16)
        gain_ref[0:1, at] += jnp.sum(d * normalized, axis=0, keepdims=True)
        d_gated = inverse * (d * gain) - gated * pull
        dy_ref[:, at] = (d_gated * act).astype(bf16)
        dz_ref[:, at] = (d_gated * y * squashed * (1.0 + z * (1.0 - squashed))).astype(bf16)


def gate_backward(y, z, d, sums, row):
    length = y.shape[0]
    whole = lambda i: (0, 0)
    along = lambda i: (i, 0)
    return pl.pallas_call(
        gate_backward_kernel,
        grid=(length // Q,),
        in_specs=[pl.BlockSpec((Q, OWN), along)] * 3
        + [pl.BlockSpec((8, Q), lambda i: (0, i)), pl.BlockSpec((8, OWN), whole)],
        out_specs=[pl.BlockSpec((Q, OWN), along)] * 3 + [pl.BlockSpec((8, OWN), whole)],
        out_shape=[jax.ShapeDtypeStruct((length, OWN), bf16)] * 3
        + [jax.ShapeDtypeStruct((8, OWN), f32)],
        compiler_params=pltpu.CompilerParams(vmem_limit_bytes=32 * 2**20),
        cost_estimate=pl.CostEstimate(
            flops=30 * length * OWN, bytes_accessed=18 * length * OWN, transcendentals=length * OWN
        ),
        name="gate_backward",
    )(y, z, d, sums, row)


def input_gradient_kernel(core_ref, z_ref, p_ref, wg_ref, wc_ref, other_ref, mine_ref):
    del core_ref
    out = (dot_nt(z_ref[...], wg_ref[...]) + dot_nt(p_ref[...], wc_ref[...])).astype(bf16)

    @pl.when(pl.program_id(0) < 2)
    def _():
        other_ref[...] = out

    @pl.when(pl.program_id(0) >= 2)
    def _():
        mine_ref[...] = out


def input_gradient(core, d_z, d_project, w_gate, w_conv):
    tokens = d_z.shape[0] // PART
    whole = lambda i, core: (0, 0)
    along = lambda i, core: (i % 2 * 2 + jnp.where(i < 2, 1 - core[0], core[0]), 0)
    return pl.pallas_call(
        input_gradient_kernel,
        grid_spec=pltpu.PrefetchScalarGridSpec(
            num_scalar_prefetch=1,
            grid=(PART,),
            in_specs=[
                pl.BlockSpec((tokens, OWN), along),
                pl.BlockSpec((tokens, CONV_COLS), along),
                pl.BlockSpec((D, OWN), whole),
                pl.BlockSpec((D, CONV_COLS), whole),
            ],
            out_specs=[
                pl.BlockSpec((tokens, D), lambda i, core: (jnp.minimum(i, 1), 0)),
                pl.BlockSpec((tokens, D), lambda i, core: (jnp.maximum(i - 2, 0), 0)),
            ],
        ),
        out_shape=[jax.ShapeDtypeStruct((2 * tokens, D), bf16)] * 2,
        compiler_params=pltpu.CompilerParams(vmem_limit_bytes=60 * 2**20),
        cost_estimate=pl.CostEstimate(
            flops=10**10, bytes_accessed=2**22, transcendentals=0
        ),
        name="input_gradient",
    )(core, d_z, d_project, w_gate, w_conv)


def products_kernel(n_ref, z_ref, r_ref, t_ref, out_ref):
    rows = D // STRIPS
    gate = dot_nn(n_ref[...].T, z_ref[...]).astype(bf16)
    rest = dot_nn(r_ref[...].T, t_ref[...]).astype(bf16)
    for k in range(out_ref.shape[0]):
        out_ref[k, :rows, :] = gate[k * rows : (k + 1) * rows]
        product = rest[k * LANES : (k + 1) * LANES]
        out_ref[k, rows : rows + LANES, :] = product[:, :OWN]
        out_ref[k, rows + LANES :, :] = product[:, OWN:]


def products(normed, d_z, rounded_out, cot):
    length = normed.shape[0]
    rows = D // STRIPS
    each = 2
    whole = lambda i: (0, 0)
    across = lambda i: (0, i)
    return pl.pallas_call(
        products_kernel,
        grid=(STRIPS // each,),
        in_specs=[
            pl.BlockSpec((length, each * rows), across),
            pl.BlockSpec((length, OWN), whole),
            pl.BlockSpec((length, each * LANES), across),
            pl.BlockSpec((length, D), whole),
        ],
        out_specs=pl.BlockSpec((each, rows + 2 * LANES, OWN), lambda i: (i, 0, 0)),
        out_shape=jax.ShapeDtypeStruct((STRIPS, rows + 2 * LANES, OWN), bf16),
        compiler_params=pltpu.CompilerParams(vmem_limit_bytes=56 * 2**20),
        cost_estimate=pl.CostEstimate(
            flops=4 * length * D * OWN, bytes_accessed=2**25, transcendentals=0
        ),
        name="products",
    )(normed, d_z, rounded_out, cot)


def rows_kernel(me_ref, *refs):
    gates, convs = refs[:PART], refs[PART : 2 * PART]
    w_ref, wdt_ref, gain_ref, grad_ref, gdt_ref, gnorm_ref = refs[2 * PART :]
    me = me_ref[0]
    rows = w_ref.shape[0]
    for k in range(PART):
        owner = jnp.bitwise_xor(me, k)
        for strip in range(STRIPS):
            at = slice(strip * LANES, (strip + 1) * LANES)
            first = pl.multiple_of((strip * PART + owner) * LANES, LANES)
            grad_ref[:, pl.ds(first, LANES)] = gates[k][:, at].astype(f32)
            grad_ref[:, pl.ds(INNER + first, LANES)] = convs[k][:, at].astype(f32)
    odd, lower = me % 2 == 1, me >= 2
    p = [convs[k][:, OWN:].astype(f32) for k in range(PART)]
    r0, r1 = jnp.where(odd, p[1], p[0]), jnp.where(odd, p[0], p[1])
    r2, r3 = jnp.where(odd, p[3], p[2]), jnp.where(odd, p[2], p[3])
    tails = (
        jnp.where(lower, r2, r0),
        jnp.where(lower, r3, r1),
        jnp.where(lower, r0, r2),
        jnp.where(lower, r1, r3),
    )
    left = lax.broadcasted_iota(jnp.int32, (1, LANES), 1) < OWN_BC
    for pair in range(2):
        low, high = tails[2 * pair], tails[2 * pair + 1]
        first = 2 * INNER + pair * LANES
        grad_ref[:, first : first + LANES] = jnp.where(left, pltpu.roll(low, OWN_BC, 1), high)
    slot = lax.broadcasted_iota(jnp.int32, (LANES, HEADS), 0)
    head = lax.broadcasted_iota(jnp.int32, (LANES, HEADS), 1)
    d_dt = jnp.zeros((rows, HEADS), f32)
    for owner in range(PART):
        chosen = (slot < OWN_HEADS) & (head == slot // 2 * 2 * PART + 2 * owner + slot % 2)
        d_dt = d_dt + dot_nn(tails[owner].astype(bf16), jnp.where(chosen, 1.0, 0.0).astype(bf16))
    gdt_ref[...] = d_dt
    total = jnp.sum(wdt_ref[...].astype(f32) * d_dt, axis=1, keepdims=True)
    for strip in range(2 * STRIPS * PART + 2):
        at = slice(strip * LANES, (strip + 1) * LANES)
        total = total + jnp.sum(w_ref[:, at].astype(f32) * grad_ref[:, at], axis=1, keepdims=True)
    square = lax.broadcasted_iota(jnp.int32, (rows, rows), 0) == lax.broadcasted_iota(
        jnp.int32, (rows, rows), 1
    )
    flat = jnp.sum(jnp.where(square, total, 0.0), axis=0, keepdims=True)
    gnorm_ref[...] = flat / gain_ref[...].astype(f32)


def projection_rows(me, gates, convs, w_in, w_dt, norm_gain):
    rows = w_in.shape[0]
    whole = lambda *block: pl.BlockSpec(block, lambda i, me: (0,) * len(block))
    columns = w_in.shape[1]
    return pl.pallas_call(
        rows_kernel,
        grid_spec=pltpu.PrefetchScalarGridSpec(
            num_scalar_prefetch=1,
            grid=(1,),
            in_specs=[whole(rows, OWN)] * PART
            + [whole(rows, CONV_COLS)] * PART
            + [whole(rows, columns), whole(rows, HEADS), whole(1, rows)],
            out_specs=[whole(rows, columns), whole(rows, HEADS), whole(1, rows)],
        ),
        out_shape=[
            jax.ShapeDtypeStruct((rows, columns), f32),
            jax.ShapeDtypeStruct((rows, HEADS), f32),
            jax.ShapeDtypeStruct((1, rows), f32),
        ],
        compiler_params=pltpu.CompilerParams(vmem_limit_bytes=60 * 2**20),
        name="projection_rows",
    )(me, *gates, *convs, w_in, w_dt, norm_gain[None, :])


def per_device(
    hidden_in,
    widths,
    norm_gain,
    w_in,
    w_dt,
    conv_weight,
    dt_bias,
    a_log,
    skip_gain,
    gate_gain,
    w_out,
    grad_out,
):
    me = lax.axis_index("seq")
    tokens = hidden_in.shape[1]
    length = tokens * PART
    rows_in = w_in.shape[0]
    used_units = INNER // 8 * jnp.left_shift(jnp.int32(1), widths[0])
    units_float = used_units.astype(f32)
    block = jnp.arange(OWN) // LANES * PART + me
    unit_used = block * LANES < used_units
    head_used = ((jnp.arange(OWN_HEADS) // 2 * PART + me) * LANES < used_units).astype(f32)

    if fast_mesh():
        conv_pieces, gate_pieces = owners_pieces(w_in, w_dt, norm_gain, gate_gain)
    else:
        every = lambda a: jnp.broadcast_to(a[None], (PART,) + a.shape)
        tail = jnp.concatenate(
            [
                heads_by_owner(w_dt),
                every(norm_gain[:, None]),
                every(gate_gain.reshape(2, rows_in).T),
                jnp.zeros((PART, rows_in, LANES - OWN_HEADS - 3 - OWN_BC), bf16),
                w_in[:, 2 * INNER :].reshape(rows_in, PART, OWN_BC).transpose(1, 0, 2),
            ],
            axis=2,
        )
        conv_pieces = jnp.concatenate([by_owner(w_in[:, INNER : 2 * INNER]), tail], axis=2)
        gate_pieces = by_owner(w_in[:, :INNER])

    gather = gather_everything if fast_mesh() else gather_plainly
    w_conv, w_gate, w_o, x_pieces, (cot_a, cot_b) = gather(
        conv_pieces, gate_pieces, w_out, hidden_in[0], grad_out[0]
    )
    order = jnp.stack([me, me ^ 1, me ^ 2, me ^ 3]).astype(jnp.int32)
    gate_all = w_conv[:, OWN + OWN_HEADS + 1 : OWN + OWN_HEADS + 3]
    gate_all = gate_all.reshape(D // rows_in, rows_in, 2).transpose(0, 2, 1)
    gate_row = lax.dynamic_index_in_dim(gate_all.reshape(STRIPS, PART, LANES), me, 1, False)
    gate_row = gate_row.reshape(1, OWN).astype(f32)
    gain_row = w_conv[:, OWN + OWN_HEADS].astype(f32)[None, :]

    def own_heads(array):
        return lax.dynamic_index_in_dim(array.reshape(STRIPS, PART, 2), me, 1, False).reshape(-1)

    bias = own_heads(dt_bias)
    rate = -jnp.exp(own_heads(a_log))
    skip = own_heads(skip_gain)
    pad_heads = lambda a: jnp.pad(a, (0, LANES - OWN_HEADS))
    rows = jnp.stack(
        [pad_heads(bias), pad_heads(rate), pad_heads(head_used)] + [jnp.zeros((LANES,), f32)] * 5
    )
    skip_row = jnp.broadcast_to(jnp.repeat(skip, HEAD_DIM)[None, :], (8, OWN))
    taps = lax.dynamic_index_in_dim(
        conv_weight[:, :INNER].reshape(CONV, STRIPS, PART, LANES), me, 2, False
    ).reshape(CONV, OWN)
    taps = jnp.pad(taps.astype(f32), ((0, 8 - CONV), (0, 0)))
    taps_bc = lax.dynamic_slice_in_dim(conv_weight[:, INNER:], me * OWN_BC, OWN_BC, 1).astype(f32)
    taps_tile = jnp.pad(taps_bc, ((0, 8 - CONV), (LANES - OWN_BC, 0)))
    place_me = me.astype(jnp.int32).reshape(1)

    normed = all_positions(x_pieces, order, jnp.broadcast_to(gain_row, (8, D)))
    dt_tile = dot_nn(normed, w_conv[:, OWN:])
    bc = bc_forward(dt_tile, taps_tile)
    bc = [bc] + [xor_seq(bc, bits) for bits in range(1, PART)]
    conv_in = jnp.where(unit_used, dot_nn(normed, w_conv[:, :OWN]), 0.0).astype(bf16)
    if fast_mesh():
        w_o += [dp_swap_x(piece) for piece in w_o[1:4]]
    else:
        cot_a = xor_seq(cot_a, 2)
    cot_b, conv_in, *bc[1:] = tie(cot_b, conv_in, *bc[1:])
    cot_b = xor_seq(cot_b, 2)
    y, act, entry = recurrence_forward(place_me, conv_in, bc, dt_tile, taps, rows, skip_row)
    if fast_mesh():
        cot_b, *w_o[5:] = after([cot_b, *w_o[5:]], [entry])
        w_o = assemble(w_o, out_places(), 512)
    else:
        (cot_b,) = after([cot_b], [entry])
    cot_pieces = (
        grad_out[0], xor_seq(grad_out[0], 1), cot_a, cot_b, xor_seq(cot_a, 1), xor_seq(cot_b, 1)
    )
    cot_all, d_rounded = pull_out(cot_pieces, order, w_o)
    row = jnp.concatenate(
        [
            gate_row,
            unit_used.astype(f32)[None, :],
            jnp.full((6, OWN), units_float),
        ],
        axis=0,
    )
    z, sums = gate_forward(normed, y, d_rounded, w_gate, row)
    rounded_out, d_y, d_z, grad_gate_rows = gate_backward(y, z, d_rounded, seq_total(sums), row)
    grad_gate_local = grad_gate_rows[0]

    if fast_mesh():
        both = products(normed, d_z, rounded_out, cot_all)
        d_y, both = tie(d_y, both)
        both_total = dp_sum(both.reshape(-1, OWN))

    d_values, d_bc, d_dt, g_conv, g_rows = recurrence_backward(
        place_me, conv_in, act, d_y, y, bc, dt_tile, entry, taps, rows, skip_row
    )
    if fast_mesh():
        d_values, d_bc, rounded_out = tie(d_values, d_bc, rounded_out)
    branch = dot_nn(rounded_out, w_o).astype(bf16).reshape(PART, tokens, D)
    branch_mine, branch_got = core_halves(branch)
    d_bc_mine, d_bc_got = seq_scatter_relative(d_bc)
    branch_keep, branch_give = halves_sum(branch_mine, branch_got)
    d_bc_got, branch_give = tie(d_bc_got, branch_give)
    d_project, g_tail = tail_backward(
        dt_tile, d_bc_mine + d_bc_got.astype(f32), d_dt, taps_tile, d_values
    )
    g_skip = jnp.sum(g_conv[4].reshape(OWN_HEADS, HEAD_DIM), axis=1)
    small = jnp.concatenate(
        [
            g_conv[:CONV].reshape(-1),
            g_tail[:CONV, LANES - OWN_BC :].reshape(-1),
            pad_heads(g_rows[0, :OWN_HEADS]),
            pad_heads(g_rows[1, :OWN_HEADS]),
            pad_heads(g_skip),
            grad_gate_local,
        ]
    )
    count = small.shape[0]
    padded = -(-count // (8 * LANES)) * 8 * LANES
    small = jnp.pad(small, (0, padded - count)).reshape(-1, LANES)
    if fast_mesh():
        conv_product = dot_tn(normed, d_project).astype(bf16)
        d_project, conv_product = tie(d_project, conv_product)
        (conv_product,) = after([conv_product], [both_total])
        conv_total = dp_sum(conv_product)
    branch_across = xor_seq(branch_give, 2)
    other, mine = input_gradient(place_me % 2, d_z, d_project, w_gate, w_conv)
    if fast_mesh():
        branch_across, other, mine = tie(branch_across, other, mine)
    mine = mine.reshape(2, tokens, D)
    got = xor_seq(other, 1).reshape(2, tokens, D)
    keep, give = halves_sum(mine, got)
    small, give = tie(small, give)
    across = xor_seq(give, 2)
    small, across = tie(dp_total(small), across)
    d_own = keep + across.astype(f32)
    if fast_mesh():
        both_total = after([both_total], [across])[0]
        small_pieces = seq_pieces(small)
        gate_rows, out_left, out_right = jnp.split(both_total, [rows_in * PART, rows_in * PART + LANES])
        grad_w_out = jnp.concatenate([out_left, out_right], axis=1).astype(f32)
        gate_rows = owners_rows(gate_rows)
        (conv_total,) = after([conv_total], [small_pieces[3], *gate_rows[1:]])
        grad_w_in, grad_w_dt, grad_norm_gain = projection_rows(
            place_me, gate_rows, owners_rows(conv_total), w_in, w_dt, norm_gain
        )
        grad_norm_gain = grad_norm_gain[0]
    else:
        small_pieces = seq_pieces(small)
        grad_w_out = scatter_out(dot_tn(rounded_out, cot_all).astype(bf16))
        grad_gate_in = scatter_in(dot_tn(normed, d_z).astype(bf16))
        grad_conv_in = scatter_in(dot_tn(normed, d_project).astype(bf16))
        grad_w_in = jnp.concatenate(
            [
                from_owner(grad_gate_in),
                from_owner(grad_conv_in[:, :, :OWN]),
                grad_conv_in[:, :, CONV_COLS - OWN_BC :].transpose(1, 0, 2).reshape(rows_in, 2 * STATE),
            ],
            axis=1,
        )
        grad_w_dt = heads_from_owner(grad_conv_in[:, :, OWN : OWN + OWN_HEADS])
        grad_norm_gain = (
            jnp.sum(w_in.astype(f32) * grad_w_in, axis=1)
            + jnp.sum(w_dt.astype(f32) * grad_w_dt, axis=1)
        ) / norm_gain.astype(f32)
    x_own = hidden_in[0].astype(f32)
    hidden_out = (x_own + branch_keep + branch_across.astype(f32)).astype(bf16)[None]
    own_rms = lax.rsqrt(jnp.mean(x_own * x_own, axis=1, keepdims=True) + epsilon)
    d_scaled = d_own * gain_row
    d_input = own_rms * d_scaled - x_own * own_rms**3 * jnp.mean(
        d_scaled * x_own, axis=1, keepdims=True
    )
    grad_in = (grad_out[0].astype(f32) + d_input).astype(bf16)[None]

    every = jnp.stack(by_partner(small_pieces)).reshape(PART, padded)
    start = 0

    def take(size):
        nonlocal start
        start += size
        return every[:, start - size : start]

    all_conv = take(CONV * OWN).reshape(PART, CONV, OWN)
    all_conv_bc = take(CONV * OWN_BC).reshape(PART, CONV, OWN_BC)
    head_sums = [heads_from_owner(take(LANES)[:, None, :OWN_HEADS]).reshape(HEADS) for _ in range(3)]
    grad_gate = lax.dynamic_index_in_dim(take(OWN), me, 0, False)
    grad_conv = jnp.concatenate(
        [from_owner(all_conv), all_conv_bc.transpose(1, 0, 2).reshape(CONV, 2 * STATE)], axis=1
    )
    place = lax.axis_index(("dp", "seq"))
    gain_rows = gate_gain.shape[0]
    if gain_rows == LANES:
        grad_gate_gain = lax.dynamic_slice_in_dim(
            grad_gate, lax.axis_index("dp") * gain_rows, gain_rows, 0
        )
    else:
        start = CONV * OWN + CONV * OWN_BC + 3 * LANES
        whole_gate = from_owner(take(OWN)[:, None, :]).reshape(INNER)
        grad_gate_gain = lax.dynamic_slice_in_dim(whole_gate, place * gain_rows, gain_rows, 0)

    return (
        hidden_out,
        grad_in,
        grad_norm_gain,
        grad_w_in,
        grad_w_dt,
        grad_conv,
        head_sums[0],
        head_sums[1],
        head_sums[2],
        grad_gate_gain,
        grad_w_out,
    )


def solution(mesh):
    return jax.shard_map(
        per_device,
        mesh=mesh,
        in_specs=(
            P("dp", "seq", None),
            P("dp"),
            P(("dp", "seq")),
            P(("dp", "seq"), None),
            P(("dp", "seq"), None),
            P(),
            P(),
            P(),
            P(),
            P(("dp", "seq")),
            P(("dp", "seq"), None),
            P("dp", "seq", None),
        ),
        out_specs=(
            P("dp", "seq", None),
            P("dp", "seq", None),
            P(("dp", "seq")),
            P(("dp", "seq"), None),
            P(("dp", "seq"), None),
            P(),
            P(),
            P(),
            P(),
            P(("dp", "seq")),
            P(("dp", "seq"), None),
        ),
        check_vma=False,
    )
```

```python
import functools

import jax
import jax.numpy as jnp
from jax import lax
from jax.experimental import pallas as pl
from jax.experimental.pallas import tpu as pltpu
from jax.sharding import PartitionSpec as P

D = 2048
INNER = 4096
HEAD_DIM = 64
STATE = 128
CONV = 4
HEADS = 64
CHANNELS = 4352

PART = 4
LANES = 128
STRIPS = INNER // LANES // PART
OWN = STRIPS * LANES
OWN_HEADS = OWN // HEAD_DIM
OWN_BC = 2 * STATE // PART
CONV_COLS = OWN + LANES
Q = 256
HALF = Q // 2
WIDE = 512

epsilon = 1e-05
highest = lax.Precision.HIGHEST
f32 = jnp.float32
bf16 = jnp.bfloat16
LOG2E = 1.4426950408889634


def swap(value, axis, pairs):
    return lax.ppermute(value, axis, pairs)


def xor_seq(value, bits):
    return lax.ppermute(value, "seq", [(s, s ^ bits) for s in range(PART)])


def core_halves(blocks):
    core = lax.axis_index("seq") % 2
    view = blocks.reshape((2, 2) + blocks.shape[1:])
    mine = lax.dynamic_index_in_dim(view, core, 1, False)
    other = lax.dynamic_index_in_dim(view, 1 - core, 1, False)
    return mine, xor_seq(other, 1)


def halves_sum(mine, received):
    row = lax.axis_index("seq") // 2

    def of(which):
        a = lax.dynamic_index_in_dim(mine, which, 0, False)
        return a.astype(f32) + lax.dynamic_index_in_dim(received, which, 0, False).astype(f32)

    return of(row), of(1 - row).astype(bf16)


def seq_scatter_relative(blocks):
    view = blocks.reshape((2, 2) + blocks.shape[1:])
    half = view[:, 0].astype(f32) + xor_seq(view[:, 1], 1).astype(f32)
    return half[0], xor_seq(half[1].astype(bf16), 2)


def by_partner(pieces):
    me = lax.axis_index("seq")
    odd, lower = me % 2 == 1, me >= 2
    a, b, c, d = pieces
    a, b = jnp.where(odd, b, a), jnp.where(odd, a, b)
    c, d = jnp.where(odd, d, c), jnp.where(odd, c, d)
    return (
        jnp.where(lower, c, a),
        jnp.where(lower, d, b),
        jnp.where(lower, a, c),
        jnp.where(lower, b, d),
    )


def seq_exchange(pieces):
    turned = by_partner([pieces[k] for k in range(PART)])
    return [turned[0]] + [xor_seq(turned[k], k) for k in range(1, PART)]


def seq_total(value):
    return value + xor_seq(value, 1) + xor_seq(value, 2) + xor_seq(value, 3)


def fast_mesh():
    return lax.axis_size("dp") == 8


def dp_shift_z(value, steps):
    pairs = [(z * 2 + x, (z + steps) % 4 * 2 + x) for z in range(4) for x in range(2)]
    return lax.ppermute(value, "dp", pairs)


def dp_swap_x(value):
    return lax.ppermute(value, "dp", [(d, d ^ 1) for d in range(8)])


def tie_kernel(*refs):
    del refs


def tie(*values):
    anywhere = pl.BlockSpec(memory_space=pl.ANY)
    return pl.pallas_call(
        tie_kernel,
        in_specs=[anywhere] * len(values),
        out_specs=[anywhere] * len(values),
        out_shape=[jax.ShapeDtypeStruct(v.shape, v.dtype) for v in values],
        input_output_aliases={k: k for k in range(len(values))},
        name="tie",
    )(*values)


def after(values, needed):
    anywhere = pl.BlockSpec(memory_space=pl.ANY)
    return pl.pallas_call(
        tie_kernel,
        in_specs=[anywhere] * (len(values) + len(needed)),
        out_specs=[anywhere] * len(values),
        out_shape=[jax.ShapeDtypeStruct(v.shape, v.dtype) for v in values],
        input_output_aliases={k: k for k in range(len(values))},
        name="after",
    )(*values, *needed)


def assemble_kernel(places_ref, *refs):
    rows = refs[0].shape[0]
    for k, piece in enumerate(refs[:-1]):
        refs[-1][pl.ds(pl.multiple_of(places_ref[k] * rows, rows), rows), :] = piece[...]


def assemble(pieces, places, tile):
    rows, columns = pieces[0].shape
    count = len(pieces)
    along = lambda i, places: (0, i)
    return pl.pallas_call(
        assemble_kernel,
        grid_spec=pltpu.PrefetchScalarGridSpec(
            num_scalar_prefetch=1,
            grid=(columns // tile,),
            in_specs=[pl.BlockSpec((rows, tile), along)] * count,
            out_specs=pl.BlockSpec((rows * count, tile), along),
        ),
        out_shape=jax.ShapeDtypeStruct((rows * count, columns), pieces[0].dtype),
        compiler_params=pltpu.CompilerParams(vmem_limit_bytes=60 * 2**20),
        cost_estimate=pl.CostEstimate(
            flops=0, bytes_accessed=4 * rows * count * columns, transcendentals=0
        ),
        name="assemble",
    )(places, *pieces)


def pieces_kernel(w_ref, dt_ref, norm_ref, gate_ref, conv_ref, gates_ref):
    rows = w_ref.shape[0]
    lane = lax.broadcasted_iota(jnp.int32, (1, LANES), 1)
    square = lax.broadcasted_iota(jnp.int32, (rows, rows), 0) == lax.broadcasted_iota(
        jnp.int32, (rows, rows), 1
    )

    def column(values):
        return jnp.sum(jnp.where(square, values, 0.0), axis=1, keepdims=True)

    gain = column(norm_ref[0:1, :].astype(f32))
    gates = [column(gate_ref[k : k + 1, :].astype(f32)) for k in range(2)]
    head = lax.broadcasted_iota(jnp.int32, (HEADS, LANES), 0)
    slot = lax.broadcasted_iota(jnp.int32, (HEADS, LANES), 1)
    for owner in range(PART):
        for strip in range(STRIPS):
            source = (strip * PART + owner) * LANES
            at = slice(strip * LANES, (strip + 1) * LANES)
            gates_ref[owner, :, at] = w_ref[:, source : source + LANES]
            conv_ref[owner, :, at] = w_ref[:, INNER + source : INNER + source + LANES]
        chosen = (slot < OWN_HEADS) & (head == slot // 2 * 2 * PART + 2 * owner + slot % 2)
        steps = dot_nn(dt_ref[...], jnp.where(chosen, 1.0, 0.0).astype(bf16))
        first = 2 * INNER + owner // 2 * LANES
        tile = w_ref[:, first : first + LANES].astype(f32)
        if owner % 2 == 0:
            tile = pltpu.roll(tile, OWN_BC, 1)
        tail = jnp.where(lane < OWN_HEADS, steps, jnp.where(lane == OWN_HEADS, gain, 0.0))
        for k in range(2):
            tail = jnp.where(lane == OWN_HEADS + 1 + k, gates[k], tail)
        tail = jnp.where(lane >= LANES - OWN_BC, tile, tail)
        conv_ref[owner, :, OWN:] = tail.astype(bf16)


def owners_pieces(w_in, w_dt, norm_gain, gate_gain):
    rows = w_in.shape[0]
    whole = lambda *block: pl.BlockSpec(block, lambda i: (0,) * len(block))

    return pl.pallas_call(
        pieces_kernel,
        grid=(1,),
        in_specs=[whole(rows, 2 * INNER + 2 * STATE), whole(rows, HEADS), whole(1, rows), whole(2, rows)],
        out_specs=[whole(PART, rows, CONV_COLS), whole(PART, rows, OWN)],
        out_shape=[
            jax.ShapeDtypeStruct((PART, rows, CONV_COLS), bf16),
            jax.ShapeDtypeStruct((PART, rows, OWN), bf16),
        ],
        compiler_params=pltpu.CompilerParams(vmem_limit_bytes=32 * 2**20),
        name="owners_pieces",
    )(w_in, w_dt, norm_gain[None, :], gate_gain.reshape(2, rows))


def seq_pass(pieces, *beside):
    me = lax.axis_index("seq")
    core, row = me % 2, me // 2
    view = pieces.reshape((2, 2) + pieces.shape[1:])
    give = lax.dynamic_index_in_dim(view, 1 - row, 0, False)
    keep = lax.dynamic_index_in_dim(view, row, 0, False)
    got, *beside = tie(xor_seq(give, 2), *beside)
    lower = jnp.where(row == 0, keep, got)
    upper = jnp.where(row == 0, got, keep)
    both = jnp.stack([lower, upper])
    mine = lax.dynamic_index_in_dim(both, core, 1, False)
    other = xor_seq(lax.dynamic_index_in_dim(both, 1 - core, 1, False), 1)
    first = jnp.where(core == 0, mine, other)
    second = jnp.where(core == 0, other, mine)
    return jnp.stack([first, second], axis=1).reshape((-1,) + pieces.shape[2:]), beside


def seq_pieces(block, after=None):
    source = block if after is None else tie(block, after)[0]
    across = xor_seq(source, 2)
    return block, xor_seq(block, 1), across, xor_seq(across, 1)


def gather_everything(conv_pieces, gate_pieces, o, x_block, cot_block):
    c, (o1,) = seq_pass(conv_pieces, dp_shift_z(o, 1))
    w_conv = lax.all_gather(c, "dp", axis=0, tiled=True)
    x_across, gate_pieces, o2, o3, o_x = tie(
        xor_seq(after([x_block], [c])[0], 2),
        gate_pieces,
        dp_shift_z(o, 2),
        dp_shift_z(o, 3),
        dp_swap_x(o),
    )
    g, _ = seq_pass(gate_pieces)
    half = cot_block.shape[0] // 2
    cot_a, cot_b = after([cot_block[:half], cot_block[half:]], [g])
    g, x_across, cot_a = after([g, x_across, xor_seq(cot_a, 2)], [w_conv])
    x_pieces = (x_block, xor_seq(x_block, 1), x_across, xor_seq(x_across, 1))
    w_gate = lax.all_gather(g, "dp", axis=0, tiled=True)
    return w_conv, w_gate, [o, o1, o2, o3, o_x], x_pieces, (cot_a, cot_b)


def out_places():
    dp = lax.axis_index("dp")
    sources = (dp // 2 - jnp.arange(4, dtype=jnp.int32) + 4) % 4 * 2
    return jnp.concatenate([sources + dp % 2, sources + 1 - dp % 2]).astype(jnp.int32)


def norm_rows(x, gain):
    x = x.astype(f32)
    inverse = lax.rsqrt(jnp.mean(x * x, axis=1, keepdims=True) + epsilon)
    return (x * inverse * gain).astype(bf16)


def positions_kernel(shares, with_norm, order_ref, *refs):
    step = pl.program_id(0)
    first = 0
    for k, share in enumerate(shares):

        @pl.when((step >= first) & (step < first + share))
        def _():
            if with_norm:
                refs[-1][...] = norm_rows(refs[k][...], refs[-2][0:1, :])
            else:
                refs[-1][...] = refs[k][...]

        first += share


def all_positions(pieces, order, gain_rows=None):
    tile = min(256, min(p.shape[0] for p in pieces))
    shares = [p.shape[0] // tile for p in pieces]
    steps = sum(shares)
    each = steps // PART

    def place(first, share):
        return lambda i, order: (jnp.clip(i - first, 0, share - 1), 0)

    specs, first = [], 0
    for share in shares:
        specs.append(pl.BlockSpec((tile, D), place(first, share)))
        first += share
    extra = []
    if gain_rows is not None:
        specs.append(pl.BlockSpec((8, D), lambda i, order: (0, 0)))
        extra.append(gain_rows)
    return pl.pallas_call(
        functools.partial(positions_kernel, shares, gain_rows is not None),
        grid_spec=pltpu.PrefetchScalarGridSpec(
            num_scalar_prefetch=1,
            grid=(steps,),
            in_specs=specs,
            out_specs=pl.BlockSpec((tile, D), lambda i, order: (order[i // each] * each + i % each, 0)),
        ),
        out_shape=jax.ShapeDtypeStruct((tile * steps, D), bf16),
        compiler_params=pltpu.CompilerParams(vmem_limit_bytes=32 * 2**20),
        cost_estimate=pl.CostEstimate(
            flops=4 * tile * steps * D, bytes_accessed=4 * tile * steps * D, transcendentals=0
        ),
        name="all_positions",
    )(order, *pieces, *extra)


def dp_total(value):
    if not fast_mesh():
        return lax.psum(value, "dp")
    value = value + dp_swap_x(value)
    return value + dp_shift_z(value, 1) + dp_shift_z(value, 2) + dp_shift_z(value, 3)


def by_owner(columns):
    rows = columns.shape[0]
    return (
        columns.reshape(rows, STRIPS, PART, LANES).transpose(2, 0, 1, 3).reshape(PART, rows, OWN)
    )


def from_owner(pieces):
    rows = pieces.shape[1]
    return (
        pieces.reshape(PART, rows, STRIPS, LANES).transpose(1, 2, 0, 3).reshape(rows, INNER)
    )


def heads_by_owner(columns):
    rows = columns.shape[0]
    return (
        columns.reshape(rows, STRIPS, PART, 2).transpose(2, 0, 1, 3).reshape(PART, rows, OWN_HEADS)
    )


def heads_from_owner(pieces):
    rows = pieces.shape[1]
    return (
        pieces.reshape(PART, rows, STRIPS, 2).transpose(1, 2, 0, 3).reshape(rows, HEADS)
    )


def gather_in(pieces):
    full = lax.all_gather(pieces, ("dp", "seq"), axis=1, tiled=True)
    return lax.dynamic_index_in_dim(full, lax.axis_index("seq"), 0, False)


def dp_sum(product):
    return lax.psum_scatter(product, "dp", scatter_dimension=0, tiled=True)


def owners_rows(total):
    return seq_exchange(total.reshape(PART, -1, total.shape[1]))


def scatter_in(grads):
    full = jnp.zeros((PART,) + grads.shape, grads.dtype)
    full = lax.dynamic_update_index_in_dim(full, grads, lax.axis_index("seq"), 0)
    return lax.psum_scatter(full, ("dp", "seq"), scatter_dimension=1, tiled=True).astype(f32)


def gather_out(rows):
    full = lax.all_gather(rows, ("dp", "seq"), axis=0, tiled=True)
    full = full.reshape(STRIPS, PART, LANES, -1)
    return lax.dynamic_index_in_dim(full, lax.axis_index("seq"), 1, False).reshape(OWN, -1)


def gather_plainly(conv_pieces, gate_pieces, out_rows, x_block, cot_block):
    return (
        gather_in(conv_pieces),
        gather_in(gate_pieces),
        gather_out(out_rows),
        seq_pieces(x_block),
        jnp.split(cot_block, 2),
    )


def scatter_out(grads):
    full = jnp.zeros((STRIPS, PART, LANES, grads.shape[1]), grads.dtype)
    full = lax.dynamic_update_index_in_dim(
        full, grads.reshape(STRIPS, LANES, -1), lax.axis_index("seq"), 1
    )
    full = full.reshape(INNER, -1)
    return lax.psum_scatter(full, ("dp", "seq"), scatter_dimension=0, tiled=True).astype(f32)


def dot_nn(a, b):
    return lax.dot_general(a, b, (((1,), (0,)), ((), ())), preferred_element_type=f32)


def dot_nt(a, b):
    return lax.dot_general(a, b, (((1,), (1,)), ((), ())), preferred_element_type=f32)


def dot_tn(a, b):
    return lax.dot_general(a, b, (((0,), (0,)), ((), ())), preferred_element_type=f32)


def dot_exact(a, b):
    return lax.dot_general(
        a, b, (((1,), (0,)), ((), ())), precision=highest, preferred_element_type=f32
    )


def sigmoid(v):
    return 0.5 + 0.5 * jnp.tanh(0.5 * v)


def bc_forward_kernel(tile_ref, taps_ref, out_ref, padded):
    length = tile_ref.shape[0]
    padded[0:8, :] = jnp.zeros((8, LANES), f32)
    padded[8 : 8 + length, :] = tile_ref[...].astype(bf16).astype(f32)
    left = lax.broadcasted_iota(jnp.int32, (1, LANES), 1) < OWN_BC
    for block in range(length // Q):
        start = block * Q
        pre = taps_ref[0:1, :] * padded[start + 5 : start + 5 + Q, :]
        for tap in range(1, CONV):
            pre = pre + taps_ref[tap : tap + 1, :] * padded[start + 5 + tap : start + 5 + tap + Q, :]
        act = pre * sigmoid(pre)
        packed = jnp.where(left, pltpu.roll(act[HALF:], OWN_BC, 1), act[:HALF])
        out_ref[block * HALF : (block + 1) * HALF, :] = packed.astype(bf16)


def bc_forward(dt_tile, taps_tile):
    length = dt_tile.shape[0]
    return pl.pallas_call(
        bc_forward_kernel,
        out_shape=jax.ShapeDtypeStruct((length // 2, LANES), bf16),
        scratch_shapes=[pltpu.VMEM((8 + length, LANES), f32)],
        compiler_params=pltpu.CompilerParams(vmem_limit_bytes=16 * 2**20),
        cost_estimate=pl.CostEstimate(
            flops=20 * length * LANES, bytes_accessed=5 * length * LANES, transcendentals=0
        ),
        name="bc_forward",
    )(dt_tile, taps_tile)


def tail_kernel(tile_ref, grad_ref, ddt_ref, taps_ref, into_ref, out_ref, sums_ref, padded, dp):
    del into_ref
    length = tile_ref.shape[0]
    padded[0:8, :] = jnp.zeros((8, LANES), f32)
    padded[8 : 8 + length, :] = tile_ref[...].astype(bf16).astype(f32)
    dp[length : length + 8, :] = jnp.zeros((8, LANES), f32)
    lane = lax.broadcasted_iota(jnp.int32, (1, LANES), 1)
    left = lane < OWN_BC
    sums_ref[...] = jnp.zeros_like(sums_ref)
    for block in reversed(range(length // Q)):
        start = block * Q
        taken = [padded[start + 5 + tap : start + 5 + tap + Q, :] for tap in range(CONV)]
        pre = taps_ref[0:1, :] * taken[0]
        for tap in range(1, CONV):
            pre = pre + taps_ref[tap : tap + 1, :] * taken[tap]
        packed = grad_ref[block * HALF : (block + 1) * HALF, :]
        grad = jnp.concatenate([packed, pltpu.roll(packed, OWN_BC, 1)], axis=0)
        squashed = sigmoid(pre)
        d_pre = jnp.where(left, 0.0, grad * squashed * (1.0 + pre * (1.0 - squashed)))
        dp[start : start + Q, :] = d_pre
        for tap in range(CONV):
            sums_ref[tap : tap + 1, :] += jnp.sum(d_pre * taken[tap], axis=0, keepdims=True)
        d_in = taps_ref[CONV - 1 : CONV, :] * d_pre
        for tap in range(CONV - 1):
            first = start + CONV - 1 - tap
            d_in = d_in + taps_ref[tap : tap + 1, :] * dp[first : first + Q, :]
        d_dt = jnp.where(lane < OWN_HEADS, ddt_ref[start : start + Q, :], 0.0)
        out_ref[start : start + Q, :] = jnp.where(left, d_dt, d_in).astype(bf16)


def tail_backward(dt_tile, grad, d_dt, taps_tile, into):
    length = dt_tile.shape[0]
    whole = lambda i: (0, 0)
    return pl.pallas_call(
        tail_kernel,
        grid=(1,),
        in_specs=[
            pl.BlockSpec((length, LANES), whole),
            pl.BlockSpec((length // 2, LANES), whole),
            pl.BlockSpec((length, LANES), whole),
            pl.BlockSpec((8, LANES), whole),
            pl.BlockSpec(memory_space=pl.ANY),
        ],
        out_specs=[
            pl.BlockSpec((length, LANES), lambda i: (0, STRIPS)),
            pl.BlockSpec((8, LANES), whole),
        ],
        out_shape=[
            jax.ShapeDtypeStruct(into.shape, bf16),
            jax.ShapeDtypeStruct((8, LANES), f32),
        ],
        input_output_aliases={4: 0},
        scratch_shapes=[pltpu.VMEM((8 + length, LANES), f32), pltpu.VMEM((8 + length, LANES), f32)],
        compiler_params=pltpu.CompilerParams(vmem_limit_bytes=60 * 2**20),
        cost_estimate=pl.CostEstimate(
            flops=40 * length * LANES, bytes_accessed=14 * length * LANES, transcendentals=0
        ),
        name="tail_backward",
    )(dt_tile, grad, d_dt, taps_tile, into)


def keys_and_reads(me, refs):
    odd, lower = me % 2 == 1, me >= 2
    p = [ref[...].astype(f32) for ref in refs]
    r0, r1 = jnp.where(odd, p[1], p[0]), jnp.where(odd, p[0], p[1])
    r2, r3 = jnp.where(odd, p[3], p[2]), jnp.where(odd, p[2], p[3])
    q = (
        jnp.where(lower, r2, r0),
        jnp.where(lower, r3, r1),
        jnp.where(lower, r0, r2),
        jnp.where(lower, r1, r3),
    )
    left = lax.broadcasted_iota(jnp.int32, (1, LANES), 1) < OWN_BC

    def join(a, b):
        top = jnp.where(left, pltpu.roll(a, OWN_BC, 1), b)
        bottom = jnp.where(left, a, pltpu.roll(b, OWN_BC, 1))
        return jnp.concatenate([top, bottom], axis=0).astype(bf16)

    return join(q[0], q[1]), join(q[2], q[3])


def give_back(me, d_keys, d_reads, out_ref):
    left = lax.broadcasted_iota(jnp.int32, (1, LANES), 1) < OWN_BC
    for pair, array in enumerate((d_keys, d_reads)):
        top, bottom = array[:HALF], array[HALF:]
        low = jnp.where(left, bottom, pltpu.roll(top, OWN_BC, 1))
        high = jnp.where(left, pltpu.roll(bottom, OWN_BC, 1), top)
        out_ref[jnp.bitwise_xor(me, 2 * pair)] = low.astype(bf16)
        out_ref[jnp.bitwise_xor(me, 2 * pair + 1)] = high.astype(bf16)


def decay_terms(dt_ref, rows_ref):
    v = dt_ref[...] * rows_ref[2:3, :] + rows_ref[0:1, :]
    steps = jnp.maximum(v, 0.0) + jnp.log1p(jnp.exp(-jnp.abs(v)))
    log2_decay = rows_ref[1:2, :] * LOG2E * steps
    row = lax.broadcasted_iota(jnp.int32, (Q, Q), 0)
    column = lax.broadcasted_iota(jnp.int32, (Q, Q), 1)
    lower = jnp.where(row >= column, 1.0, 0.0)
    running = dot_exact(lower, log2_decay)
    shifted = running - jnp.log(steps) * LOG2E
    end = running[Q - 1 : Q, :]
    return v, steps, running, shifted, end


def spread_heads(values, spread):
    high = values.astype(bf16)
    low = (values - high.astype(f32)).astype(bf16)
    return dot_nn(high, spread) + dot_nn(low, spread)


def forward_kernel(
    me_ref, ci_ref, b0, b1, b2, b3, dt_ref, cw_ref, rows_ref, skip_ref, y_ref, act_ref, s_ref, state, xf,
    e_wide, w_wide
):
    @pl.when(pl.program_id(0) == 0)
    def _():
        state[...] = jnp.zeros_like(state)
        xf[0:8, :] = jnp.zeros((8, OWN), f32)

    @pl.when(pl.program_id(0) > 0)
    def _():
        xf[0:8, :] = xf[Q : Q + 8, :]

    xf[8 : Q + 8, :] = ci_ref[...].astype(f32)
    _, _, running, shifted, end = decay_terms(dt_ref, rows_ref)
    shifted_t = shifted.T
    e_run = jnp.exp2(running)
    w_end = jnp.exp2(end - shifted)
    e_end = jnp.exp2(end)
    keys, reads = keys_and_reads(me_ref[0], (b0, b1, b2, b3))
    keys_t = keys.T
    cb = dot_nt(reads, keys)
    causal = lax.broadcasted_iota(jnp.int32, (HALF, HALF), 0) >= lax.broadcasted_iota(
        jnp.int32, (HALF, HALF), 1
    )
    left = lax.broadcasted_iota(jnp.int32, (1, LANES), 1) < HEAD_DIM
    spread = lax.broadcasted_iota(jnp.int32, (LANES, OWN), 0) == (
        lax.broadcasted_iota(jnp.int32, (LANES, OWN), 1) // HEAD_DIM
    )
    spread = jnp.where(spread, 1.0, 0.0).astype(bf16)
    e_wide[...] = spread_heads(e_run, spread)
    w_wide[...] = spread_heads(w_end, spread)
    s_ref[0] = state[...].astype(bf16)
    for strip in range(STRIPS):
        at = slice(strip * LANES, (strip + 1) * LANES)
        h0, h1 = 2 * strip, 2 * strip + 1
        pre = cw_ref[0:1, at] * xf[5 : 5 + Q, at]
        for tap in range(1, CONV):
            pre = pre + cw_ref[tap : tap + 1, at] * xf[5 + tap : 5 + tap + Q, at]
        act = (pre * sigmoid(pre)).astype(bf16)
        act_ref[:, at] = act
        actf = act.astype(f32)
        inter = dot_nn(reads, s_ref[0, :, at]) * e_wide[:, at]
        inter = inter + skip_ref[0:1, at] * actf
        top, bottom = inter[:HALF], inter[HALF:]
        for h, side in ((h0, left), (h1, jnp.logical_not(left))):
            x_h = jnp.where(side, act, jnp.zeros_like(act))
            m00 = jnp.where(
                causal,
                jnp.exp2(running[:HALF, h : h + 1] - shifted_t[h : h + 1, :HALF]) * cb[:HALF, :HALF],
                0.0,
            )
            m10 = jnp.exp2(running[HALF:, h : h + 1] - shifted_t[h : h + 1, :HALF]) * cb[HALF:, :HALF]
            m11 = jnp.where(
                causal,
                jnp.exp2(running[HALF:, h : h + 1] - shifted_t[h : h + 1, HALF:]) * cb[HALF:, HALF:],
                0.0,
            )
            top = top + dot_nn(m00.astype(bf16), x_h[:HALF])
            bottom = bottom + dot_nn(
                jnp.concatenate([m10.astype(bf16), m11.astype(bf16)], axis=1), x_h
            )
        y_ref[:HALF, at] = top
        y_ref[HALF:, at] = bottom
        weighted = (actf * w_wide[:, at]).astype(bf16)
        state[:, at] = state[:, at] * jnp.where(
            left, e_end[:, h0 : h0 + 1], e_end[:, h1 : h1 + 1]
        ) + dot_nn(keys_t, weighted)


def recurrence_forward(me, conv_in, bc, dt_tile, taps, rows, skip_row):
    length = conv_in.shape[0]
    blocks = length // Q
    whole = lambda i, me: (0, 0)
    along = lambda i, me: (i, 0)
    return pl.pallas_call(
        forward_kernel,
        grid_spec=pltpu.PrefetchScalarGridSpec(
            num_scalar_prefetch=1,
            grid=(blocks,),
            in_specs=[pl.BlockSpec((Q, OWN), along)]
            + [pl.BlockSpec((HALF, LANES), along)] * PART
            + [
                pl.BlockSpec((Q, LANES), along),
                pl.BlockSpec((8, OWN), whole),
                pl.BlockSpec((8, LANES), whole),
                pl.BlockSpec((8, OWN), whole),
            ],
            out_specs=[
                pl.BlockSpec((Q, OWN), along),
                pl.BlockSpec((Q, OWN), along),
                pl.BlockSpec((1, STATE, OWN), lambda i, me: (i, 0, 0)),
            ],
            scratch_shapes=[
                pltpu.VMEM((STATE, OWN), f32),
                pltpu.VMEM((Q + 8, OWN), f32),
                pltpu.VMEM((Q, OWN), f32),
                pltpu.VMEM((Q, OWN), f32),
            ],
        ),
        out_shape=[
            jax.ShapeDtypeStruct((length, OWN), f32),
            jax.ShapeDtypeStruct((length, OWN), bf16),
            jax.ShapeDtypeStruct((blocks, STATE, OWN), bf16),
        ],
        compiler_params=pltpu.CompilerParams(
            dimension_semantics=("arbitrary",), vmem_limit_bytes=60 * 2**20
        ),
        cost_estimate=pl.CostEstimate(
            flops=40 * 10**9, bytes_accessed=2**24, transcendentals=10**7
        ),
        name="recurrence_forward",
    )(me, conv_in, *bc, dt_tile, taps, rows, skip_row)


def backward_kernel(
    me_ref,
    ci_ref,
    prev_ref,
    act_ref,
    dy_ref,
    y_ref,
    b0,
    b1,
    b2,
    b3,
    dt_ref,
    s_ref,
    cw_ref,
    rows_ref,
    skip_ref,
    dci_ref,
    dbc_ref,
    ddt_ref,
    gconv_ref,
    grow_ref,
    back,
    back16,
    dp,
    xf,
    edy,
    wx,
    dcb,
    p12h,
    p12l,
    p3,
    p23,
    cross,
):
    step = pl.program_id(0)
    last = pl.num_programs(0) - 1

    @pl.when(step == 0)
    def _():
        back[...] = jnp.zeros_like(back)
        dp[Q : Q + 8, :] = jnp.zeros((8, OWN), f32)
        gconv_ref[...] = jnp.zeros_like(gconv_ref)
        grow_ref[...] = jnp.zeros_like(grow_ref)
        cross[...] = jnp.zeros_like(cross)

    @pl.when(step > 0)
    def _():
        dp[Q : Q + 8, :] = dp[0:8, :]

    before = prev_ref[8:16, :].astype(f32)
    xf[0:8, :] = jnp.where(step == last, 0.0, before)
    xf[8 : Q + 8, :] = ci_ref[...].astype(f32)
    v, steps, running, shifted, end = decay_terms(dt_ref, rows_ref)
    running_t = running.T
    e_run = jnp.exp2(running)
    w_end = jnp.exp2(end - shifted)
    e_end = jnp.exp2(end)
    keys, reads = keys_and_reads(me_ref[0], (b0, b1, b2, b3))
    reads_t = reads.T
    cbt = dot_nt(keys, reads)
    ahead = lax.broadcasted_iota(jnp.int32, (HALF, HALF), 0) <= lax.broadcasted_iota(
        jnp.int32, (HALF, HALF), 1
    )
    left = lax.broadcasted_iota(jnp.int32, (1, LANES), 1) < HEAD_DIM
    back16[...] = back[...].astype(bf16)
    dcb[...] = jnp.zeros_like(dcb)
    for strip in range(STRIPS):
        at = slice(strip * LANES, (strip + 1) * LANES)
        h0, h1 = 2 * strip, 2 * strip + 1
        act = act_ref[:, at]
        dy = dy_ref[:, at]
        actf = act.astype(f32)
        dyf = dy.astype(f32)
        skip = skip_ref[0:1, at]
        w_pair = jnp.where(left, w_end[:, h0 : h0 + 1], w_end[:, h1 : h1 + 1])
        e_pair = jnp.where(left, e_run[:, h0 : h0 + 1], e_run[:, h1 : h1 + 1])
        decayed = (dyf * e_pair).astype(bf16)
        edy[:, at] = decayed
        wx[:, at] = (actf * w_pair).astype(bf16)
        inter = dot_nn(keys, back16[:, at]) * w_pair
        top = jnp.zeros((HALF, LANES), f32)
        bottom = jnp.zeros((HALF, LANES), f32)
        for h, side in ((h0, left), (h1, jnp.logical_not(left))):
            x_h = jnp.where(side, actf, 0.0).astype(bf16)
            dy_h = jnp.where(side, dyf, 0.0).astype(bf16)
            g_top = dot_nt(x_h[:HALF], dy)
            g_bottom = dot_nt(x_h[HALF:], dy[HALF:])
            l00 = jnp.exp2(running_t[h : h + 1, :HALF] - shifted[:HALF, h : h + 1])
            l01 = jnp.exp2(running_t[h : h + 1, HALF:] - shifted[:HALF, h : h + 1])
            l11 = jnp.exp2(running_t[h : h + 1, HALF:] - shifted[HALF:, h : h + 1])
            m00 = jnp.where(ahead, l00 * cbt[:HALF, :HALF], 0.0).astype(bf16)
            m01 = (l01 * cbt[:HALF, HALF:]).astype(bf16)
            m11 = jnp.where(ahead, l11 * cbt[HALF:, HALF:], 0.0).astype(bf16)
            top = top + dot_nn(jnp.concatenate([m00, m01], axis=1), dy_h)
            bottom = bottom + dot_nn(m11, dy_h[HALF:])
            dcb[:HALF, :HALF] += jnp.where(ahead, l00 * g_top[:, :HALF], 0.0)
            dcb[:HALF, HALF:] += l01 * g_top[:, HALF:]
            dcb[HALF:, HALF:] += jnp.where(ahead, l11 * g_bottom, 0.0)
        intra = jnp.concatenate([top, bottom], axis=0)
        d_values = intra + inter
        p_12 = dyf * (y_ref[:, at] - skip * actf) - actf * intra
        p_12h = p_12.astype(bf16)
        p12h[:, at] = p_12h
        p12l[:, at] = (p_12 - p_12h.astype(f32)).astype(bf16)
        p3[:, at] = (actf * inter).astype(bf16)
        p23[:, at] = (actf * d_values).astype(bf16)
        d_act = d_values + skip * dyf
        pre = cw_ref[0:1, at] * xf[5 : 5 + Q, at]
        for tap in range(1, CONV):
            pre = pre + cw_ref[tap : tap + 1, at] * xf[5 + tap : 5 + tap + Q, at]
        squashed = sigmoid(pre)
        d_pre = d_act * squashed * (1.0 + pre * (1.0 - squashed))
        dp[0:Q, at] = d_pre
        sums = [
            jnp.sum(d_pre * xf[5 + tap : 5 + tap + Q, at], axis=0, keepdims=True)
            for tap in range(CONV)
        ]
        sums.append(jnp.sum(dyf * actf, axis=0, keepdims=True))
        for place, total in enumerate(sums):
            gconv_ref[place : place + 1, at] += total
        d_in = cw_ref[CONV - 1 : CONV, at] * d_pre
        for tap in range(CONV - 1):
            d_in = d_in + cw_ref[tap : tap + 1, at] * dp[CONV - 1 - tap : CONV - 1 - tap + Q, at]
        dci_ref[:, at] = d_in.astype(bf16)
        kept = back[:, at] * jnp.where(left, e_end[:, h0 : h0 + 1], e_end[:, h1 : h1 + 1])
        cross[0:1, at] = jnp.sum(kept * s_ref[0, :, at].astype(f32), axis=0, keepdims=True)
        back[:, at] = kept + dot_nn(reads_t, decayed)
    dcb_t = dcb[...]
    d_keys = dot_nn(dcb_t.astype(bf16), reads) + dot_nt(wx[...], back16[...])
    d_reads = dot_nn(dcb_t.T.astype(bf16), keys) + dot_nt(edy[...], s_ref[0])
    give_back(me_ref[0], d_keys, d_reads, dbc_ref)
    unit = lax.broadcasted_iota(jnp.int32, (OWN, LANES), 0)
    head = lax.broadcasted_iota(jnp.int32, (OWN, LANES), 1)
    member = jnp.where(unit // HEAD_DIM == head, 1.0, 0.0)
    member16 = member.astype(bf16)
    s_12 = dot_nn(p12h[...], member16) + dot_nn(p12l[...], member16)
    s_3 = dot_nn(p3[...], member16)
    s_23 = dot_nn(p23[...], member16)
    through = dot_exact(cross[...], member)[0:1, :]
    row = lax.broadcasted_iota(jnp.int32, (Q, Q), 0)
    column = lax.broadcasted_iota(jnp.int32, (Q, Q), 1)
    suffix = jnp.where(column >= row, 1.0, 0.0)
    prefix = jnp.where(column < row, 1.0, 0.0)
    d_log = dot_exact(suffix, s_12) + dot_exact(prefix, s_3) + through
    slope = sigmoid(v)
    ratio = jnp.where(steps > 0.0, slope / steps, 0.0)
    rate = rows_ref[1:2, :]
    d_sum = s_23 * ratio + rate * d_log * slope
    ddt_ref[...] = d_sum * rows_ref[2:3, :]
    grow_ref[0:1, :] += jnp.sum(d_sum, axis=0, keepdims=True)
    grow_ref[1:2, :] += jnp.sum(d_log * rate * steps, axis=0, keepdims=True)


def recurrence_backward(me, conv_in, act, dy, y, bc, dt_tile, entry, taps, rows, skip_row):
    length = conv_in.shape[0]
    blocks = length // Q
    whole = lambda i, me: (0, 0)
    along = lambda i, me: (blocks - 1 - i, 0)
    previous = lambda i, me: (jnp.maximum((blocks - 1 - i) * (Q // 16) - 1, 0), 0)
    return pl.pallas_call(
        backward_kernel,
        grid_spec=pltpu.PrefetchScalarGridSpec(
            num_scalar_prefetch=1,
            grid=(blocks,),
            in_specs=[
                pl.BlockSpec((Q, OWN), along),
                pl.BlockSpec((16, OWN), previous),
                pl.BlockSpec((Q, OWN), along),
                pl.BlockSpec((Q, OWN), along),
                pl.BlockSpec((Q, OWN), along),
            ]
            + [pl.BlockSpec((HALF, LANES), along)] * PART
            + [
                pl.BlockSpec((Q, LANES), along),
                pl.BlockSpec((1, STATE, OWN), lambda i, me: (blocks - 1 - i, 0, 0)),
                pl.BlockSpec((8, OWN), whole),
                pl.BlockSpec((8, LANES), whole),
                pl.BlockSpec((8, OWN), whole),
            ],
            out_specs=[
                pl.BlockSpec((Q, OWN), along),
                pl.BlockSpec((PART, HALF, LANES), lambda i, me: (0, blocks - 1 - i, 0)),
                pl.BlockSpec((Q, LANES), along),
                pl.BlockSpec((8, OWN), whole),
                pl.BlockSpec((8, LANES), whole),
            ],
            scratch_shapes=[
                pltpu.VMEM((STATE, OWN), f32),
                pltpu.VMEM((STATE, OWN), bf16),
                pltpu.VMEM((Q + 8, OWN), f32),
                pltpu.VMEM((Q + 8, OWN), f32),
                pltpu.VMEM((Q, OWN), bf16),
                pltpu.VMEM((Q, OWN), bf16),
                pltpu.VMEM((Q, Q), f32),
                pltpu.VMEM((Q, OWN), bf16),
                pltpu.VMEM((Q, OWN), bf16),
                pltpu.VMEM((Q, OWN), bf16),
                pltpu.VMEM((Q, OWN), bf16),
                pltpu.VMEM((8, OWN), f32),
            ],
        ),
        out_shape=[
            jax.ShapeDtypeStruct((length, CONV_COLS), bf16),
            jax.ShapeDtypeStruct((PART, length // 2, LANES), bf16),
            jax.ShapeDtypeStruct((length, LANES), f32),
            jax.ShapeDtypeStruct((8, OWN), f32),
            jax.ShapeDtypeStruct((8, LANES), f32),
        ],
        compiler_params=pltpu.CompilerParams(
            dimension_semantics=("arbitrary",), vmem_limit_bytes=60 * 2**20
        ),
        cost_estimate=pl.CostEstimate(
            flops=70 * 10**9, bytes_accessed=2**24, transcendentals=10**7
        ),
        name="recurrence_backward",
    )(me, conv_in, conv_in, act, dy, y, *bc, dt_tile, entry, taps, rows, skip_row)


def pull_out_kernel(order_ref, own, sibling, across_a, across_b, corner_a, corner_b, wo_ref, cot_ref, d_ref):
    del order_ref
    step = pl.program_id(0)
    half = across_a.shape[0]
    for k, ref in enumerate((own, sibling)):

        @pl.when(step == k)
        def _():
            cot_ref[...] = ref[...]

    for k, (first, second) in enumerate(((across_a, across_b), (corner_a, corner_b))):

        @pl.when(step == 2 + k)
        def _():
            cot_ref[:half, :] = first[...]
            cot_ref[half:, :] = second[...]

    d_ref[...] = dot_nt(cot_ref[...], wo_ref[...])


def pull_out(pieces, order, w_o):
    tile = pieces[0].shape[0]
    whole = lambda i, order: (0, 0)
    there = lambda i, order: (order[i], 0)
    length = tile * PART
    return pl.pallas_call(
        pull_out_kernel,
        grid_spec=pltpu.PrefetchScalarGridSpec(
            num_scalar_prefetch=1,
            grid=(PART,),
            in_specs=[pl.BlockSpec(piece.shape, whole) for piece in pieces]
            + [pl.BlockSpec((OWN, D), whole)],
            out_specs=[pl.BlockSpec((tile, D), there), pl.BlockSpec((tile, OWN), there)],
        ),
        out_shape=[
            jax.ShapeDtypeStruct((length, D), bf16),
            jax.ShapeDtypeStruct((length, OWN), f32),
        ],
        compiler_params=pltpu.CompilerParams(vmem_limit_bytes=52 * 2**20),
        cost_estimate=pl.CostEstimate(
            flops=2 * length * D * OWN, bytes_accessed=2**25, transcendentals=0
        ),
        name="pull_out",
    )(order, *pieces, w_o)


def gate_forward_kernel(n_ref, y_ref, d_ref, wg_ref, row_ref, z_ref, sums_ref):
    z = dot_nn(n_ref[...], wg_ref[...]) * row_ref[1:2, :]
    z_ref[...] = z
    gated = y_ref[...] * (z * sigmoid(z))
    squares = jnp.sum(gated * gated, axis=1, keepdims=True)
    cross = jnp.sum(d_ref[...] * row_ref[0:1, :] * gated, axis=1, keepdims=True)
    lane = lax.broadcasted_iota(jnp.int32, (1, LANES), 1)
    both = jnp.where(lane == 0, squares, jnp.where(lane == 1, cross, 0.0))
    sums_ref[...] = both.T[0:8, :]


def gate_forward(normed, y, d, w_gate, row):
    length = normed.shape[0]
    whole = lambda i: (0, 0)
    along = lambda i: (i, 0)
    return pl.pallas_call(
        gate_forward_kernel,
        grid=(length // WIDE,),
        in_specs=[
            pl.BlockSpec((WIDE, D), along),
            pl.BlockSpec((WIDE, OWN), along),
            pl.BlockSpec((WIDE, OWN), along),
            pl.BlockSpec((D, OWN), whole),
            pl.BlockSpec((8, OWN), whole),
        ],
        out_specs=[
            pl.BlockSpec((WIDE, OWN), along),
            pl.BlockSpec((8, WIDE), lambda i: (0, i)),
        ],
        out_shape=[
            jax.ShapeDtypeStruct((length, OWN), f32),
            jax.ShapeDtypeStruct((8, length), f32),
        ],
        compiler_params=pltpu.CompilerParams(vmem_limit_bytes=52 * 2**20),
        cost_estimate=pl.CostEstimate(
            flops=2 * length * D * OWN, bytes_accessed=2**25, transcendentals=length * OWN
        ),
        name="gate_forward",
    )(normed, y, d, w_gate, row)


def gate_backward_kernel(y_ref, z_ref, d_ref, sums_ref, row_ref, out_ref, dy_ref, dz_ref, gain_ref):
    @pl.when(pl.program_id(0) == 0)
    def _():
        gain_ref[...] = jnp.zeros_like(gain_ref)

    units = row_ref[2:3, 0:1]
    sums = sums_ref[...]
    inverse = lax.rsqrt(sums[0:1, :] / units + epsilon)
    pull = inverse * inverse * inverse * sums[1:2, :] / units
    row = lax.broadcasted_iota(jnp.int32, (LANES, 1), 0)
    columns = jnp.where(row == 0, inverse, jnp.where(row == 1, pull, 0.0)).T
    inverse, pull = columns[:, 0:1], columns[:, 1:2]
    for strip in range(STRIPS):
        at = slice(strip * LANES, (strip + 1) * LANES)
        y, z, d = y_ref[:, at], z_ref[:, at], d_ref[:, at]
        gain = row_ref[0:1, at]
        squashed = sigmoid(z)
        act = z * squashed
        gated = y * act
        normalized = gated * inverse
        out_ref[:, at] = (normalized * gain).astype(bf16)
        gain_ref[0:1, at] += jnp.sum(d * normalized, axis=0, keepdims=True)
        d_gated = inverse * (d * gain) - gated * pull
        dy_ref[:, at] = (d_gated * act).astype(bf16)
        dz_ref[:, at] = (d_gated * y * squashed * (1.0 + z * (1.0 - squashed))).astype(bf16)


def gate_backward(y, z, d, sums, row):
    length = y.shape[0]
    whole = lambda i: (0, 0)
    along = lambda i: (i, 0)
    return pl.pallas_call(
        gate_backward_kernel,
        grid=(length // Q,),
        in_specs=[pl.BlockSpec((Q, OWN), along)] * 3
        + [pl.BlockSpec((8, Q), lambda i: (0, i)), pl.BlockSpec((8, OWN), whole)],
        out_specs=[pl.BlockSpec((Q, OWN), along)] * 3 + [pl.BlockSpec((8, OWN), whole)],
        out_shape=[jax.ShapeDtypeStruct((length, OWN), bf16)] * 3
        + [jax.ShapeDtypeStruct((8, OWN), f32)],
        compiler_params=pltpu.CompilerParams(vmem_limit_bytes=32 * 2**20),
        cost_estimate=pl.CostEstimate(
            flops=30 * length * OWN, bytes_accessed=18 * length * OWN, transcendentals=length * OWN
        ),
        name="gate_backward",
    )(y, z, d, sums, row)


def input_gradient_kernel(core_ref, z_ref, p_ref, wg_ref, wc_ref, other_ref, mine_ref):
    del core_ref
    out = (dot_nt(z_ref[...], wg_ref[...]) + dot_nt(p_ref[...], wc_ref[...])).astype(bf16)

    @pl.when(pl.program_id(0) < 2)
    def _():
        other_ref[...] = out

    @pl.when(pl.program_id(0) >= 2)
    def _():
        mine_ref[...] = out


def input_gradient(core, d_z, d_project, w_gate, w_conv):
    tokens = d_z.shape[0] // PART
    whole = lambda i, core: (0, 0)
    along = lambda i, core: (i % 2 * 2 + jnp.where(i < 2, 1 - core[0], core[0]), 0)
    return pl.pallas_call(
        input_gradient_kernel,
        grid_spec=pltpu.PrefetchScalarGridSpec(
            num_scalar_prefetch=1,
            grid=(PART,),
            in_specs=[
                pl.BlockSpec((tokens, OWN), along),
                pl.BlockSpec((tokens, CONV_COLS), along),
                pl.BlockSpec((D, OWN), whole),
                pl.BlockSpec((D, CONV_COLS), whole),
            ],
            out_specs=[
                pl.BlockSpec((tokens, D), lambda i, core: (jnp.minimum(i, 1), 0)),
                pl.BlockSpec((tokens, D), lambda i, core: (jnp.maximum(i - 2, 0), 0)),
            ],
        ),
        out_shape=[jax.ShapeDtypeStruct((2 * tokens, D), bf16)] * 2,
        compiler_params=pltpu.CompilerParams(vmem_limit_bytes=60 * 2**20),
        cost_estimate=pl.CostEstimate(
            flops=10**10, bytes_accessed=2**22, transcendentals=0
        ),
        name="input_gradient",
    )(core, d_z, d_project, w_gate, w_conv)


def products_kernel(n_ref, z_ref, r_ref, t_ref, out_ref):
    rows = D // STRIPS
    gate = dot_nn(n_ref[...].T, z_ref[...]).astype(bf16)
    rest = dot_nn(r_ref[...].T, t_ref[...]).astype(bf16)
    for k in range(out_ref.shape[0]):
        out_ref[k, :rows, :] = gate[k * rows : (k + 1) * rows]
        product = rest[k * LANES : (k + 1) * LANES]
        out_ref[k, rows : rows + LANES, :] = product[:, :OWN]
        out_ref[k, rows + LANES :, :] = product[:, OWN:]


def products(normed, d_z, rounded_out, cot):
    length = normed.shape[0]
    rows = D // STRIPS
    each = 1
    whole = lambda i: (0, 0)
    across = lambda i: (0, i)
    return pl.pallas_call(
        products_kernel,
        grid=(STRIPS // each,),
        in_specs=[
            pl.BlockSpec((length, each * rows), across),
            pl.BlockSpec((length, OWN), whole),
            pl.BlockSpec((length, each * LANES), across),
            pl.BlockSpec((length, D), whole),
        ],
        out_specs=pl.BlockSpec((each, rows + 2 * LANES, OWN), lambda i: (i, 0, 0)),
        out_shape=jax.ShapeDtypeStruct((STRIPS, rows + 2 * LANES, OWN), bf16),
        compiler_params=pltpu.CompilerParams(vmem_limit_bytes=38 * 2**20),
        cost_estimate=pl.CostEstimate(
            flops=4 * length * D * OWN, bytes_accessed=2**25, transcendentals=0
        ),
        name="products",
    )(normed, d_z, rounded_out, cot)


def rows_kernel(me_ref, *refs):
    gates, convs = refs[:PART], refs[PART : 2 * PART]
    w_ref, wdt_ref, gain_ref, grad_ref, gdt_ref, gnorm_ref = refs[2 * PART :]
    me = me_ref[0]
    rows = w_ref.shape[0]
    for k in range(PART):
        owner = jnp.bitwise_xor(me, k)
        for strip in range(STRIPS):
            at = slice(strip * LANES, (strip + 1) * LANES)
            first = pl.multiple_of((strip * PART + owner) * LANES, LANES)
            grad_ref[:, pl.ds(first, LANES)] = gates[k][:, at].astype(f32)
            grad_ref[:, pl.ds(INNER + first, LANES)] = convs[k][:, at].astype(f32)
    odd, lower = me % 2 == 1, me >= 2
    p = [convs[k][:, OWN:].astype(f32) for k in range(PART)]
    r0, r1 = jnp.where(odd, p[1], p[0]), jnp.where(odd, p[0], p[1])
    r2, r3 = jnp.where(odd, p[3], p[2]), jnp.where(odd, p[2], p[3])
    tails = (
        jnp.where(lower, r2, r0),
        jnp.where(lower, r3, r1),
        jnp.where(lower, r0, r2),
        jnp.where(lower, r1, r3),
    )
    left = lax.broadcasted_iota(jnp.int32, (1, LANES), 1) < OWN_BC
    for pair in range(2):
        low, high = tails[2 * pair], tails[2 * pair + 1]
        first = 2 * INNER + pair * LANES
        grad_ref[:, first : first + LANES] = jnp.where(left, pltpu.roll(low, OWN_BC, 1), high)
    slot = lax.broadcasted_iota(jnp.int32, (LANES, HEADS), 0)
    head = lax.broadcasted_iota(jnp.int32, (LANES, HEADS), 1)
    d_dt = jnp.zeros((rows, HEADS), f32)
    for owner in range(PART):
        chosen = (slot < OWN_HEADS) & (head == slot // 2 * 2 * PART + 2 * owner + slot % 2)
        d_dt = d_dt + dot_nn(tails[owner].astype(bf16), jnp.where(chosen, 1.0, 0.0).astype(bf16))
    gdt_ref[...] = d_dt
    total = jnp.sum(wdt_ref[...].astype(f32) * d_dt, axis=1, keepdims=True)
    for strip in range(2 * STRIPS * PART + 2):
        at = slice(strip * LANES, (strip + 1) * LANES)
        total = total + jnp.sum(w_ref[:, at].astype(f32) * grad_ref[:, at], axis=1, keepdims=True)
    square = lax.broadcasted_iota(jnp.int32, (rows, rows), 0) == lax.broadcasted_iota(
        jnp.int32, (rows, rows), 1
    )
    flat = jnp.sum(jnp.where(square, total, 0.0), axis=0, keepdims=True)
    gnorm_ref[...] = flat / gain_ref[...].astype(f32)


def projection_rows(me, gates, convs, w_in, w_dt, norm_gain):
    rows = w_in.shape[0]
    whole = lambda *block: pl.BlockSpec(block, lambda i, me: (0,) * len(block))
    columns = w_in.shape[1]
    return pl.pallas_call(
        rows_kernel,
        grid_spec=pltpu.PrefetchScalarGridSpec(
            num_scalar_prefetch=1,
            grid=(1,),
            in_specs=[whole(rows, OWN)] * PART
            + [whole(rows, CONV_COLS)] * PART
            + [whole(rows, columns), whole(rows, HEADS), whole(1, rows)],
            out_specs=[whole(rows, columns), whole(rows, HEADS), whole(1, rows)],
        ),
        out_shape=[
            jax.ShapeDtypeStruct((rows, columns), f32),
            jax.ShapeDtypeStruct((rows, HEADS), f32),
            jax.ShapeDtypeStruct((1, rows), f32),
        ],
        compiler_params=pltpu.CompilerParams(vmem_limit_bytes=60 * 2**20),
        name="projection_rows",
    )(me, *gates, *convs, w_in, w_dt, norm_gain[None, :])


def per_device(
    hidden_in,
    widths,
    norm_gain,
    w_in,
    w_dt,
    conv_weight,
    dt_bias,
    a_log,
    skip_gain,
    gate_gain,
    w_out,
    grad_out,
):
    me = lax.axis_index("seq")
    tokens = hidden_in.shape[1]
    length = tokens * PART
    rows_in = w_in.shape[0]
    used_units = INNER // 8 * jnp.left_shift(jnp.int32(1), widths[0])
    units_float = used_units.astype(f32)
    block = jnp.arange(OWN) // LANES * PART + me
    unit_used = block * LANES < used_units
    head_used = ((jnp.arange(OWN_HEADS) // 2 * PART + me) * LANES < used_units).astype(f32)

    if fast_mesh():
        conv_pieces, gate_pieces = owners_pieces(w_in, w_dt, norm_gain, gate_gain)
    else:
        every = lambda a: jnp.broadcast_to(a[None], (PART,) + a.shape)
        tail = jnp.concatenate(
            [
                heads_by_owner(w_dt),
                every(norm_gain[:, None]),
                every(gate_gain.reshape(2, rows_in).T),
                jnp.zeros((PART, rows_in, LANES - OWN_HEADS - 3 - OWN_BC), bf16),
                w_in[:, 2 * INNER :].reshape(rows_in, PART, OWN_BC).transpose(1, 0, 2),
            ],
            axis=2,
        )
        conv_pieces = jnp.concatenate([by_owner(w_in[:, INNER : 2 * INNER]), tail], axis=2)
        gate_pieces = by_owner(w_in[:, :INNER])

    gather = gather_everything if fast_mesh() else gather_plainly
    w_conv, w_gate, w_o, x_pieces, (cot_a, cot_b) = gather(
        conv_pieces, gate_pieces, w_out, hidden_in[0], grad_out[0]
    )
    order = jnp.stack([me, me ^ 1, me ^ 2, me ^ 3]).astype(jnp.int32)
    gate_all = w_conv[:, OWN + OWN_HEADS + 1 : OWN + OWN_HEADS + 3]
    gate_all = gate_all.reshape(D // rows_in, rows_in, 2).transpose(0, 2, 1)
    gate_row = lax.dynamic_index_in_dim(gate_all.reshape(STRIPS, PART, LANES), me, 1, False)
    gate_row = gate_row.reshape(1, OWN).astype(f32)
    gain_row = w_conv[:, OWN + OWN_HEADS].astype(f32)[None, :]

    def own_heads(array):
        return lax.dynamic_index_in_dim(array.reshape(STRIPS, PART, 2), me, 1, False).reshape(-1)

    bias = own_heads(dt_bias)
    rate = -jnp.exp(own_heads(a_log))
    skip = own_heads(skip_gain)
    pad_heads = lambda a: jnp.pad(a, (0, LANES - OWN_HEADS))
    rows = jnp.stack(
        [pad_heads(bias), pad_heads(rate), pad_heads(head_used)] + [jnp.zeros((LANES,), f32)] * 5
    )
    skip_row = jnp.broadcast_to(jnp.repeat(skip, HEAD_DIM)[None, :], (8, OWN))
    taps = lax.dynamic_index_in_dim(
        conv_weight[:, :INNER].reshape(CONV, STRIPS, PART, LANES), me, 2, False
    ).reshape(CONV, OWN)
    taps = jnp.pad(taps.astype(f32), ((0, 8 - CONV), (0, 0)))
    taps_bc = lax.dynamic_slice_in_dim(conv_weight[:, INNER:], me * OWN_BC, OWN_BC, 1).astype(f32)
    taps_tile = jnp.pad(taps_bc, ((0, 8 - CONV), (LANES - OWN_BC, 0)))
    place_me = me.astype(jnp.int32).reshape(1)

    normed = all_positions(x_pieces, order, jnp.broadcast_to(gain_row, (8, D)))
    dt_tile = dot_nn(normed, w_conv[:, OWN:])
    bc = bc_forward(dt_tile, taps_tile)
    bc = [bc] + [xor_seq(bc, bits) for bits in range(1, PART)]
    conv_in = jnp.where(unit_used, dot_nn(normed, w_conv[:, :OWN]), 0.0).astype(bf16)
    if fast_mesh():
        w_o += [dp_swap_x(piece) for piece in w_o[1:4]]
    else:
        cot_a = xor_seq(cot_a, 2)
    cot_b, conv_in, *bc[1:] = tie(cot_b, conv_in, *bc[1:])
    cot_b = xor_seq(cot_b, 2)
    y, act, entry = recurrence_forward(place_me, conv_in, bc, dt_tile, taps, rows, skip_row)
    if fast_mesh():
        cot_b, *w_o[5:] = after([cot_b, *w_o[5:]], [entry])
        w_o = assemble(w_o, out_places(), 512)
    else:
        (cot_b,) = after([cot_b], [entry])
    cot_pieces = (
        grad_out[0], xor_seq(grad_out[0], 1), cot_a, cot_b, xor_seq(cot_a, 1), xor_seq(cot_b, 1)
    )
    cot_all, d_rounded = pull_out(cot_pieces, order, w_o)
    row = jnp.concatenate(
        [
            gate_row,
            unit_used.astype(f32)[None, :],
            jnp.full((6, OWN), units_float),
        ],
        axis=0,
    )
    z, sums = gate_forward(normed, y, d_rounded, w_gate, row)
    rounded_out, d_y, d_z, grad_gate_rows = gate_backward(y, z, d_rounded, seq_total(sums), row)
    grad_gate_local = grad_gate_rows[0]

    if fast_mesh():
        both = products(normed, d_z, rounded_out, cot_all)
        d_y, both = tie(d_y, both)
        both_total = dp_sum(both.reshape(-1, OWN))

    d_values, d_bc, d_dt, g_conv, g_rows = recurrence_backward(
        place_me, conv_in, act, d_y, y, bc, dt_tile, entry, taps, rows, skip_row
    )
    if fast_mesh():
        d_values, d_bc, rounded_out = tie(d_values, d_bc, rounded_out)
    branch = dot_nn(rounded_out, w_o).astype(bf16).reshape(PART, tokens, D)
    branch_mine, branch_got = core_halves(branch)
    d_bc_mine, d_bc_got = seq_scatter_relative(d_bc)
    branch_keep, branch_give = halves_sum(branch_mine, branch_got)
    d_bc_got, branch_give = tie(d_bc_got, branch_give)
    d_project, g_tail = tail_backward(
        dt_tile, d_bc_mine + d_bc_got.astype(f32), d_dt, taps_tile, d_values
    )
    g_skip = jnp.sum(g_conv[4].reshape(OWN_HEADS, HEAD_DIM), axis=1)
    small = jnp.concatenate(
        [
            g_conv[:CONV].reshape(-1),
            g_tail[:CONV, LANES - OWN_BC :].reshape(-1),
            pad_heads(g_rows[0, :OWN_HEADS]),
            pad_heads(g_rows[1, :OWN_HEADS]),
            pad_heads(g_skip),
            grad_gate_local,
        ]
    )
    count = small.shape[0]
    padded = -(-count // (8 * LANES)) * 8 * LANES
    small = jnp.pad(small, (0, padded - count)).reshape(-1, LANES)
    if fast_mesh():
        conv_product = dot_tn(normed, d_project).astype(bf16)
        d_project, conv_product = tie(d_project, conv_product)
        (conv_product,) = after([conv_product], [both_total])
        conv_total = dp_sum(conv_product)
    branch_across = xor_seq(branch_give, 2)
    other, mine = input_gradient(place_me % 2, d_z, d_project, w_gate, w_conv)
    if fast_mesh():
        branch_across, other, mine = tie(branch_across, other, mine)
    mine = mine.reshape(2, tokens, D)
    got = xor_seq(other, 1).reshape(2, tokens, D)
    keep, give = halves_sum(mine, got)
    small, give = tie(small, give)
    across = xor_seq(give, 2)
    small, across = tie(dp_total(small), across)
    d_own = keep + across.astype(f32)
    if fast_mesh():
        both_total = after([both_total], [across])[0]
        small_pieces = seq_pieces(small)
        gate_rows, out_left, out_right = jnp.split(both_total, [rows_in * PART, rows_in * PART + LANES])
        grad_w_out = jnp.concatenate([out_left, out_right], axis=1).astype(f32)
        gate_rows = owners_rows(gate_rows)
        (conv_total,) = after([conv_total], [small_pieces[3], *gate_rows[1:]])
        grad_w_in, grad_w_dt, grad_norm_gain = projection_rows(
            place_me, gate_rows, owners_rows(conv_total), w_in, w_dt, norm_gain
        )
        grad_norm_gain = grad_norm_gain[0]
    else:
        small_pieces = seq_pieces(small)
        grad_w_out = scatter_out(dot_tn(rounded_out, cot_all).astype(bf16))
        grad_gate_in = scatter_in(dot_tn(normed, d_z).astype(bf16))
        grad_conv_in = scatter_in(dot_tn(normed, d_project).astype(bf16))
        grad_w_in = jnp.concatenate(
            [
                from_owner(grad_gate_in),
                from_owner(grad_conv_in[:, :, :OWN]),
                grad_conv_in[:, :, CONV_COLS - OWN_BC :].transpose(1, 0, 2).reshape(rows_in, 2 * STATE),
            ],
            axis=1,
        )
        grad_w_dt = heads_from_owner(grad_conv_in[:, :, OWN : OWN + OWN_HEADS])
        grad_norm_gain = (
            jnp.sum(w_in.astype(f32) * grad_w_in, axis=1)
            + jnp.sum(w_dt.astype(f32) * grad_w_dt, axis=1)
        ) / norm_gain.astype(f32)
    x_own = hidden_in[0].astype(f32)
    hidden_out = (x_own + branch_keep + branch_across.astype(f32)).astype(bf16)[None]
    own_rms = lax.rsqrt(jnp.mean(x_own * x_own, axis=1, keepdims=True) + epsilon)
    d_scaled = d_own * gain_row
    d_input = own_rms * d_scaled - x_own * own_rms**3 * jnp.mean(
        d_scaled * x_own, axis=1, keepdims=True
    )
    grad_in = (grad_out[0].astype(f32) + d_input).astype(bf16)[None]

    every = jnp.stack(by_partner(small_pieces)).reshape(PART, padded)
    start = 0

    def take(size):
        nonlocal start
        start += size
        return every[:, start - size : start]

    all_conv = take(CONV * OWN).reshape(PART, CONV, OWN)
    all_conv_bc = take(CONV * OWN_BC).reshape(PART, CONV, OWN_BC)
    head_sums = [heads_from_owner(take(LANES)[:, None, :OWN_HEADS]).reshape(HEADS) for _ in range(3)]
    grad_gate = lax.dynamic_index_in_dim(take(OWN), me, 0, False)
    grad_conv = jnp.concatenate(
        [from_owner(all_conv), all_conv_bc.transpose(1, 0, 2).reshape(CONV, 2 * STATE)], axis=1
    )
    place = lax.axis_index(("dp", "seq"))
    gain_rows = gate_gain.shape[0]
    if gain_rows == LANES:
        grad_gate_gain = lax.dynamic_slice_in_dim(
            grad_gate, lax.axis_index("dp") * gain_rows, gain_rows, 0
        )
    else:
        start = CONV * OWN + CONV * OWN_BC + 3 * LANES
        whole_gate = from_owner(take(OWN)[:, None, :]).reshape(INNER)
        grad_gate_gain = lax.dynamic_slice_in_dim(whole_gate, place * gain_rows, gain_rows, 0)

    return (
        hidden_out,
        grad_in,
        grad_norm_gain,
        grad_w_in,
        grad_w_dt,
        grad_conv,
        head_sums[0],
        head_sums[1],
        head_sums[2],
        grad_gate_gain,
        grad_w_out,
    )


def solution(mesh):
    return jax.shard_map(
        per_device,
        mesh=mesh,
        in_specs=(
            P("dp", "seq", None),
            P("dp"),
            P(("dp", "seq")),
            P(("dp", "seq"), None),
            P(("dp", "seq"), None),
            P(),
            P(),
            P(),
            P(),
            P(("dp", "seq")),
            P(("dp", "seq"), None),
            P("dp", "seq", None),
        ),
        out_specs=(
            P("dp", "seq", None),
            P("dp", "seq", None),
            P(("dp", "seq")),
            P(("dp", "seq"), None),
            P(("dp", "seq"), None),
            P(),
            P(),
            P(),
            P(),
            P(("dp", "seq")),
            P(("dp", "seq"), None),
        ),
        check_vma=False,
    )
```
